32 devices in a mesh: gx: 2 (over y), gy: 16 (over z, x, core).
Axes of the slice: x: 2, y: 2, z: 4, core: 2. Of those that a mesh axis runs over, the one named last changes fastest.
Arguments:
- hidden_states_in: bfloat16 [32, 512, 768], P(('gx', 'gy')), may hold values from -6 to 6
- piece_sizes: int32 [32, 8], P(('gx', 'gy')), may hold values from 1 to 88, as said below
- matching_passage_number: int32 [128], P(('gx', 'gy')), may hold values from 0 to 127, each once
- softmax_sharpness: float32 [1], replicated, may hold values from 0.02 to 0.04
- question_projection: bfloat16 [768, 768], replicated, may hold values from -0.21875 to 0.21875
- question_offset: bfloat16 [768], replicated, may hold values from -2 to 2
- lookup_projection: bfloat16 [768, 768], replicated, may hold values from -0.21875 to 0.21875
- content_projection: bfloat16 [768, 768], replicated, may hold values from -0.21875 to 0.21875
- content_offset: bfloat16 [768], replicated, may hold values from -2 to 2
- mixing_result_projection: bfloat16 [768, 768], replicated, may hold values from -1.5 to 1.5
- mixing_result_offset: bfloat16 [768], replicated, may hold values from -2 to 2
- mixing_layernorm_scale: bfloat16 [768], replicated, may hold values from 0.5 to 1.5
- mixing_layernorm_offset: bfloat16 [768], replicated, may hold values from -2 to 2
- widening_projection: bfloat16 [768, 3072], replicated, may hold values from -0.21875 to 0.21875
- widening_offset: bfloat16 [3072], replicated, may hold values from -2 to 2
- narrowing_projection: bfloat16 [3072, 768], replicated, may hold values from -0.109375 to 0.109375
- narrowing_offset: bfloat16 [768], replicated, may hold values from -2 to 2
- perceptron_layernorm_scale: bfloat16 [768], replicated, may hold values from 0.5 to 1.5
- perceptron_layernorm_offset: bfloat16 [768], replicated, may hold values from -0.5 to 0.5
Outputs:
- loss: float32 [1], replicated
- pooled: float32 [32, 8, 768], P(('gx', 'gy'))
- grad_tokens: float32 [32, 512, 768], P(('gx', 'gy'))
- grad_w_query: float32 [768, 768], P('gy')
- grad_b_query: float32 [768], P('gy')
- grad_w_key: float32 [768, 768], P('gy')
- grad_w_value: float32 [768, 768], P('gy')
- grad_b_value: float32 [768], P('gy')
- grad_w_output: float32 [768, 768], P('gy')
- grad_b_output: float32 [768], P('gy')
- grad_gain_attn: float32 [768], P('gy')
- grad_shift_attn: float32 [768], P('gy')
- grad_w_inner: float32 [768, 3072], P('gy')
- grad_b_inner: float32 [3072], P('gy')
- grad_w_outer: float32 [3072, 768], P('gy')
- grad_b_outer: float32 [768], P('gy')
- grad_gain_ffn: float32 [768], P('gy')
- grad_shift_ffn: float32 [768], P('gy')
The draws below stay inside these ranges and needn't reach their ends.
Inputs may be any that keep to these rules, and one draw needn't show every extreme that they name: `piece_sizes`: segments alternate query, document, beginning with a query; a query has at most 32 tokens, a document at least 32; segments fill each row from its start and the rest of the row is padding. `matching_passage_number`: every document is the positive of exactly one query.
All inputs are finite; a program needn't handle non-finite values.
Results may differ from the reference program's by a relative error of at most 0.015.
Values may be sent and summed in bfloat16 or wider, within the bound.
No kernel may reach another device: no remote copies, remote signals or barrier semaphores. Data moves between devices by JAX's collectives and lax.ppermute only.
A program may use at most 192 MiB of HBM per device.

```python
import jax
import jax.numpy as jnp
from jax import lax

D = 768
HEADS = 12
HD = 64
FF = 3072
LEN = 512
SEG = 8
ROWS = 32
QUERIES = 128


def draw_piece_sizes(key, part):
    key = jax.random.fold_in(key, 11)
    key_query, key_doc, key_pick = jax.random.split(key, 3)
    short_low = max(1, LEN // 64)
    short_high = LEN // 16
    long_low = LEN // 16
    long_high = LEN * 11 // 64
    half = SEG // 2
    query_len = jax.random.randint(key_query, (ROWS, half), short_low, short_high + 1)
    doc_len = jax.random.randint(key_doc, (ROWS, half), long_low, long_high + 1)
    picked = jax.random.randint(key_pick, (), 0, ROWS * half)
    doc_len = doc_len.reshape(ROWS * half).at[picked].set(long_high).reshape(ROWS, half)
    return jnp.stack([query_len, doc_len], axis=2).reshape(ROWS, SEG).astype(jnp.int32)


def level_of(rng, shape, pieces, least, top_value):
    level = 1.0
    for axis_at, shards_of in pieces:
        heights = jax.random.uniform(jax.random.fold_in(jax.random.fold_in(rng, 6), axis_at), (shards_of,), jnp.float32, least / len(pieces), top_value / len(pieces))
        level = level * jnp.repeat(jnp.exp(heights), shape[axis_at] // shards_of).reshape((-1,) + (1,) * (len(shape) - 1 - axis_at))
    return level


def scatter_about(rng, dims, width, reach, pieces=(), kind=jnp.bfloat16):
    result = width * jax.random.normal(rng, dims, jnp.float32)
    if pieces:
        result = result * level_of(rng, dims, pieces, -0.22, 0.18)
    return jnp.clip(result, -reach, reach).astype(kind)


def setup_inputs(seed: int = 0) -> dict:
    key_of = jax.random.split(jax.random.key(seed), 20)
    return {
        "hidden_states_in": scatter_about(key_of[0], (ROWS, LEN, D), 1.0, 6.0, ((0, 32),)),
        "piece_sizes": draw_piece_sizes(jax.random.fold_in(key_of[19], 71), 0),
        "matching_passage_number": jax.random.permutation(key_of[2], QUERIES).astype(jnp.int32),
        "softmax_sharpness": jnp.clip(jax.random.uniform(key_of[3], (1,), jnp.float32, 0.02, 0.04), 0.02, 0.04),
        "question_projection": scatter_about(key_of[4], (D, D), D ** -0.5, 0.21875),
        "question_offset": scatter_about(key_of[5], (D,), 0.3, 2.0),
        "lookup_projection": scatter_about(key_of[6], (D, D), D ** -0.5, 0.21875),
        "content_projection": scatter_about(key_of[7], (D, D), D ** -0.5, 0.21875),
        "content_offset": scatter_about(key_of[8], (D,), 0.3, 2.0),
        "mixing_result_projection": scatter_about(key_of[9], (D, D), (max(1, D // 48)) ** -0.5, 1.5),
        "mixing_result_offset": scatter_about(key_of[10], (D,), 0.3, 2.0),
        "mixing_layernorm_scale": jnp.clip(1.0 + 0.1 * jax.random.normal(key_of[11], (D,), jnp.float32), 0.5, 1.5).astype(jnp.bfloat16),
        "mixing_layernorm_offset": scatter_about(key_of[12], (D,), 0.3, 2.0),
        "widening_projection": scatter_about(key_of[13], (D, FF), D ** -0.5, 0.21875),
        "widening_offset": scatter_about(key_of[14], (FF,), 0.3, 2.0),
        "narrowing_projection": scatter_about(key_of[15], (FF, D), FF ** -0.5, 0.109375),
        "narrowing_offset": scatter_about(key_of[16], (D,), 0.3, 2.0),
        "perceptron_layernorm_scale": jnp.clip(1.0 + 0.1 * jax.random.normal(key_of[17], (D,), jnp.float32), 0.5, 1.5).astype(jnp.bfloat16),
        "perceptron_layernorm_offset": scatter_about(key_of[18], (D,), 0.05, 0.5),
    }


@jax.custom_vjp
def low(v):
    return lax.optimization_barrier(v.astype(jnp.bfloat16)).astype(jnp.float32)

@jax.custom_vjp
def low_back(v):
    return v

def low_keep(v):
    return (low(v), None)

def low_pass(kept, grad):
    return (grad,)

def back_keep(v):
    return (v, None)

def back_low(kept, grad):
    return (low(grad),)
low.defvjp(low_keep, low_pass)
low_back.defvjp(back_keep, back_low)
EPS_NORM = 1e-12
EPS_UNIT = 1e-06
NEG_FILL = -1e+30
FULL_ACCURACY = lax.Precision.HIGHEST

def membership(lengths_row, length):
    seg_ends = jnp.cumsum(lengths_row)
    seg_starts = seg_ends - lengths_row
    places = jnp.arange(length, dtype=jnp.int32)
    return (places[None, :] >= seg_starts[:, None]) & (places[None, :] < seg_ends[:, None])

def normalize(hidden, gain, shift):
    center = hidden - lax.optimization_barrier(jnp.mean(hidden, axis=-1, keepdims=True))
    spread = lax.optimization_barrier(jnp.mean(center * center, axis=-1, keepdims=True))
    return center * lax.rsqrt(spread + EPS_NORM) * gain + shift

def row_forward(learned_parameters, x_row, lengths_row):
    question_projection, question_offset, lookup_projection, content_projection, content_offset, mixing_result_projection, mixing_result_offset, mixing_layernorm_scale, mixing_layernorm_offset, widening_projection, widening_offset, narrowing_projection, narrowing_offset, perceptron_layernorm_scale, perceptron_layernorm_offset = learned_parameters
    member = membership(lengths_row, LEN)
    numbers = jnp.arange(1, SEG + 1, dtype=jnp.int32)
    seg_of = lax.optimization_barrier(jnp.sum(member.astype(jnp.int32) * numbers[:, None], axis=0)) - 1
    allowed = seg_of[:, None] == seg_of[None, :]
    queries = low(low_back(jnp.dot(x_row, question_projection, precision=FULL_ACCURACY) + question_offset)).reshape(LEN, HEADS, HD)
    keys_proj = low(low_back(jnp.dot(x_row, lookup_projection, precision=FULL_ACCURACY))).reshape(LEN, HEADS, HD)
    values = low(low_back(jnp.dot(x_row, content_projection, precision=FULL_ACCURACY) + content_offset)).reshape(LEN, HEADS, HD)
    scores = low_back(jnp.einsum('qhd,khd->hqk', queries, keys_proj, precision=FULL_ACCURACY) * HD ** (-0.5))
    scores = jnp.where(allowed[None], scores, NEG_FILL)
    probs = jax.nn.softmax(scores, axis=-1)
    attended = jnp.einsum('hqk,khd->qhd', low(probs), values, precision=FULL_ACCURACY).reshape(LEN, D)
    attn = low(low_back(attended))
    hidden_one = x_row + low_back(jnp.dot(attn, mixing_result_projection, precision=FULL_ACCURACY) + mixing_result_offset)
    out_one = normalize(hidden_one, mixing_layernorm_scale, mixing_layernorm_offset)
    inner_pre = low_back(jnp.dot(low(out_one), widening_projection, precision=FULL_ACCURACY) + widening_offset)
    inner_act = low(jax.nn.gelu(inner_pre, approximate=False))
    hidden_two = out_one + low_back(jnp.dot(inner_act, narrowing_projection, precision=FULL_ACCURACY) + narrowing_offset)
    out_two = normalize(hidden_two, perceptron_layernorm_scale, perceptron_layernorm_offset)
    sums = jnp.dot(member.astype(jnp.float32), out_two, precision=FULL_ACCURACY)
    return sums / lengths_row.astype(jnp.float32)[:, None]

def evaluate_layer(learned_parameters, hidden_state_reals, piece_sizes, matching_passage_number, softmax_sharpness):

    def one_row(element):
        return row_forward(learned_parameters, element[0], element[1])
    pooled = lax.map(jax.checkpoint(one_row), (hidden_state_reals, piece_sizes))
    units = pooled * lax.rsqrt(lax.optimization_barrier(jnp.sum(pooled * pooled, axis=-1, keepdims=True)) + EPS_UNIT)
    units = low(units)
    question_directions = units[:, 0::2].reshape(QUERIES, D)
    passage_directions = units[:, 1::2].reshape(QUERIES, D)
    cosine_score_table = low_back(jnp.dot(question_directions, passage_directions.T, precision=FULL_ACCURACY)) / softmax_sharpness[0]
    log_total = jax.nn.logsumexp(cosine_score_table, axis=1)
    chosen = matching_passage_number[:, None] == jnp.arange(QUERIES, dtype=jnp.int32)[None, :]
    positive = lax.optimization_barrier(jnp.sum(jnp.where(chosen, cosine_score_table, 0.0), axis=1))
    return (jnp.mean(log_total - positive), pooled)

def reference(hidden_states_in, piece_sizes, matching_passage_number, softmax_sharpness, question_projection, question_offset, lookup_projection, content_projection, content_offset, mixing_result_projection, mixing_result_offset, mixing_layernorm_scale, mixing_layernorm_offset, widening_projection, widening_offset, narrowing_projection, narrowing_offset, perceptron_layernorm_scale, perceptron_layernorm_offset):
    learned_parameters = tuple((item.astype(jnp.float32) for item in (question_projection, question_offset, lookup_projection, content_projection, content_offset, mixing_result_projection, mixing_result_offset, mixing_layernorm_scale, mixing_layernorm_offset, widening_projection, widening_offset, narrowing_projection, narrowing_offset, perceptron_layernorm_scale, perceptron_layernorm_offset)))
    hidden_state_reals = hidden_states_in.astype(jnp.float32)

    def objective(parameter_tuple, argument_tensors):
        return evaluate_layer(parameter_tuple, argument_tensors, piece_sizes, matching_passage_number, softmax_sharpness)
    loss, backward, pooled = jax.vjp(objective, learned_parameters, hidden_state_reals, has_aux=True)
    grad_weights, grad_tokens = backward(jnp.ones((), jnp.float32))
    return (loss.reshape(1), pooled, grad_tokens, grad_weights[0], grad_weights[1], grad_weights[2], grad_weights[3], grad_weights[4], grad_weights[5], grad_weights[6], grad_weights[7], grad_weights[8], grad_weights[9], grad_weights[10], grad_weights[11], grad_weights[12], grad_weights[13], grad_weights[14])
```

```python
import functools

import jax
import jax.numpy as jnp
import numpy as np
from jax import lax
from jax.experimental import pallas as pl
from jax.experimental.pallas import tpu as pltpu
from jax.sharding import PartitionSpec as P

HEADS = 12
HD = 64


EPS_NORM = 1e-12
EPS_UNIT = 1e-06
NEG_FILL = -1e30
FULL_ACCURACY = lax.Precision.HIGHEST


def membership(piece_sizes, length):
    seg_ends = jnp.cumsum(piece_sizes, axis=-1)
    seg_starts = seg_ends - piece_sizes
    places = jnp.arange(length, dtype=jnp.int32)
    return (places[None, None, :] >= seg_starts[:, :, None]) & (
        places[None, None, :] < seg_ends[:, :, None]
    )


def standardize(hidden):
    center = hidden - jnp.mean(hidden, axis=-1, keepdims=True)
    inv_scale = lax.rsqrt(jnp.mean(center * center, axis=-1, keepdims=True) + EPS_NORM)
    return (center * inv_scale, inv_scale)


def standardize_back(normed, inv_scale, grad_normed):
    mean_grad = jnp.mean(grad_normed, axis=-1, keepdims=True)
    mean_both = jnp.mean(grad_normed * normed, axis=-1, keepdims=True)
    return inv_scale * (grad_normed - mean_grad - normed * mean_both)


def gelu_slope(values):
    normal_cdf = 0.5 * (1.0 + lax.erf(values * 0.7071067811865476))
    normal_pdf = jnp.exp(-0.5 * values * values) * 0.3989422804014327
    return normal_cdf + values * normal_pdf


def contract_rows(left, right):
    return lax.dot_general(
        left, right, (((0,), (0,)), ((), ())), preferred_element_type=jnp.float32
    )


def reduce_along_second_axis(left, right):
    return lax.dot_general(
        left, right, (((1,), (1,)), ((), ())), preferred_element_type=jnp.float32
    )


def row_scores(row_query, row_keys, row_seg):
    allowed = row_seg[:, None] == row_seg[None, :]
    scores = jnp.einsum(
        "qhd,khd->hqk", row_query, row_keys, preferred_element_type=jnp.float32
    ) * HD ** (-0.5)
    return jnp.where(allowed[None], scores, NEG_FILL)


def attend_row(element):
    row_query, row_keys, row_values, row_seg = element
    scores = row_scores(row_query, row_keys, row_seg)
    top_score = jnp.max(scores, axis=-1, keepdims=True)
    expo = jnp.exp(scores - top_score)
    total = jnp.sum(expo, axis=-1, keepdims=True)
    probs_low = (expo / total).astype(jnp.bfloat16)
    mixed = jnp.einsum("hqk,khd->qhd", probs_low, row_values, preferred_element_type=jnp.float32)
    return (mixed.astype(jnp.bfloat16), (top_score + jnp.log(total))[..., 0])


def attend_back(element):
    row_query, row_keys, row_values, row_seg, row_lse, row_grad = element
    scores = row_scores(row_query, row_keys, row_seg)
    probs = jnp.exp(scores - row_lse[..., None])
    probs_low = probs.astype(jnp.bfloat16)
    grad_values = jnp.einsum(
        "hqk,qhd->khd", probs_low, row_grad, preferred_element_type=jnp.float32
    )
    grad_probs = jnp.einsum(
        "qhd,khd->hqk", row_grad, row_values, preferred_element_type=jnp.float32
    )
    inner = jnp.sum(grad_probs * probs, axis=-1, keepdims=True)
    grad_scores = (probs * (grad_probs - inner)).astype(jnp.bfloat16)
    grad_query = jnp.einsum(
        "hqk,khd->qhd", grad_scores, row_keys, preferred_element_type=jnp.float32
    ) * HD ** (-0.5)
    grad_keys = jnp.einsum(
        "hqk,qhd->khd", grad_scores, row_query, preferred_element_type=jnp.float32
    ) * HD ** (-0.5)
    return (
        grad_query.astype(jnp.bfloat16),
        grad_keys.astype(jnp.bfloat16),
        grad_values.astype(jnp.bfloat16),
    )


LANES = 128


def powers_below(count):
    bits = []
    bit = 1
    while bit < count:
        bits.append(bit)
        bit *= 2
    return bits


def swap_with(value, axis, bit):
    count = lax.axis_size(axis)
    return lax.ppermute(value, axis, [(i, i ^ bit) for i in range(count)])


def gather_steps():
    gy = powers_below(lax.axis_size("gy"))
    far = [("gy", bit) for bit in reversed(gy[2:])]
    near = [("gy", bit) for bit in reversed(gy[:2])]
    return far + [("gx", bit) for bit in powers_below(lax.axis_size("gx"))] + near


def gather_blocks(block):
    groups_y = lax.axis_size("gy")
    gathered = block[None]
    number = np.zeros((1,), np.int32)
    place = 0
    for step, (axis, bit) in enumerate(gather_steps()):
        other = swap_with(gathered, axis, bit)
        high = (lax.axis_index(axis) & bit) != 0
        gathered = jnp.concatenate(
            [jnp.where(high, other, gathered), jnp.where(high, gathered, other)], axis=0
        )
        number = np.concatenate([number, number + bit * (groups_y if axis == "gx" else 1)])
        place = place + jnp.where(high, 1 << step, 0)
    return gathered, number, place


def gradient_kernel(masks, share_rows, here_ref, left_ref, right_ref, keep_ref, send_ref, product):
    here = here_ref[0]
    product[...] = lax.dot_general(
        left_ref[...], right_ref[...], (((0,), (0,)), ((), ())), preferred_element_type=jnp.float32
    )
    rows = keep_ref.shape[2]
    parts = share_rows // rows
    tiles = right_ref.shape[1] // LANES
    for place, mask in enumerate(masks):
        target = keep_ref if place < len(masks) // 2 else send_ref
        spot = place % (len(masks) // 2)
        share = jnp.bitwise_xor(here, mask)
        start = pl.multiple_of(share * share_rows, 8)
        for tile in range(tiles):
            for part in range(parts):
                target[spot, tile * parts + part] = product[
                    pl.ds(start + part * rows, rows), tile * LANES : (tile + 1) * LANES
                ].astype(target.dtype)


def packed_gradient(left, right, order, rows):
    groups_y = lax.axis_size("gy")
    tokens, outer = left.shape
    share_rows = outer // groups_y
    parts = share_rows // rows
    wide = min(right.shape[1], 2 * LANES)
    tiles = wide // LANES
    blocks = right.shape[1] // LANES * parts
    masks = place_masks([1] + order)
    here = lax.axis_index("gy").astype(jnp.int32).reshape(1)
    half = groups_y // 2
    shape = jax.ShapeDtypeStruct((half, blocks, rows, LANES), jnp.bfloat16)
    return pl.pallas_call(
        functools.partial(gradient_kernel, masks, share_rows),
        grid=(right.shape[1] // wide,),
        in_specs=[
            pl.BlockSpec(memory_space=pltpu.SMEM),
            pl.BlockSpec((tokens, outer), lambda i: (0, 0)),
            pl.BlockSpec((tokens, wide), lambda i: (0, i)),
        ],
        out_specs=[pl.BlockSpec((half, tiles * parts, rows, LANES), lambda i: (0, i, 0, 0))] * 2,
        out_shape=[shape, shape],
        scratch_shapes=[pltpu.VMEM((outer, wide), jnp.float32)],
        compiler_params=pltpu.CompilerParams(vmem_limit_bytes=48 * 1024 * 1024),
        cost_estimate=pl.CostEstimate(
            flops=2 * tokens * outer * right.shape[1],
            bytes_accessed=2 * (tokens * outer + tokens * right.shape[1] + outer * right.shape[1]),
            transcendentals=0,
        ),
    )(here, left, right)


def place_masks(bits):
    masks = [0]
    for bit in reversed(bits):
        masks = masks + [mask ^ bit for mask in masks]
    return masks


def widen(value):
    return value.astype(jnp.float32)


def halve(current, axis, bit):
    half = current.shape[0] // 2
    received = swap_with(current[half:].astype(jnp.bfloat16), axis, bit)
    return widen(current[:half]) + widen(received)


def swap_sum(current, axis, bit):
    mine = current.astype(jnp.bfloat16)
    return widen(mine) + widen(swap_with(mine, axis, bit))


def reduce_chunk(keep, send, order, first_gx):
    gx_bits = powers_below(lax.axis_size("gx"))
    current = widen(keep) + widen(swap_with(send, "gy", 1))
    if first_gx:
        high = (lax.axis_index("gx") & 1) != 0
        half = current.shape[1] // 2
        lower, upper = current[:, :half], current[:, half:]
        give = jnp.where(high, lower, upper).astype(jnp.bfloat16)
        current = jnp.where(high, upper, lower) + widen(swap_with(give, "gx", 1))
    for bit in order:
        current = halve(current, "gy", bit)
    for bit in gx_bits[1:] if first_gx else gx_bits:
        current = swap_sum(current, "gx", bit)
    current = current[0]
    if first_gx:
        mine = current.astype(jnp.bfloat16)
        other = swap_with(mine, "gx", 1)
        current = widen(
            jnp.concatenate([jnp.where(high, other, mine), jnp.where(high, mine, other)], axis=0)
        )
    return current


def share_of(blocks, columns):
    tiles = columns // LANES
    count, rows, _ = blocks.shape
    parts = count // tiles
    view = blocks.reshape(tiles, parts, rows, LANES)
    return view.transpose(1, 2, 0, 3).reshape(parts * rows, columns)


def body(
    hidden_states_in,
    piece_sizes,
    matching_passage_number,
    softmax_sharpness,
    question_projection,
    question_offset,
    lookup_projection,
    content_projection,
    content_offset,
    mixing_result_projection,
    mixing_result_offset,
    mixing_layernorm_scale,
    mixing_layernorm_offset,
    widening_projection,
    widening_offset,
    narrowing_projection,
    narrowing_offset,
    perceptron_layernorm_scale,
    perceptron_layernorm_offset,
):
    rows_here, length, width = hidden_states_in.shape
    count_tokens = rows_here * length
    segments = piece_sizes.shape[1]
    half = segments // 2
    flat_tokens = hidden_states_in.reshape(count_tokens, width)
    member = membership(piece_sizes, length)
    numbers = jnp.arange(1, segments + 1, dtype=jnp.int32)
    token_seg = jnp.sum(member.astype(jnp.int32) * numbers[None, :, None], axis=1) - 1
    queries = (
        jnp.dot(flat_tokens, question_projection, preferred_element_type=jnp.float32)
        + question_offset
    ).astype(jnp.bfloat16)
    keys_proj = jnp.dot(flat_tokens, lookup_projection, preferred_element_type=jnp.float32).astype(
        jnp.bfloat16
    )
    values = (
        jnp.dot(flat_tokens, content_projection, preferred_element_type=jnp.float32)
        + content_offset
    ).astype(jnp.bfloat16)
    head_shape = (rows_here, length, HEADS, HD)
    query_rows = queries.reshape(head_shape)
    key_rows = keys_proj.reshape(head_shape)
    value_rows = values.reshape(head_shape)
    attn_rows, lse_rows = lax.map(attend_row, (query_rows, key_rows, value_rows, token_seg))
    attn_flat = attn_rows.reshape(count_tokens, width)
    hidden_one = (
        flat_tokens.astype(jnp.float32)
        + jnp.dot(attn_flat, mixing_result_projection, preferred_element_type=jnp.float32)
        + mixing_result_offset
    )
    normed_one, inv_one = standardize(hidden_one)
    out_one = normed_one * mixing_layernorm_scale + mixing_layernorm_offset
    out_one_low = out_one.astype(jnp.bfloat16)
    inner_pre = (
        jnp.dot(out_one_low, widening_projection, preferred_element_type=jnp.float32)
        + widening_offset
    )
    inner_low = jax.nn.gelu(inner_pre, approximate=False).astype(jnp.bfloat16)
    hidden_two = (
        out_one
        + jnp.dot(inner_low, narrowing_projection, preferred_element_type=jnp.float32)
        + narrowing_offset
    )
    normed_two, inv_two = standardize(hidden_two)
    out_two = normed_two * perceptron_layernorm_scale + perceptron_layernorm_offset
    member_f = member.astype(jnp.float32)
    counts = piece_sizes.astype(jnp.float32)[..., None]
    pooled = (
        jnp.einsum(
            "rsl,rld->rsd",
            member_f,
            out_two.reshape(rows_here, length, width),
            precision=FULL_ACCURACY,
        )
        / counts
    )
    inv_norm = lax.rsqrt(jnp.sum(pooled * pooled, axis=-1, keepdims=True) + EPS_UNIT)
    units = pooled * inv_norm
    units_low = units.astype(jnp.bfloat16)
    here_units = units_low.reshape(rows_here * half, 2, width)
    low_digits = matching_passage_number & 255
    high_digits = matching_passage_number >> 8
    digits = jnp.concatenate([low_digits, high_digits]).astype(jnp.bfloat16)
    per_device = rows_here * half
    message = jnp.concatenate(
        [
            here_units[:, 0],
            here_units[:, 1],
            jnp.zeros((8, width), jnp.bfloat16).at[0, : 2 * per_device].set(digits),
        ],
        axis=0,
    )
    gathered, numbers_of, place = gather_blocks(message)
    total_docs = numbers_of.shape[0] * per_device
    questions = gathered[:, :per_device].reshape(total_docs, width)
    passages = gathered[:, per_device : 2 * per_device].reshape(total_docs, width)
    all_digits = gathered[:, 2 * per_device, : 2 * per_device].astype(jnp.int32)
    matching = (all_digits[:, :per_device] + 256 * all_digits[:, per_device:]).reshape(total_docs)
    passage_numbers = jnp.asarray(
        (numbers_of[:, None] * per_device + np.arange(per_device)[None, :]).reshape(total_docs),
        jnp.int32,
    )
    cosine_score_table = reduce_along_second_axis(questions, passages) / softmax_sharpness[0]
    sim_top = jnp.max(cosine_score_table, axis=1, keepdims=True)
    sim_exp = jnp.exp(cosine_score_table - sim_top)
    sim_total = jnp.sum(sim_exp, axis=1, keepdims=True)
    log_total = sim_top[:, 0] + jnp.log(sim_total[:, 0])
    chosen = matching[:, None] == passage_numbers[None, :]
    positive = jnp.sum(jnp.where(chosen, cosine_score_table, 0.0), axis=1)
    loss_out = (jnp.sum(log_total - positive) / total_docs).reshape(1)
    cosine_score_derivative = (sim_exp / sim_total - chosen.astype(jnp.float32)) / total_docs
    cotangent = (cosine_score_derivative / softmax_sharpness[0]).astype(jnp.bfloat16)
    row_terms = lax.dynamic_slice_in_dim(cotangent, place * per_device, per_device, axis=0)
    column_terms = lax.dynamic_slice_in_dim(cotangent, place * per_device, per_device, axis=1)
    grad_query_units = jnp.dot(row_terms, passages, preferred_element_type=jnp.float32)
    grad_doc_units = contract_rows(column_terms, questions)
    grad_units = jnp.stack(
        [
            grad_query_units.reshape(rows_here, half, width),
            grad_doc_units.reshape(rows_here, half, width),
        ],
        axis=2,
    ).reshape(rows_here, segments, width)
    along = jnp.sum(units * grad_units, axis=-1, keepdims=True)
    grad_pooled = inv_norm * (grad_units - units * along)
    grad_out_two = jnp.einsum(
        "rsl,rsd->rld", member_f, grad_pooled / counts, precision=FULL_ACCURACY
    ).reshape(count_tokens, width)
    grad_gain_ffn = jnp.sum(grad_out_two * normed_two, axis=0)
    grad_shift_ffn = jnp.sum(grad_out_two, axis=0)
    grad_hidden_two = standardize_back(
        normed_two, inv_two, grad_out_two * perceptron_layernorm_scale
    )
    grad_branch_two = grad_hidden_two.astype(jnp.bfloat16)
    grad_b_outer = jnp.sum(grad_branch_two, axis=0, dtype=jnp.float32)
    gy_bits = powers_below(lax.axis_size("gy"))[1:]
    rows = width // lax.axis_size("gy")
    x_first = gy_bits
    z_first = gy_bits[1:] + gy_bits[:1]
    outer_keep, outer_send = packed_gradient(inner_low, grad_branch_two, x_first, rows)
    grad_w_outer = reduce_chunk(outer_keep, outer_send, x_first, False)
    grad_act = reduce_along_second_axis(grad_branch_two, narrowing_projection)
    grad_pre = (grad_act * gelu_slope(inner_pre)).astype(jnp.bfloat16)
    grad_b_inner = jnp.sum(grad_pre, axis=0, dtype=jnp.float32)
    inner_keep, inner_send = packed_gradient(out_one_low, grad_pre, x_first, rows)
    grad_w_inner = reduce_chunk(inner_keep, inner_send, x_first, True)
    grad_out_one = grad_hidden_two + reduce_along_second_axis(grad_pre, widening_projection)
    grad_gain_attn = jnp.sum(grad_out_one * normed_one, axis=0)
    grad_shift_attn = jnp.sum(grad_out_one, axis=0)
    grad_hidden_one = standardize_back(normed_one, inv_one, grad_out_one * mixing_layernorm_scale)
    grad_branch_one = grad_hidden_one.astype(jnp.bfloat16)
    grad_b_output = jnp.sum(grad_branch_one, axis=0, dtype=jnp.float32)
    grad_attn = reduce_along_second_axis(grad_branch_one, mixing_result_projection).astype(
        jnp.bfloat16
    )
    grad_q_rows, grad_k_rows, grad_v_rows = lax.map(
        attend_back,
        (query_rows, key_rows, value_rows, token_seg, lse_rows, grad_attn.reshape(head_shape)),
    )
    grad_queries = grad_q_rows.reshape(count_tokens, width)
    grad_keys = grad_k_rows.reshape(count_tokens, width)
    grad_values = grad_v_rows.reshape(count_tokens, width)
    grad_b_query = jnp.sum(grad_queries, axis=0, dtype=jnp.float32)
    grad_b_value = jnp.sum(grad_values, axis=0, dtype=jnp.float32)
    grad_tokens = (
        grad_hidden_one
        + reduce_along_second_axis(grad_queries, question_projection)
        + reduce_along_second_axis(grad_keys, lookup_projection)
        + reduce_along_second_axis(grad_values, content_projection)
    )
    packed = [
        packed_gradient(left, right, z_first, rows)
        for left, right in (
            (flat_tokens, grad_queries),
            (flat_tokens, grad_keys),
            (flat_tokens, grad_values),
            (attn_flat, grad_branch_one),
        )
    ]
    groups_y = lax.axis_size("gy")
    narrow = [
        grad_b_query,
        grad_b_value,
        grad_b_output,
        grad_gain_attn,
        grad_shift_attn,
        grad_b_outer,
        grad_gain_ffn,
        grad_shift_ffn,
        grad_b_inner,
    ]
    columns = [item.reshape(width, -1) for item in narrow]
    used = sum(item.shape[1] for item in columns)
    columns = jnp.concatenate(columns + [jnp.zeros((width, LANES - used), jnp.float32)], axis=1)
    columns = columns.reshape(groups_y, 1, rows, LANES).astype(jnp.bfloat16)
    masks = jnp.asarray(place_masks([1] + z_first), jnp.int32)
    columns = jnp.take(columns, jnp.bitwise_xor(masks, lax.axis_index("gy")), axis=0)
    keep = jnp.concatenate([keep for keep, _ in packed] + [columns[: groups_y // 2]], axis=1)
    send = jnp.concatenate([send for _, send in packed] + [columns[groups_y // 2 :]], axis=1)
    attn_sums = reduce_chunk(keep, send, z_first, False)
    tiles = width // LANES
    grad_w_query, grad_w_key, grad_w_value, grad_w_output = [
        share_of(attn_sums[i * tiles : (i + 1) * tiles], width) for i in range(4)
    ]
    narrow_sums = attn_sums[4 * tiles]
    vectors = [narrow_sums[:, i] for i in range(8)]
    b_query, b_value, b_output, gain_attn, shift_attn, b_outer, gain_ffn, shift_ffn = vectors
    return (
        loss_out,
        pooled,
        grad_tokens.reshape(rows_here, length, width),
        grad_w_query,
        b_query,
        grad_w_key,
        grad_w_value,
        b_value,
        grad_w_output,
        b_output,
        gain_attn,
        shift_attn,
        share_of(grad_w_inner, widening_offset.shape[0]),
        narrow_sums[:, 8:used].reshape(-1),
        share_of(grad_w_outer, width),
        b_outer,
        gain_ffn,
        shift_ffn,
    )


def solution(mesh):
    return jax.shard_map(
        body,
        mesh=mesh,
        in_specs=(
            P(("gx", "gy"), None, None),
            P(("gx", "gy"), None),
            P(("gx", "gy")),
            P(),
            P(),
            P(),
            P(),
            P(),
            P(),
            P(),
            P(),
            P(),
            P(),
            P(),
            P(),
            P(),
            P(),
            P(),
            P(),
        ),
        out_specs=(
            P(),
            P(("gx", "gy"), None, None),
            P(("gx", "gy"), None, None),
            P("gy", None),
            P("gy"),
            P("gy", None),
            P("gy", None),
            P("gy"),
            P("gy", None),
            P("gy"),
            P("gy"),
            P("gy"),
            P("gy", None),
            P("gy"),
            P("gy", None),
            P("gy"),
            P("gy"),
            P("gy"),
        ),
        check_vma=False,
    )
```

```python
import functools

import jax
import jax.numpy as jnp
import numpy as np
from jax import lax
from jax.experimental import pallas as pl
from jax.experimental.pallas import tpu as pltpu
from jax.sharding import PartitionSpec as P

HEADS = 12
HD = 64
LANES = 128
VMEM_BYTES = 60 * 1024 * 1024

EPS_NORM = 1e-12
EPS_UNIT = 1e-06
NEG_FILL = -1e30


def standardize(hidden):
    center = hidden - jnp.mean(hidden, axis=-1, keepdims=True)
    inv_scale = lax.rsqrt(jnp.mean(center * center, axis=-1, keepdims=True) + EPS_NORM)
    return (center * inv_scale, inv_scale)


def standardize_back(normed, inv_scale, grad_normed):
    mean_grad = jnp.mean(grad_normed, axis=-1, keepdims=True)
    mean_both = jnp.mean(grad_normed * normed, axis=-1, keepdims=True)
    return inv_scale * (grad_normed - mean_grad - normed * mean_both)


def widen(value):
    return value.astype(jnp.float32)


def powers_below(count):
    bits = []
    bit = 1
    while bit < count:
        bits.append(bit)
        bit *= 2
    return bits


def place_masks(bits):
    masks = [0]
    for bit in reversed(bits):
        masks = masks + [mask ^ bit for mask in masks]
    return masks


def swap_with(value, axis, bit):
    count = lax.axis_size(axis)
    return lax.ppermute(value, axis, [(i, i ^ bit) for i in range(count)])


def tie(*values):
    return lax.optimization_barrier(values)


def gather_steps():
    gy = powers_below(lax.axis_size("gy"))
    far = [("gy", bit) for bit in reversed(gy[2:])]
    near = [("gy", bit) for bit in reversed(gy[:2])]
    return far + [("gx", bit) for bit in powers_below(lax.axis_size("gx"))] + near


def gather_blocks(block, beside):
    groups_y = lax.axis_size("gy")
    gathered = block[None]
    number = np.zeros((1,), np.int32)
    place = 0
    for step, (axis, bit) in enumerate(gather_steps()):
        if step == 3:
            gathered, beside = tie(gathered, beside)
        gathered = jnp.concatenate([gathered, swap_with(gathered, axis, bit)], axis=0)
        high = (lax.axis_index(axis) & bit) != 0
        number = np.concatenate([number, number + bit * (groups_y if axis == "gx" else 1)])
        place = place + jnp.where(high, 1 << step, 0)
    return gathered, number, place, beside


def add_halves(keep, got):
    half = keep.shape[0] // 2
    kept = widen(keep[:half]) + widen(got[:half])
    return kept, (widen(keep[half:]) + widen(got[half:])).astype(jnp.bfloat16)


def swap_sum(current, axis, bit):
    mine = current.astype(jnp.bfloat16)
    return widen(mine) + widen(swap_with(mine, axis, bit))


def sum_over_gx(current, bits):
    for bit in bits:
        current = swap_sum(current, "gx", bit)
    return current


def finish_shares(keep, got, bits):
    for bit in bits:
        keep, send = add_halves(keep, got)
        got = swap_with(send, "gy", bit)
    return widen(keep[0]) + widen(got[0])


def gather_over_gx(mine):
    mine = mine.astype(jnp.bfloat16)
    other = swap_with(mine, "gx", 1)
    high = (lax.axis_index("gx") & 1) != 0
    return widen(
        jnp.concatenate([jnp.where(high, other, mine), jnp.where(high, mine, other)], axis=0)
    )


def halve_row(current, bit):
    half = current.shape[0] // 2
    lower, upper = current[:half], current[half:]
    high = (lax.axis_index("gy") & bit) != 0
    received = swap_with(jnp.where(high, lower, upper), "gy", bit)
    return jnp.where(high, upper, lower) + received


def share_of(blocks, columns):
    tiles = columns // LANES
    count, rows, _ = blocks.shape
    parts = count // tiles
    view = blocks.reshape(tiles, parts, rows, LANES)
    return view.transpose(1, 2, 0, 3).reshape(parts * rows, columns)


def compiler_params():
    return pltpu.CompilerParams(vmem_limit_bytes=VMEM_BYTES)


def dot_nt(left, right):
    return lax.dot_general(
        left, right, (((1,), (1,)), ((), ())), preferred_element_type=jnp.float32
    )


def dot_nn(left, right):
    return jnp.dot(left, right, preferred_element_type=jnp.float32)


def start_all(copies):
    for copy in copies:
        copy.start()


def wait_all(copies):
    for copy in copies:
        copy.wait()


def as_row(ref):
    return ref[...].astype(jnp.float32).reshape(1, ref.shape[0])


def lengths_as_row(sizes_ref, lanes, segments):
    lane = lax.broadcasted_iota(jnp.int32, (1, lanes), 1) % segments
    start = jnp.zeros((1, lanes), jnp.int32)
    end = jnp.zeros((1, lanes), jnp.int32)
    at = jnp.int32(0)
    for segment in range(segments):
        size = sizes_ref[0, segment]
        start = jnp.where(lane == segment, at, start)
        at = at + size
        end = jnp.where(lane == segment, at, end)
    return start, end


def counts_as_column(sizes_ref, segments):
    row = lax.broadcasted_iota(jnp.int32, (segments, 1), 0)
    counts = jnp.zeros((segments, 1), jnp.float32)
    for segment in range(segments):
        counts = jnp.where(row == segment, sizes_ref[0, segment].astype(jnp.float32), counts)
    return counts


def starts_as_column(sizes_ref, segments):
    row = lax.broadcasted_iota(jnp.int32, (segments, 1), 0)
    start = jnp.zeros((segments, 1), jnp.int32)
    end = jnp.zeros((segments, 1), jnp.int32)
    at = jnp.int32(0)
    for segment in range(segments):
        size = sizes_ref[0, segment]
        start = jnp.where(row == segment, at, start)
        at = at + size
        end = jnp.where(row == segment, at, end)
    return start, end


def band(length):
    return [(0, length // 2, 0, 3 * length // 4), (length // 2, length, length // 4, length)]


def mask_of(sizes_ref, segments, query_at, query_end, key_at, key_end):
    query = query_at + lax.broadcasted_iota(jnp.int32, (1, query_end - query_at), 1)
    low = jnp.zeros_like(query)
    high = jnp.zeros_like(query)
    at = jnp.int32(0)
    for segment in range(segments):
        end = at + sizes_ref[0, segment]
        inside = (query >= at) & (query < end)
        low = jnp.where(inside, at, low)
        high = jnp.where(inside, end, high)
        at = end
    padding = query >= at
    low = jnp.where(padding, at, low)
    high = jnp.where(padding, key_end, high)
    key = key_at + lax.broadcasted_iota(jnp.int32, (key_end - key_at, query_end - query_at), 0)
    return jnp.where((key >= low) & (key < high), 0.0, NEG_FILL)


def vmem_spec():
    return pl.BlockSpec(memory_space=pltpu.VMEM)


def smem_spec():
    return pl.BlockSpec(memory_space=pltpu.SMEM)


def any_spec():
    return pl.BlockSpec(memory_space=pltpu.HBM)


def cost(microseconds):
    return pl.CostEstimate(
        flops=int(microseconds * 1.1e9), bytes_accessed=1000000, transcendentals=0
    )


def forward_kernel(segments, masks_x, masks_z, here_ref, sizes_ref, matching_ref, *refs):
    given, refs = refs[:16], refs[16:]
    results, refs = refs[:14], refs[14:]
    side_own, side_send = results[-2:]
    local, refs = refs[:16], refs[16:]
    made, refs = refs[:12], refs[12:]
    (
        tokens_ref,
        question_w,
        lookup_w,
        content_w,
        mixing_w,
        widening_w,
        narrowing_w,
        question_row,
        content_row,
        mixing_row,
        gain_one_row,
        shift_one_row,
        widening_row,
        narrowing_row,
        gain_two_row,
        shift_two_row,
    ) = local
    (
        query_ref,
        key_ref,
        key_t_ref,
        value_ref,
        lse_ref,
        normed_one_ref,
        inv_one_ref,
        slope_ref,
        normed_two_ref,
        inv_two_ref,
        pooled_ref,
        message_ref,
    ) = made
    value_t, token_t, attn_t, out_one_t, inner_t, fill = refs[:6]
    out_one, out_one_low, total, in_sems, out_sems, side_sems = refs[6:]
    length, width = tokens_ref.shape
    hidden_units = widening_w.shape[1]
    here = here_ref[0]
    share_rows = side_own.shape[1] // (hidden_units // width + 3)
    inner_rows = hidden_units // width * share_rows
    first_rows = inner_rows // 2
    copies = [
        pltpu.make_async_copy(source, target, in_sems.at[i])
        for i, (source, target) in enumerate(zip(given, local))
    ]
    outward = [
        pltpu.make_async_copy(source, target, out_sems.at[i])
        for i, (source, target) in enumerate(zip(made, results))
    ]
    side_copies = []

    def send_side(source, source_rows, offset, count, at, masks):
        for place, mask in enumerate(masks):
            for flip, target in enumerate((side_own, side_send)):
                share = jnp.bitwise_xor(here, mask ^ flip)
                first = pl.multiple_of(share * source_rows + offset, 8)
                copy = pltpu.make_async_copy(
                    source.at[pl.ds(first, count)],
                    target.at[place, pl.ds(at, count)],
                    side_sems.at[len(side_copies)],
                )
                copy.start()
                side_copies.append(copy)

    start_all(copies)
    ranges = band(length)
    for i, (query_at, query_end, key_at, key_end) in enumerate(ranges):
        fill[i] = mask_of(sizes_ref, segments, query_at, query_end, key_at, key_end)
    wait_all(copies[7:])
    copies[0].wait()
    token_t[...] = tokens_ref[...].T
    send_side(token_t, share_rows, 0, share_rows, inner_rows + share_rows, masks_x)
    wide = 2 * LANES
    copies[1].wait()
    for at in range(0, width, wide):
        product = dot_nn(tokens_ref[...], question_w[:, at : at + wide])
        product = (product + as_row(question_row)[:, at : at + wide]).astype(jnp.bfloat16)
        query_ref[:, at : at + wide] = product * jnp.bfloat16(HD ** (-0.5))
    copies[2].wait()
    for at in range(0, width, wide):
        product = dot_nn(tokens_ref[...], lookup_w[:, at : at + wide]).astype(jnp.bfloat16)
        key_ref[:, at : at + wide] = product
        key_t_ref[at : at + wide, :] = product.T
    copies[3].wait()
    for at in range(0, width, wide):
        product = dot_nn(tokens_ref[...], content_w[:, at : at + wide])
        product = (product + as_row(content_row)[:, at : at + wide]).astype(jnp.bfloat16)
        value_ref[:, at : at + wide] = product
        value_t[at : at + wide, :] = product.T
    start_all(outward[:4])
    lane = lax.broadcasted_iota(jnp.int32, (1, LANES), 1)
    for pair in range(width // LANES):
        lanes = slice(pair * LANES, (pair + 1) * LANES)
        for i, (query_at, query_end, key_at, key_end) in enumerate(ranges):
            keys = key_ref[key_at:key_end, lanes]
            for which in range(LANES // HD):
                at = pair * (LANES // HD) + which
                query = jnp.where((lane // HD) == which, query_ref[query_at:query_end, lanes], 0)
                scores = dot_nt(keys, query) + fill[i]
                top = jnp.max(scores, axis=0, keepdims=True)
                expo = jnp.exp(scores - top)
                norm = jnp.sum(expo, axis=0, keepdims=True)
                probs = (expo * (1.0 / norm)).astype(jnp.bfloat16)
                lse_ref[at : at + 1, query_at:query_end] = top + jnp.log(norm)
                mixed = dot_nn(value_t[at * HD : (at + 1) * HD, key_at:key_end], probs)
                attn_t[at * HD : (at + 1) * HD, query_at:query_end] = mixed.astype(
                    jnp.bfloat16
                )
    outward[4].start()
    send_side(attn_t, share_rows, 0, share_rows, inner_rows + 2 * share_rows, masks_x)
    copies[4].wait()
    chunk = min(length, 128)
    for at in range(0, length, chunk):
        rows = slice(at, at + chunk)
        hidden = (
            tokens_ref[rows].astype(jnp.float32)
            + dot_nn(attn_t[:, rows].T, mixing_w[...])
            + as_row(mixing_row)
        )
        normed, inv = standardize(hidden)
        normed_one_ref[rows] = normed
        inv_one_ref[rows] = inv
        shifted = normed * as_row(gain_one_row) + as_row(shift_one_row)
        out_one[rows] = shifted
        low = shifted.astype(jnp.bfloat16)
        out_one_low[rows] = low
        out_one_t[:, rows] = low.T
        total[rows] = shifted + as_row(narrowing_row)
    start_all(outward[5:7])
    send_side(out_one_t, share_rows, 0, share_rows, inner_rows, masks_x)
    copies[5].wait()
    copies[6].wait()
    tile = 2 * LANES

    def widen_tile(step, carry):
        at = pl.multiple_of(step * tile, tile)
        inner_parts = []
        for row in range(0, length, chunk):
            rows = slice(row, row + chunk)
            before = (
                dot_nn(out_one_low[rows], widening_w[:, pl.ds(at, tile)])
                + widening_row[pl.ds(at, tile)].astype(jnp.float32).reshape(1, tile)
            )
            cdf = 0.5 * (1.0 + lax.erf(before * 0.7071067811865476))
            pdf = jnp.exp(-0.5 * before * before) * 0.3989422804014327
            inner = (before * cdf).astype(jnp.bfloat16)
            slope_ref[rows, pl.ds(at, tile)] = (cdf + before * pdf).astype(jnp.bfloat16)
            inner_t[pl.ds(at, tile), rows] = inner.T
            total[rows] += dot_nn(inner, narrowing_w[pl.ds(at, tile), :])
        return carry

    lax.fori_loop(0, hidden_units // tile, widen_tile, 0)
    outward[7].start()
    send_side(inner_t, inner_rows, 0, first_rows, 0, masks_x)
    send_side(inner_t, inner_rows, first_rows, inner_rows - first_rows, first_rows, masks_z)
    start, end = starts_as_column(sizes_ref, segments)
    sums = jnp.zeros((segments, width), jnp.float32)
    for at in range(0, length, chunk):
        rows = slice(at, at + chunk)
        normed, inv = standardize(total[rows])
        normed_two_ref[rows] = normed
        inv_two_ref[rows] = inv
        out_two = normed * as_row(gain_two_row) + as_row(shift_two_row)
        upper = out_two.astype(jnp.bfloat16)
        lower = (out_two - upper.astype(jnp.float32)).astype(jnp.bfloat16)
        token = at + lax.broadcasted_iota(jnp.int32, (segments, chunk), 1)
        member = jnp.where((token >= start) & (token < end), 1.0, 0.0).astype(jnp.bfloat16)
        sums = sums + dot_nn(member, upper) + dot_nn(member, lower)
    pooled = sums / counts_as_column(sizes_ref, segments)
    pooled_ref[...] = pooled
    inv_norm = lax.rsqrt(jnp.sum(pooled * pooled, axis=1, keepdims=True) + EPS_UNIT)
    units = (pooled * inv_norm).astype(jnp.bfloat16)
    half = segments // 2
    place = lax.broadcasted_iota(jnp.int32, (segments, segments), 0)
    source = lax.broadcasted_iota(jnp.int32, (segments, segments), 1)
    wanted = jnp.where(place < half, 2 * place, 2 * (place - half) + 1)
    pick = jnp.where(source == wanted, 1.0, 0.0).astype(jnp.bfloat16)
    message_ref[:, :width] = dot_nn(pick, units).astype(jnp.bfloat16)
    row = lax.broadcasted_iota(jnp.int32, (segments, LANES), 0)
    column = lax.broadcasted_iota(jnp.int32, (segments, LANES), 1)
    digits = jnp.zeros((segments, LANES), jnp.float32)
    for i in range(half):
        number = matching_ref[i]
        digit = jnp.where(column == 0, number & 255, number >> 8).astype(jnp.float32)
        digits = jnp.where((row == i) & (column < 2), digit, digits)
    message_ref[:, width:] = digits.astype(jnp.bfloat16)
    start_all(outward[8:])
    wait_all(outward)
    wait_all(side_copies)


def forward_step(here, sizes, matching, masks_x, masks_z, given):
    tokens, hidden_units = given[0], given[5].shape[1]
    length, width = tokens.shape
    segments = sizes.shape[1]
    half = len(masks_x)
    query_at, query_end, key_at, key_end = band(length)[0]
    low, full = jnp.bfloat16, jnp.float32
    side = ((half, (hidden_units // width + 3) * (width // half // 2), length), low)
    made = [
        ((length, width), low),
        ((length, width), low),
        ((width, length), low),
        ((length, width), low),
        ((HEADS, length), full),
        ((length, width), full),
        ((length, 1), full),
        ((length, hidden_units), low),
        ((length, width), full),
        ((length, 1), full),
        ((segments, width), full),
        ((segments, width + LANES), low),
    ]
    return pl.pallas_call(
        functools.partial(forward_kernel, segments, masks_x, masks_z),
        in_specs=[smem_spec()] * 3 + [any_spec()] * len(given),
        out_specs=[any_spec()] * (len(made) + 2),
        out_shape=[jax.ShapeDtypeStruct(shape, kind) for shape, kind in made + [side, side]],
        scratch_shapes=[pltpu.VMEM(item.shape, item.dtype) for item in given]
        + [pltpu.VMEM(shape, kind) for shape, kind in made]
        + [
            pltpu.VMEM((width, length), low),
            pltpu.VMEM((width, length), low),
            pltpu.VMEM((width, length), low),
            pltpu.VMEM((width, length), low),
            pltpu.VMEM((hidden_units, length), low),
            pltpu.VMEM((2, key_end - key_at, query_end - query_at), full),
            pltpu.VMEM((length, width), full),
            pltpu.VMEM((length, width), low),
            pltpu.VMEM((length, width), full),
            pltpu.SemaphoreType.DMA((len(given),)),
            pltpu.SemaphoreType.DMA((len(made),)),
            pltpu.SemaphoreType.DMA((2 * 5 * half,)),
        ],
        compiler_params=compiler_params(),
        cost_estimate=cost(28),
        name="forward_step",
    )(here, sizes, matching, *given)


def loss_kernel(
    place_ref,
    sizes_ref,
    sharpness_ref,
    numbers_ref,
    gathered_hbm,
    pooled_hbm,
    normed_hbm,
    inv_hbm,
    gain_hbm,
    loss_ref,
    grad_hidden_hbm,
    grad_branch_hbm,
    sums_ref,
    gathered_ref,
    pooled_ref,
    normed_ref,
    inv_ref,
    gain_ref,
    grad_hidden_ref,
    grad_branch_ref,
    sems,
):
    given = [
        (gathered_hbm, gathered_ref),
        (pooled_hbm, pooled_ref),
        (normed_hbm, normed_ref),
        (inv_hbm, inv_ref),
        (gain_hbm, gain_ref),
    ]
    copies = [
        pltpu.make_async_copy(source, target, sems.at[i])
        for i, (source, target) in enumerate(given)
    ]
    start_all(copies)
    segments, width = pooled_ref.shape
    half = segments // 2
    devices = gathered_ref.shape[0]
    total = devices * half
    sharpness = sharpness_ref[0]
    row = lax.broadcasted_iota(jnp.int32, (total, devices * segments), 0)
    column = lax.broadcasted_iota(jnp.int32, (total, devices * segments), 1)
    source = jnp.bitwise_xor(row // half, place_ref[0]) * segments + row % half
    copies[0].wait()
    gathered = gathered_ref[...].reshape(devices * segments, width + LANES)
    pick = jnp.where(column == source, 1.0, 0.0).astype(jnp.bfloat16)
    picked = dot_nn(pick, gathered)
    questions = picked[:, :width].astype(jnp.bfloat16)
    digits = picked[:, width:]
    pick = jnp.where(column == source + half, 1.0, 0.0).astype(jnp.bfloat16)
    passages = dot_nn(pick, gathered[:, :width]).astype(jnp.bfloat16)
    matching = (digits[:, 0:1] + 256.0 * digits[:, 1:2]).astype(jnp.int32)
    table = dot_nt(questions, passages) / sharpness
    top = jnp.max(table, axis=1, keepdims=True)
    expo = jnp.exp(table - top)
    expo_total = jnp.sum(expo, axis=1, keepdims=True)
    chosen = matching == numbers_ref[...]
    positive = jnp.sum(jnp.where(chosen, table, 0.0), axis=1, keepdims=True)
    loss_ref[...] = (
        jnp.sum(top + jnp.log(expo_total) - positive, axis=0, keepdims=True) / total
    )
    slope = (expo / expo_total - chosen.astype(jnp.float32)) / total
    grad_dot = (slope / sharpness).astype(jnp.bfloat16)
    segment_at = lax.broadcasted_iota(jnp.int32, (segments, total), 0)
    column = lax.broadcasted_iota(jnp.int32, (segments, total), 1)
    mine = column == place_ref[0] * half + segment_at // 2
    is_query = segment_at % 2 == 0
    pick_query = jnp.where(mine & is_query, 1.0, 0.0).astype(jnp.bfloat16)
    pick_passage = jnp.where(mine & ~is_query, 1.0, 0.0).astype(jnp.bfloat16)
    row_terms = dot_nn(pick_query, grad_dot).astype(jnp.bfloat16)
    column_terms = dot_nt(pick_passage, grad_dot).astype(jnp.bfloat16)
    grad_units = dot_nn(row_terms, passages) + dot_nn(column_terms, questions)
    wait_all(copies[1:])
    pooled = pooled_ref[...]
    inv_norm = lax.rsqrt(jnp.sum(pooled * pooled, axis=1, keepdims=True) + EPS_UNIT)
    units = pooled * inv_norm
    along = jnp.sum(units * grad_units, axis=1, keepdims=True)
    grad_pooled = inv_norm * (grad_units - units * along) / counts_as_column(sizes_ref, segments)
    upper = grad_pooled.astype(jnp.bfloat16)
    lower = (grad_pooled - upper.astype(jnp.float32)).astype(jnp.bfloat16)
    both = jnp.concatenate([upper, lower], axis=0)
    start, end = lengths_as_row(sizes_ref, 2 * segments, segments)
    gain = as_row(gain_ref)
    outward = []
    tokens = normed_ref.shape[0]
    chunk = min(tokens, 128)
    gain_sum = jnp.zeros((1, width), jnp.float32)
    shift_sum = jnp.zeros((1, width), jnp.float32)
    bias_sum = jnp.zeros((1, width), jnp.float32)
    for at in range(0, tokens, chunk):
        token = at + lax.broadcasted_iota(jnp.int32, (chunk, 2 * segments), 0)
        member = jnp.where((token >= start) & (token < end), 1.0, 0.0).astype(jnp.bfloat16)
        grad_out = dot_nn(member, both)
        normed = normed_ref[at : at + chunk]
        gain_sum = gain_sum + jnp.sum(grad_out * normed, axis=0, keepdims=True)
        shift_sum = shift_sum + jnp.sum(grad_out, axis=0, keepdims=True)
        grad_hidden = standardize_back(normed, inv_ref[at : at + chunk], grad_out * gain)
        grad_hidden_ref[at : at + chunk] = grad_hidden
        low = grad_hidden.astype(jnp.bfloat16)
        grad_branch_ref[at : at + chunk] = low
        bias_sum = bias_sum + jnp.sum(low.astype(jnp.float32), axis=0, keepdims=True)
        for source_ref, target in (
            (grad_hidden_ref, grad_hidden_hbm),
            (grad_branch_ref, grad_branch_hbm),
        ):
            copy = pltpu.make_async_copy(
                source_ref.at[at : at + chunk],
                target.at[at : at + chunk],
                sems.at[len(copies) + len(outward)],
            )
            copy.start()
            outward.append(copy)
    sums_ref[...] = jnp.concatenate([bias_sum, gain_sum, shift_sum], axis=0)
    wait_all(outward)


def loss_step(place, sizes, sharpness, numbers, gathered, pooled, normed, inv, gain):
    tokens, width = normed.shape
    low, full = jnp.bfloat16, jnp.float32
    chunks = -(-tokens // 128)
    return pl.pallas_call(
        loss_kernel,
        in_specs=[smem_spec()] * 3 + [vmem_spec()] + [any_spec()] * 5,
        out_specs=[vmem_spec(), any_spec(), any_spec(), vmem_spec()],
        out_shape=[
            jax.ShapeDtypeStruct((1, 1), full),
            jax.ShapeDtypeStruct((tokens, width), full),
            jax.ShapeDtypeStruct((tokens, width), low),
            jax.ShapeDtypeStruct((3, width), full),
        ],
        scratch_shapes=[
            pltpu.VMEM(gathered.shape, low),
            pltpu.VMEM(pooled.shape, full),
            pltpu.VMEM(normed.shape, full),
            pltpu.VMEM(inv.shape, full),
            pltpu.VMEM(gain.shape, low),
            pltpu.VMEM((tokens, width), full),
            pltpu.VMEM((tokens, width), low),
            pltpu.SemaphoreType.DMA((5 + 2 * chunks,)),
        ],
        compiler_params=compiler_params(),
        cost_estimate=cost(4),
        name="loss_step",
    )(place, sizes, sharpness, numbers, gathered, pooled, normed, inv, gain)


def before_kernel(branch_ref, slope_ref, narrowing_ref, grad_pre_ref, bias_ref):
    tokens = slope_ref.shape[0]
    chunk = min(tokens, 256)
    bias = jnp.zeros((1, slope_ref.shape[1]), jnp.float32)
    for at in range(0, tokens, chunk):
        grad_act = dot_nt(branch_ref[at : at + chunk], narrowing_ref[...])
        grad_pre = (grad_act * widen(slope_ref[at : at + chunk])).astype(jnp.bfloat16)
        grad_pre_ref[at : at + chunk] = grad_pre
        bias = bias + jnp.sum(widen(grad_pre), axis=0, keepdims=True)
    bias_ref[...] = bias


def before_step(branch, slope, narrowing):
    tokens, hidden_units = slope.shape
    width = branch.shape[1]
    tile = 4 * LANES
    return pl.pallas_call(
        before_kernel,
        grid=(hidden_units // tile,),
        in_specs=[
            pl.BlockSpec((tokens, width), lambda i: (0, 0)),
            pl.BlockSpec((tokens, tile), lambda i: (0, i)),
            pl.BlockSpec((tile, width), lambda i: (i, 0)),
        ],
        out_specs=[
            pl.BlockSpec((tokens, tile), lambda i: (0, i)),
            pl.BlockSpec((1, tile), lambda i: (0, i)),
        ],
        out_shape=[
            jax.ShapeDtypeStruct((tokens, hidden_units), jnp.bfloat16),
            jax.ShapeDtypeStruct((1, hidden_units), jnp.float32),
        ],
        compiler_params=compiler_params(),
        cost_estimate=cost(6),
        name="before_step",
    )(branch, slope, narrowing)


def side_copies(own_ref, other_ref, at, count, target, sems):
    tokens = own_ref.shape[2]
    return [
        pltpu.make_async_copy(
            source.at[:, pl.ds(at, count)],
            target.at[:, :, pl.ds(i * tokens, tokens)],
            sems.at[i],
        )
        for i, source in enumerate((own_ref, other_ref))
    ]


def flat(ref):
    places, rows, tokens = ref.shape
    return ref[...].reshape(places * rows, tokens)


def store_shares(product, parts, at, keep, send):
    rows = keep.shape[2]
    low = product.astype(jnp.bfloat16)
    for place in range(low.shape[0] // rows // parts):
        target = keep if place < keep.shape[0] else send
        for tile in range(low.shape[1] // LANES):
            for part in range(parts):
                row = (place * parts + part) * rows
                target[place % keep.shape[0], at + tile * parts + part] = low[
                    row : row + rows, tile * LANES : (tile + 1) * LANES
                ]


def outer_kernel(
    own_ref,
    other_ref,
    branch_own_ref,
    branch_other_ref,
    keep_x,
    send_x,
    keep_z,
    send_z,
    left_x,
    left_z,
    sems,
):
    count = left_x.shape[1]
    parts = count // keep_x.shape[2]
    copies_x = side_copies(own_ref, other_ref, 0, count, left_x, sems.at[0])
    copies_z = side_copies(own_ref, other_ref, count, count, left_z, sems.at[1])
    first = pl.program_id(0) == 0

    @pl.when(first)
    def _():
        start_all(copies_x + copies_z)
        wait_all(copies_x)

    right = jnp.concatenate([branch_own_ref[...], branch_other_ref[...]], axis=0)
    store_shares(dot_nn(flat(left_x), right), parts, 0, keep_x, send_x)

    @pl.when(first)
    def _():
        wait_all(copies_z)

    store_shares(dot_nn(flat(left_z), right), parts, 0, keep_z, send_z)


def outer_step(own, other, branch_own, branch_other, count):
    places, _, tokens = own.shape
    width = branch_own.shape[1]
    wide = 2 * LANES
    parts = 2
    rows = count // parts
    shape = jax.ShapeDtypeStruct(
        (places // 2, width // LANES * parts, rows, LANES), jnp.bfloat16
    )
    column = pl.BlockSpec((tokens, wide), lambda i: (0, i))
    return pl.pallas_call(
        outer_kernel,
        grid=(width // wide,),
        in_specs=[any_spec(), any_spec(), column, column],
        out_specs=[pl.BlockSpec((places // 2, 2 * parts, rows, LANES), lambda i: (0, i, 0, 0))]
        * 4,
        out_shape=[shape] * 4,
        scratch_shapes=[
            pltpu.VMEM((places, count, 2 * tokens), jnp.bfloat16),
            pltpu.VMEM((places, count, 2 * tokens), jnp.bfloat16),
            pltpu.SemaphoreType.DMA((2, 2)),
        ],
        compiler_params=compiler_params(),
        cost_estimate=cost(6),
        name="outer_step",
    )(own, other, branch_own, branch_other)


def inner_kernel(
    at,
    side_ref,
    own_ref,
    other_ref,
    grad_own_ref,
    grad_other_ref,
    widening_ref,
    hidden_hbm,
    normed_hbm,
    inv_hbm,
    gain_hbm,
    mixing_hbm,
    keep_ref,
    send_ref,
    grad_hidden_ref,
    grad_branch_ref,
    grad_attn_ref,
    sums_ref,
    left,
    total,
    normed_ref,
    inv_ref,
    gain_ref,
    mixing_ref,
    side_sems,
    sems,
):
    step = pl.program_id(0)
    steps = pl.num_programs(0)
    first = step == 0
    left_copies = side_copies(own_ref, other_ref, at, left.shape[1], left, side_sems)
    given = [
        (hidden_hbm, total),
        (normed_hbm, normed_ref),
        (inv_hbm, inv_ref),
        (gain_hbm, gain_ref),
        (mixing_hbm, mixing_ref),
    ]
    copies = [
        pltpu.make_async_copy(source, target, sems.at[i])
        for i, (source, target) in enumerate(given)
    ]

    @pl.when(first)
    def _():
        start_all(left_copies + copies)
        wait_all(left_copies)
        copies[0].wait()

    tokens = grad_own_ref.shape[0]
    product = dot_nn(flat(left)[:, :tokens], grad_own_ref[...]) + dot_nn(
        flat(left)[:, tokens:], grad_other_ref[...]
    )

    @pl.when(step < steps // 2)
    def _():
        store_shares(product, 1, 0, keep_ref, keep_ref)

    @pl.when(step >= steps // 2)
    def _():
        store_shares(product, 1, 0, send_ref, send_ref)

    total[...] += dot_nt(grad_own_ref[...], widening_ref[...])

    @pl.when(step == steps - 1)
    def _():
        wait_all(copies[1:])
        width = normed_ref.shape[1]
        chunk = min(tokens, 128)
        gain = as_row(gain_ref)
        gain_sum = jnp.zeros((1, width), jnp.float32)
        shift_sum = jnp.zeros((1, width), jnp.float32)
        bias_sum = jnp.zeros((1, width), jnp.float32)
        for row in range(0, tokens, chunk):
            grad_out = total[row : row + chunk]
            normed = normed_ref[row : row + chunk]
            gain_sum = gain_sum + jnp.sum(grad_out * normed, axis=0, keepdims=True)
            shift_sum = shift_sum + jnp.sum(grad_out, axis=0, keepdims=True)
            grad_hidden = standardize_back(normed, inv_ref[row : row + chunk], grad_out * gain)
            grad_hidden_ref[row : row + chunk] = grad_hidden
            low = grad_hidden.astype(jnp.bfloat16)
            grad_branch_ref[row : row + chunk] = low
            bias_sum = bias_sum + jnp.sum(widen(low), axis=0, keepdims=True)
            grad_attn_ref[row : row + chunk] = dot_nt(low, mixing_ref[...]).astype(jnp.bfloat16)
        sums_ref[...] = jnp.concatenate([bias_sum, gain_sum, shift_sum], axis=0)


def inner_step(
    side, own, other, at, rows, grad_own, grad_other, widening, hidden, normed, inv, gain, mixing
):
    places, _, tokens = own.shape
    width = normed.shape[1]
    hidden_units = grad_own.shape[1]
    tile = 4 * LANES
    steps = hidden_units // tile
    low, full = jnp.bfloat16, jnp.float32
    shape = jax.ShapeDtypeStruct((places, hidden_units // LANES // 2, rows, LANES), low)
    block = (places, tile // LANES, rows, LANES)

    def tile_of(i, side):
        return (i + side[0] * (steps // 2)) % steps

    def whole(kind):
        return pl.BlockSpec((tokens, width), lambda i, side: (0, 0))

    return pl.pallas_call(
        functools.partial(inner_kernel, at),
        grid_spec=pltpu.PrefetchScalarGridSpec(
            num_scalar_prefetch=1,
            grid=(steps,),
            in_specs=[
                any_spec(),
                any_spec(),
                pl.BlockSpec((tokens, tile), lambda i, side: (0, tile_of(i, side))),
                pl.BlockSpec((tokens, tile), lambda i, side: (0, tile_of(i, side))),
                pl.BlockSpec((width, tile), lambda i, side: (0, tile_of(i, side))),
                any_spec(),
                any_spec(),
                any_spec(),
                any_spec(),
                any_spec(),
            ],
            out_specs=[
                pl.BlockSpec(block, lambda i, side: (0, jnp.minimum(i, steps // 2 - 1), 0, 0)),
                pl.BlockSpec(block, lambda i, side: (0, jnp.maximum(i - steps // 2, 0), 0, 0)),
                whole(full),
                whole(low),
                whole(low),
                pl.BlockSpec((3, width), lambda i, side: (0, 0)),
            ],
            scratch_shapes=[
                pltpu.VMEM((places, rows, 2 * tokens), low),
                pltpu.VMEM((tokens, width), full),
                pltpu.VMEM(normed.shape, full),
                pltpu.VMEM(inv.shape, full),
                pltpu.VMEM(gain.shape, low),
                pltpu.VMEM(mixing.shape, low),
                pltpu.SemaphoreType.DMA((2,)),
                pltpu.SemaphoreType.DMA((5,)),
            ],
        ),
        out_shape=[
            shape,
            shape,
            jax.ShapeDtypeStruct((tokens, width), full),
            jax.ShapeDtypeStruct((tokens, width), low),
            jax.ShapeDtypeStruct((tokens, width), low),
            jax.ShapeDtypeStruct((3, width), full),
        ],
        compiler_params=compiler_params(),
        cost_estimate=cost(12),
        name="inner_step",
    )(side, own, other, grad_own, grad_other, widening, hidden, normed, inv, gain, mixing)


def attend_back_kernel(
    segments,
    sizes_ref,
    query_ref,
    key_ref,
    key_t_ref,
    value_ref,
    lse_ref,
    grad_ref,
    grads_ref,
    sums_ref,
    fill,
    query_t,
    total_key,
    total_value,
):
    length, wide = query_ref.shape
    ranges = band(length)
    step = pl.program_id(0)

    @pl.when(step == 0)
    def _():
        for i, (query_at, query_end, key_at, key_end) in enumerate(ranges):
            fill[i] = mask_of(sizes_ref, segments, query_at, query_end, key_at, key_end)

    total_key[...] = jnp.zeros_like(total_key)
    total_value[...] = jnp.zeros_like(total_value)
    lane = lax.broadcasted_iota(jnp.int32, (1, LANES), 1)
    for pair in range(wide // LANES):
        lanes = slice(pair * LANES, (pair + 1) * LANES)
        for i, (query_at, query_end, key_at, key_end) in enumerate(ranges):
            keys = key_ref[key_at:key_end, lanes]
            values = value_ref[key_at:key_end, lanes]
            grad_key = None
            grad_value = None
            for which in range(LANES // HD):
                head = (lane // HD) == which
                query = jnp.where(head, query_ref[query_at:query_end, lanes], 0)
                grad = jnp.where(head, grad_ref[query_at:query_end, lanes], 0)
                at = pair * (LANES // HD) + which
                scores = dot_nt(keys, query) + fill[i]
                probs = jnp.exp(scores - lse_ref[0, at : at + 1, query_at:query_end])
                grad_probs = dot_nt(values, grad)
                inner = jnp.sum(grad_probs * probs, axis=0, keepdims=True)
                grad_scores = (probs * (grad_probs - inner)).astype(jnp.bfloat16)
                value_term = dot_nn(probs.astype(jnp.bfloat16), grad)
                key_term = dot_nn(grad_scores, query)
                query_t[at * HD : (at + 1) * HD, query_at:query_end] = dot_nn(
                    key_t_ref[at * HD : (at + 1) * HD, key_at:key_end], grad_scores
                )
                grad_key = key_term if grad_key is None else grad_key + key_term
                grad_value = value_term if grad_value is None else grad_value + value_term
            total_key[key_at:key_end, lanes] += grad_key
            total_value[key_at:key_end, lanes] += grad_value
    grad_query = (query_t[...] * HD ** (-0.5)).T.astype(jnp.bfloat16)
    grad_value = total_value[...].astype(jnp.bfloat16)
    grads_ref[0] = grad_query
    grads_ref[1] = total_key[...].astype(jnp.bfloat16)
    grads_ref[2] = grad_value
    sums_ref[...] = jnp.concatenate(
        [
            jnp.sum(widen(grad_query), axis=0, keepdims=True),
            jnp.sum(widen(grad_value), axis=0, keepdims=True),
        ],
        axis=0,
    )


def attend_back_step(sizes, query, key, key_t, value, lse, grad):
    tokens, width = query.shape
    heads_here = lse.shape[1]
    wide = heads_here * HD
    columns = pl.BlockSpec((tokens, wide), lambda i: (0, i))
    query_at, query_end, key_at, key_end = band(tokens)[0]
    return pl.pallas_call(
        functools.partial(attend_back_kernel, sizes.shape[1]),
        grid=(width // wide,),
        in_specs=[
            smem_spec(),
            columns,
            columns,
            pl.BlockSpec((wide, tokens), lambda i: (i, 0)),
            columns,
            pl.BlockSpec((1, heads_here, tokens), lambda i: (i, 0, 0)),
            columns,
        ],
        out_specs=[
            pl.BlockSpec((3, tokens, wide), lambda i: (0, 0, i)),
            pl.BlockSpec((2, wide), lambda i: (0, i)),
        ],
        out_shape=[
            jax.ShapeDtypeStruct((3, tokens, width), jnp.bfloat16),
            jax.ShapeDtypeStruct((2, width), jnp.float32),
        ],
        scratch_shapes=[
            pltpu.VMEM((2, key_end - key_at, query_end - query_at), jnp.float32),
            pltpu.VMEM((wide, tokens), jnp.float32),
            pltpu.VMEM((tokens, wide), jnp.float32),
            pltpu.VMEM((tokens, wide), jnp.float32),
        ],
        compiler_params=compiler_params(),
        cost_estimate=cost(12),
        name="attend_back_step",
    )(sizes, query, key, key_t, value, lse, grad)


def token_kernel(hidden_ref, grads_ref, question_ref, lookup_ref, content_ref, out_ref):
    out_ref[...] = (
        hidden_ref[...]
        + dot_nt(grads_ref[0], question_ref[...])
        + dot_nt(grads_ref[1], lookup_ref[...])
        + dot_nt(grads_ref[2], content_ref[...])
    )


def token_step(hidden, grads, question, lookup, content):
    tokens, width = hidden.shape
    wide = 2 * LANES
    weight = pl.BlockSpec((wide, width), lambda i: (i, 0))
    column = pl.BlockSpec((tokens, wide), lambda i: (0, i))
    return pl.pallas_call(
        token_kernel,
        grid=(width // wide,),
        in_specs=[column, pl.BlockSpec((3, tokens, width), lambda i: (0, 0, 0))] + [weight] * 3,
        out_specs=column,
        out_shape=jax.ShapeDtypeStruct((tokens, width), jnp.float32),
        compiler_params=compiler_params(),
        cost_estimate=cost(5),
        name="token_step",
    )(hidden, grads, question, lookup, content)


def attention_kernel(
    token_at,
    attn_at,
    side_ref,
    own_ref,
    other_ref,
    grads_own_ref,
    grads_other_ref,
    branch_own_ref,
    branch_other_ref,
    keep_x,
    send_x,
    keep_y,
    send_y,
    token_left,
    attn_left,
    sems,
):
    first = pl.program_id(0) == 0
    rows = token_left.shape[1]
    copies = side_copies(own_ref, other_ref, token_at, rows, token_left, sems.at[0])
    copies = copies + side_copies(own_ref, other_ref, attn_at, rows, attn_left, sems.at[1])

    @pl.when(first)
    def _():
        start_all(copies)
        wait_all(copies)

    side = side_ref[0]

    def both(index):
        return jnp.concatenate([grads_own_ref[index], grads_other_ref[index]], axis=0)

    token = flat(token_left)
    store_shares(dot_nn(token, both(0)), 1, 0, keep_x.at[:, 0], send_x.at[:, 0])
    branch = jnp.concatenate([branch_own_ref[...], branch_other_ref[...]], axis=0)
    store_shares(dot_nn(flat(attn_left), branch), 1, 0, keep_x.at[:, 1], send_x.at[:, 1])
    store_shares(dot_nn(token, both(1 + side)), 1, 0, keep_y, keep_y)
    store_shares(dot_nn(token, both(2 - side)), 1, 0, send_y, send_y)


def attention_step(
    side, own, other, token_at, attn_at, rows, grads_own, grads_other, branch_own, branch_other
):
    places, _, tokens = own.shape
    width = branch_own.shape[1]
    wide = 2 * LANES
    tiles = width // LANES
    low = jnp.bfloat16
    shape_x = jax.ShapeDtypeStruct((places // 2, 2, tiles, rows, LANES), low)
    shape_y = jax.ShapeDtypeStruct((places, tiles, rows, LANES), low)
    block_x = pl.BlockSpec((places // 2, 2, 2, rows, LANES), lambda i: (0, 0, i, 0, 0))
    block_y = pl.BlockSpec((places, 2, rows, LANES), lambda i: (0, i, 0, 0))
    grads = pl.BlockSpec((3, tokens, wide), lambda i: (0, 0, i))
    column = pl.BlockSpec((tokens, wide), lambda i: (0, i))
    return pl.pallas_call(
        functools.partial(attention_kernel, token_at, attn_at),
        grid=(width // wide,),
        in_specs=[smem_spec(), any_spec(), any_spec(), grads, grads, column, column],
        out_specs=[block_x, block_x, block_y, block_y],
        out_shape=[shape_x, shape_x, shape_y, shape_y],
        scratch_shapes=[
            pltpu.VMEM((places, rows, 2 * tokens), low),
            pltpu.VMEM((places, rows, 2 * tokens), low),
            pltpu.SemaphoreType.DMA((2, 2)),
        ],
        compiler_params=compiler_params(),
        cost_estimate=cost(5),
        name="attention_step",
    )(side, own, other, grads_own, grads_other, branch_own, branch_other)


def body(
    hidden_states_in,
    piece_sizes,
    matching_passage_number,
    softmax_sharpness,
    question_projection,
    question_offset,
    lookup_projection,
    content_projection,
    content_offset,
    mixing_result_projection,
    mixing_result_offset,
    mixing_layernorm_scale,
    mixing_layernorm_offset,
    widening_projection,
    widening_offset,
    narrowing_projection,
    narrowing_offset,
    perceptron_layernorm_scale,
    perceptron_layernorm_offset,
):
    rows_here, length, width = hidden_states_in.shape
    segments = piece_sizes.shape[1]
    per_device = segments // 2
    groups_y = lax.axis_size("gy")
    tiles = width // LANES
    rows = width // groups_y
    inner_rows = widening_offset.shape[0] // groups_y
    gy_bits = powers_below(groups_y)
    order_x = gy_bits[1:]
    order_z = gy_bits[2:] + gy_bits[1:2]
    here = lax.axis_index("gy").astype(jnp.int32).reshape(1)
    side = (lax.axis_index("gx").astype(jnp.int32) & 1).reshape(1)
    (
        queries,
        keys,
        keys_t,
        values,
        lse,
        normed_one,
        inv_one,
        slope,
        normed_two,
        inv_two,
        pooled,
        message,
        side_own,
        side_send,
    ) = forward_step(
        here,
        piece_sizes,
        matching_passage_number,
        place_masks(order_x),
        place_masks(order_z),
        [
            hidden_states_in[0],
            question_projection,
            lookup_projection,
            content_projection,
            mixing_result_projection,
            widening_projection,
            narrowing_projection,
            question_offset,
            content_offset,
            mixing_result_offset,
            mixing_layernorm_scale,
            mixing_layernorm_offset,
            widening_offset,
            narrowing_offset,
            perceptron_layernorm_scale,
            perceptron_layernorm_offset,
        ],
    )
    gathered, numbers_of, place, side_other = gather_blocks(
        message, swap_with(side_send, "gy", 1)
    )
    numbers = (numbers_of[:, None] * per_device + np.arange(per_device)[None, :]).reshape(1, -1)
    loss_out, grad_hidden_two, branch_two, sums_two = loss_step(
        place.astype(jnp.int32).reshape(1),
        piece_sizes,
        softmax_sharpness,
        jnp.asarray(numbers, jnp.int32),
        gathered,
        pooled,
        normed_two,
        inv_two,
        perceptron_layernorm_scale,
    )
    branch_two_other = swap_with(branch_two, "gy", 1)
    grad_pre, grad_b_inner = before_step(branch_two, slope, narrowing_projection)
    branch_two_other, grad_pre = tie(branch_two_other, grad_pre)
    grad_pre_other = swap_with(grad_pre, "gy", 1)
    outer_keep_x, outer_send_x, outer_keep_z, outer_send_z = outer_step(
        side_own, side_other, branch_two, branch_two_other, inner_rows // 2
    )
    grad_pre_other, outer_send_x, outer_send_z = tie(grad_pre_other, outer_send_x, outer_send_z)
    outer_got_x = swap_with(outer_send_x, "gy", order_x[0])
    outer_got_z = swap_with(outer_send_z, "gy", order_z[0])
    inner_keep, inner_send, grad_hidden_one, branch_one, grad_attn, sums_one = inner_step(
        side,
        side_own,
        side_other,
        inner_rows,
        rows,
        grad_pre,
        grad_pre_other,
        widening_projection,
        grad_hidden_two,
        normed_one,
        inv_one,
        mixing_layernorm_scale,
        mixing_result_projection,
    )
    gx_bits = powers_below(lax.axis_size("gx"))
    outer_got_x, outer_got_z, branch_one, inner_send = tie(
        outer_got_x, outer_got_z, branch_one, inner_send
    )
    outer_keep_x, outer_send_x = add_halves(outer_keep_x, outer_got_x)
    outer_keep_z, outer_send_z = add_halves(outer_keep_z, outer_got_z)
    inner_got = swap_with(inner_send, "gx", 1)
    outer_got_x = swap_with(outer_send_x, "gy", order_x[1])
    outer_got_z = swap_with(outer_send_z, "gy", order_z[1])
    branch_one_other = swap_with(branch_one, "gy", 1)
    heads_at_once = 4
    grads, sums_attn = attend_back_step(
        piece_sizes,
        queries,
        keys,
        keys_t,
        values,
        lse.reshape(HEADS // heads_at_once, heads_at_once, length),
        grad_attn,
    )
    branch_one_other, grads = tie(branch_one_other, grads)
    grads_other = swap_with(grads, "gy", 1)
    grad_tokens = token_step(
        grad_hidden_one, grads, question_projection, lookup_projection, content_projection
    )
    grads_other, grad_tokens = tie(grads_other, grad_tokens)
    attn_keep_x, attn_send_x, attn_keep_y, attn_send_y = attention_step(
        side,
        side_own,
        side_other,
        inner_rows + rows,
        inner_rows + 2 * rows,
        rows,
        grads,
        grads_other,
        branch_one,
        branch_one_other,
    )
    outer_got_x, outer_got_z, attn_send_x, attn_send_y, sums_attn = tie(
        outer_got_x, outer_got_z, attn_send_x, attn_send_y, sums_attn
    )
    attn_got_x = swap_with(attn_send_x, "gy", order_x[0])
    attn_got_y = swap_with(attn_send_y, "gx", 1)
    vectors = jnp.concatenate([sums_attn, sums_one, sums_two], axis=0)
    vectors = vectors.reshape(8, groups_y, rows).transpose(1, 0, 2).reshape(groups_y, 8 * rows)
    vectors = jnp.concatenate([vectors, grad_b_inner.reshape(groups_y, -1)], axis=1)
    for bit in reversed(gy_bits):
        vectors = halve_row(vectors, bit)
    for bit in gx_bits:
        vectors = vectors + swap_with(vectors, "gx", bit)
    vector_sums = vectors[0]
    b_query, b_value, b_output, gain_attn, shift_attn, b_outer, gain_ffn, shift_ffn = [
        vector_sums[i * rows : (i + 1) * rows] for i in range(8)
    ]
    outer_x = finish_shares(outer_keep_x, outer_got_x, order_x[2:])
    outer_z = finish_shares(outer_keep_z, outer_got_z, order_z[2:])
    outer_both = sum_over_gx(jnp.concatenate([outer_x, outer_z], axis=0), gx_bits)
    outer_x, outer_z = jnp.split(outer_both, 2, axis=0)
    attn_x = finish_shares(attn_keep_x, attn_got_x, order_x[1:])
    attn_x = sum_over_gx(attn_x, gx_bits)
    keep = jnp.concatenate([inner_keep, attn_keep_y], axis=1)
    got = jnp.concatenate([inner_got, attn_got_y], axis=1)
    both_y = finish_shares(keep, got, order_x)
    both_y = sum_over_gx(both_y, gx_bits[1:])
    split_at = inner_keep.shape[1]
    both_y = gather_over_gx(both_y).reshape((2,) + both_y.shape)
    inner_sums = both_y[:, :split_at].reshape((-1,) + both_y.shape[2:])
    attn_y = both_y[:, split_at:].reshape((-1,) + both_y.shape[2:])
    grad_w_outer = jnp.concatenate([share_of(outer_x, width), share_of(outer_z, width)], axis=0)
    return (
        loss_out.reshape(1),
        pooled[None],
        grad_tokens.reshape(rows_here, length, width),
        share_of(attn_x[0], width),
        b_query,
        share_of(attn_y[:tiles], width),
        share_of(attn_y[tiles:], width),
        b_value,
        share_of(attn_x[1], width),
        b_output,
        gain_attn,
        shift_attn,
        share_of(inner_sums, widening_offset.shape[0]),
        vector_sums[8 * rows :],
        grad_w_outer,
        b_outer,
        gain_ffn,
        shift_ffn,
    )


def solution(mesh):
    return jax.shard_map(
        body,
        mesh=mesh,
        in_specs=(
            P(("gx", "gy"), None, None),
            P(("gx", "gy"), None),
            P(("gx", "gy")),
            P(),
            P(),
            P(),
            P(),
            P(),
            P(),
            P(),
            P(),
            P(),
            P(),
            P(),
            P(),
            P(),
            P(),
            P(),
            P(),
        ),
        out_specs=(
            P(),
            P(("gx", "gy"), None, None),
            P(("gx", "gy"), None, None),
            P("gy", None),
            P("gy"),
            P("gy", None),
            P("gy", None),
            P("gy"),
            P("gy", None),
            P("gy"),
            P("gy"),
            P("gy"),
            P("gy", None),
            P("gy"),
            P("gy", None),
            P("gy"),
            P("gy"),
            P("gy"),
        ),
        check_vma=False,
    )
```

```python
import functools

import jax
import jax.numpy as jnp
import numpy as np
from jax import lax
from jax.experimental import pallas as pl
from jax.experimental.pallas import tpu as pltpu
from jax.sharding import PartitionSpec as P

HEADS = 12
HD = 64
LANES = 128
VMEM_BYTES = 60 * 1024 * 1024

EPS_NORM = 1e-12
EPS_UNIT = 1e-06
NEG_FILL = -1e30


def standardize(hidden):
    center = hidden - jnp.mean(hidden, axis=-1, keepdims=True)
    inv_scale = lax.rsqrt(jnp.mean(center * center, axis=-1, keepdims=True) + EPS_NORM)
    return (center * inv_scale, inv_scale)


def standardize_back(normed, inv_scale, grad_normed):
    mean_grad = jnp.mean(grad_normed, axis=-1, keepdims=True)
    mean_both = jnp.mean(grad_normed * normed, axis=-1, keepdims=True)
    return inv_scale * (grad_normed - mean_grad - normed * mean_both)


def widen(value):
    return value.astype(jnp.float32)


def powers_below(count):
    bits = []
    bit = 1
    while bit < count:
        bits.append(bit)
        bit *= 2
    return bits


def place_masks(bits):
    masks = [0]
    for bit in reversed(bits):
        masks = masks + [mask ^ bit for mask in masks]
    return masks


def swap_with(value, axis, bit):
    count = lax.axis_size(axis)
    return lax.ppermute(value, axis, [(i, i ^ bit) for i in range(count)])


def tie(*values):
    return lax.optimization_barrier(values)


def gather_steps():
    gy = powers_below(lax.axis_size("gy"))
    far = [("gy", bit) for bit in reversed(gy[2:])]
    near = [("gy", bit) for bit in reversed(gy[:2])]
    return far + [("gx", bit) for bit in powers_below(lax.axis_size("gx"))] + near


def gather_blocks(block, beside):
    groups_y = lax.axis_size("gy")
    gathered = block[None]
    number = np.zeros((1,), np.int32)
    place = 0
    for step, (axis, bit) in enumerate(gather_steps()):
        if step == 3:
            gathered, beside = tie(gathered, beside)
        gathered = jnp.concatenate([gathered, swap_with(gathered, axis, bit)], axis=0)
        high = (lax.axis_index(axis) & bit) != 0
        number = np.concatenate([number, number + bit * (groups_y if axis == "gx" else 1)])
        place = place + jnp.where(high, 1 << step, 0)
    return gathered, number, place, beside


def share_of(blocks, columns):
    tiles = columns // LANES
    count, rows, _ = blocks.shape
    parts = count // tiles
    view = blocks.reshape(tiles, parts, rows, LANES)
    return view.transpose(1, 2, 0, 3).reshape(parts * rows, columns)


def compiler_params():
    return pltpu.CompilerParams(vmem_limit_bytes=VMEM_BYTES)


def dot_nt(left, right):
    return lax.dot_general(
        left, right, (((1,), (1,)), ((), ())), preferred_element_type=jnp.float32
    )


def dot_nn(left, right):
    return jnp.dot(left, right, preferred_element_type=jnp.float32)


def start_all(copies):
    for copy in copies:
        copy.start()


def wait_all(copies):
    for copy in copies:
        copy.wait()


def as_row(ref):
    return ref[...].astype(jnp.float32).reshape(1, ref.shape[0])


def lengths_as_row(sizes_ref, lanes, segments):
    lane = lax.broadcasted_iota(jnp.int32, (1, lanes), 1) % segments
    start = jnp.zeros((1, lanes), jnp.int32)
    end = jnp.zeros((1, lanes), jnp.int32)
    at = jnp.int32(0)
    for segment in range(segments):
        size = sizes_ref[0, segment]
        start = jnp.where(lane == segment, at, start)
        at = at + size
        end = jnp.where(lane == segment, at, end)
    return start, end


def counts_as_column(sizes_ref, segments):
    row = lax.broadcasted_iota(jnp.int32, (segments, 1), 0)
    counts = jnp.zeros((segments, 1), jnp.float32)
    for segment in range(segments):
        counts = jnp.where(row == segment, sizes_ref[0, segment].astype(jnp.float32), counts)
    return counts


def starts_as_column(sizes_ref, segments):
    row = lax.broadcasted_iota(jnp.int32, (segments, 1), 0)
    start = jnp.zeros((segments, 1), jnp.int32)
    end = jnp.zeros((segments, 1), jnp.int32)
    at = jnp.int32(0)
    for segment in range(segments):
        size = sizes_ref[0, segment]
        start = jnp.where(row == segment, at, start)
        at = at + size
        end = jnp.where(row == segment, at, end)
    return start, end


def band(length):
    return [(0, length // 2, 0, 3 * length // 4), (length // 2, length, length // 4, length)]


def mask_of(sizes_ref, segments, query_at, query_end, key_at, key_end):
    query = query_at + lax.broadcasted_iota(jnp.int32, (1, query_end - query_at), 1)
    low = jnp.zeros_like(query)
    high = jnp.zeros_like(query)
    at = jnp.int32(0)
    for segment in range(segments):
        end = at + sizes_ref[0, segment]
        inside = (query >= at) & (query < end)
        low = jnp.where(inside, at, low)
        high = jnp.where(inside, end, high)
        at = end
    padding = query >= at
    low = jnp.where(padding, at, low)
    high = jnp.where(padding, key_end, high)
    key = key_at + lax.broadcasted_iota(jnp.int32, (key_end - key_at, query_end - query_at), 0)
    return jnp.where((key >= low) & (key < high), 0.0, NEG_FILL)


def got_spec():
    return pl.BlockSpec(memory_space=pl.ANY)


def vmem_spec():
    return pl.BlockSpec(memory_space=pltpu.VMEM)


def smem_spec():
    return pl.BlockSpec(memory_space=pltpu.SMEM)


def any_spec():
    return pl.BlockSpec(memory_space=pltpu.HBM)


def cost(microseconds):
    return pl.CostEstimate(
        flops=int(microseconds * 1.1e9), bytes_accessed=1000000, transcendentals=0
    )


def forward_kernel(segments, masks_x, masks_z, here_ref, sizes_ref, matching_ref, *refs):
    given, refs = refs[:16], refs[16:]
    results, refs = refs[:14], refs[14:]
    side_own, side_send = results[-2:]
    local, refs = refs[:16], refs[16:]
    made, refs = refs[:12], refs[12:]
    (
        tokens_ref,
        question_w,
        lookup_w,
        content_w,
        mixing_w,
        widening_w,
        narrowing_w,
        question_row,
        content_row,
        mixing_row,
        gain_one_row,
        shift_one_row,
        widening_row,
        narrowing_row,
        gain_two_row,
        shift_two_row,
    ) = local
    (
        query_ref,
        key_ref,
        key_t_ref,
        value_ref,
        lse_ref,
        normed_one_ref,
        inv_one_ref,
        slope_ref,
        normed_two_ref,
        inv_two_ref,
        pooled_ref,
        message_ref,
    ) = made
    value_t, token_t, attn_t, out_one_t, inner_t, fill = refs[:6]
    out_one, out_one_low, total, in_sems, out_sems, side_sems = refs[6:]
    length, width = tokens_ref.shape
    hidden_units = widening_w.shape[1]
    here = here_ref[0]
    share_rows = side_own.shape[1] // (hidden_units // width + 3)
    inner_rows = hidden_units // width * share_rows
    first_rows = inner_rows // 2
    copies = [
        pltpu.make_async_copy(source, target, in_sems.at[i])
        for i, (source, target) in enumerate(zip(given, local))
    ]
    outward = [
        pltpu.make_async_copy(source, target, out_sems.at[i])
        for i, (source, target) in enumerate(zip(made, results))
    ]
    side_copies = []

    def send_side(source, source_rows, offset, count, at, masks):
        for place, mask in enumerate(masks):
            for flip, target in enumerate((side_own, side_send)):
                share = jnp.bitwise_xor(here, mask ^ flip)
                first = pl.multiple_of(share * source_rows + offset, 8)
                copy = pltpu.make_async_copy(
                    source.at[pl.ds(first, count)],
                    target.at[place, pl.ds(at, count)],
                    side_sems.at[len(side_copies)],
                )
                copy.start()
                side_copies.append(copy)

    start_all(copies[:2] + copies[7:] + copies[2:4])
    ranges = band(length)
    for i, (query_at, query_end, key_at, key_end) in enumerate(ranges):
        fill[i] = mask_of(sizes_ref, segments, query_at, query_end, key_at, key_end)
    wait_all(copies[:2] + copies[7:])
    start_all(copies[4:7])
    product = dot_nn(tokens_ref[...], question_w[...]) + as_row(question_row)
    query_ref[...] = product.astype(jnp.bfloat16) * jnp.bfloat16(HD ** (-0.5))
    token_t[...] = tokens_ref[...].T
    copies[2].wait()
    product = dot_nn(tokens_ref[...], lookup_w[...]).astype(jnp.bfloat16)
    key_ref[...] = product
    key_t_ref[...] = product.T
    copies[3].wait()
    product = (dot_nn(tokens_ref[...], content_w[...]) + as_row(content_row)).astype(jnp.bfloat16)
    value_ref[...] = product
    value_t[...] = product.T
    start_all(outward[:4])
    send_side(token_t, share_rows, 0, share_rows, inner_rows + share_rows, masks_x)
    lane = lax.broadcasted_iota(jnp.int32, (1, LANES), 1)
    units = [(at, i) for at in range(HEADS) for i in range(len(ranges))]

    def scores_of(unit):
        at, i = unit
        query_at, query_end, key_at, key_end = ranges[i]
        first = at * HD // LANES * LANES
        lanes = slice(first, first + LANES)
        which = (at * HD - first) // HD
        query = jnp.where((lane // HD) == which, query_ref[query_at:query_end, lanes], 0)
        return dot_nt(key_ref[key_at:key_end, lanes], query) + fill[i]

    def attend(unit, scores):
        at, i = unit
        query_at, query_end, key_at, key_end = ranges[i]
        top = jnp.max(scores, axis=0, keepdims=True)
        expo = jnp.exp(scores - top)
        norm = jnp.sum(expo, axis=0, keepdims=True)
        probs = (expo * (1.0 / norm)).astype(jnp.bfloat16)
        lse_ref[at // 4, at % 4 : at % 4 + 1, query_at:query_end] = top + jnp.log(norm)
        mixed = dot_nn(value_t[at * HD : (at + 1) * HD, key_at:key_end], probs)
        attn_t[at * HD : (at + 1) * HD, query_at:query_end] = mixed.astype(jnp.bfloat16)

    ahead = 4
    waiting = [scores_of(unit) for unit in units[:ahead]]
    for n, unit in enumerate(units):
        if n + ahead < len(units):
            waiting.append(scores_of(units[n + ahead]))
        attend(unit, waiting.pop(0))
    outward[4].start()
    send_side(attn_t, share_rows, 0, share_rows, inner_rows + 2 * share_rows, masks_x)
    copies[4].wait()
    chunk = min(length, 128)
    for at in range(0, length, chunk):
        rows = slice(at, at + chunk)
        hidden = (
            tokens_ref[rows].astype(jnp.float32)
            + dot_nn(attn_t[:, rows].T, mixing_w[...])
            + as_row(mixing_row)
        )
        normed, inv = standardize(hidden)
        normed_one_ref[rows] = normed
        inv_one_ref[rows] = inv
        shifted = normed * as_row(gain_one_row) + as_row(shift_one_row)
        out_one[rows] = shifted
        low = shifted.astype(jnp.bfloat16)
        out_one_low[rows] = low
        out_one_t[:, rows] = low.T
        total[rows] = shifted + as_row(narrowing_row)
    start_all(outward[5:7])
    send_side(out_one_t, share_rows, 0, share_rows, inner_rows, masks_x)
    copies[5].wait()
    copies[6].wait()
    tile = hidden_units // 4
    taller = min(length, 256)
    units = [(at, row) for at in range(0, hidden_units, tile) for row in range(0, length, taller)]

    def widened(unit):
        at, row = unit
        return dot_nn(out_one_low[row : row + taller], widening_w[:, at : at + tile])

    def activate(unit, before):
        at, row = unit
        rows = slice(row, row + taller)
        before = before + widening_row[at : at + tile].astype(jnp.float32).reshape(1, tile)
        cdf = 0.5 * (1.0 + lax.erf(before * 0.7071067811865476))
        pdf = jnp.exp(-0.5 * before * before) * 0.3989422804014327
        inner = (before * cdf).astype(jnp.bfloat16)
        slope_ref[rows, at : at + tile] = (cdf + before * pdf).astype(jnp.bfloat16)
        inner_t[at : at + tile, rows] = inner.T
        total[rows] += dot_nn(inner, narrowing_w[at : at + tile, :])

    ahead = 1
    waiting = [widened(unit) for unit in units[:ahead]]
    for n, unit in enumerate(units):
        if n + ahead < len(units):
            waiting.append(widened(units[n + ahead]))
        activate(unit, waiting.pop(0))
    outward[7].start()
    send_side(inner_t, inner_rows, 0, first_rows, 0, masks_x)
    send_side(inner_t, inner_rows, first_rows, inner_rows - first_rows, first_rows, masks_z)
    start, end = starts_as_column(sizes_ref, segments)
    sums = jnp.zeros((segments, width), jnp.float32)
    for at in range(0, length, chunk):
        rows = slice(at, at + chunk)
        normed, inv = standardize(total[rows])
        normed_two_ref[rows] = normed
        inv_two_ref[rows] = inv
        out_two = normed * as_row(gain_two_row) + as_row(shift_two_row)
        upper = out_two.astype(jnp.bfloat16)
        lower = (out_two - upper.astype(jnp.float32)).astype(jnp.bfloat16)
        token = at + lax.broadcasted_iota(jnp.int32, (segments, chunk), 1)
        member = jnp.where((token >= start) & (token < end), 1.0, 0.0).astype(jnp.bfloat16)
        sums = sums + dot_nn(member, upper) + dot_nn(member, lower)
    pooled = sums / counts_as_column(sizes_ref, segments)
    pooled_ref[...] = pooled
    inv_norm = lax.rsqrt(jnp.sum(pooled * pooled, axis=1, keepdims=True) + EPS_UNIT)
    units = (pooled * inv_norm).astype(jnp.bfloat16)
    half = segments // 2
    place = lax.broadcasted_iota(jnp.int32, (segments, segments), 0)
    source = lax.broadcasted_iota(jnp.int32, (segments, segments), 1)
    wanted = jnp.where(place < half, 2 * place, 2 * (place - half) + 1)
    pick = jnp.where(source == wanted, 1.0, 0.0).astype(jnp.bfloat16)
    message_ref[:, :width] = dot_nn(pick, units).astype(jnp.bfloat16)
    row = lax.broadcasted_iota(jnp.int32, (segments, LANES), 0)
    column = lax.broadcasted_iota(jnp.int32, (segments, LANES), 1)
    digits = jnp.zeros((segments, LANES), jnp.float32)
    for i in range(half):
        number = matching_ref[i]
        digit = jnp.where(column == 0, number & 255, number >> 8).astype(jnp.float32)
        digits = jnp.where((row == i) & (column < 2), digit, digits)
    message_ref[:, width:] = digits.astype(jnp.bfloat16)
    start_all(outward[8:])
    wait_all(outward)
    wait_all(side_copies)


def forward_step(here, sizes, matching, masks_x, masks_z, given):
    tokens, hidden_units = given[0], given[5].shape[1]
    length, width = tokens.shape
    segments = sizes.shape[1]
    half = len(masks_x)
    query_at, query_end, key_at, key_end = band(length)[0]
    low, full = jnp.bfloat16, jnp.float32
    side = ((half, (hidden_units // width + 3) * (width // half // 2), length), low)
    made = [
        ((length, width), low),
        ((length, width), low),
        ((width, length), low),
        ((length, width), low),
        ((HEADS // 4, 4, length), full),
        ((length, width), full),
        ((length, 1), full),
        ((length, hidden_units), low),
        ((length, width), full),
        ((length, 1), full),
        ((segments, width), full),
        ((segments, width + LANES), low),
    ]
    return pl.pallas_call(
        functools.partial(forward_kernel, segments, masks_x, masks_z),
        in_specs=[smem_spec()] * 3 + [any_spec()] * len(given),
        out_specs=[any_spec()] * (len(made) + 2),
        out_shape=[jax.ShapeDtypeStruct(shape, kind) for shape, kind in made + [side, side]],
        scratch_shapes=[pltpu.VMEM(item.shape, item.dtype) for item in given]
        + [pltpu.VMEM(shape, kind) for shape, kind in made]
        + [
            pltpu.VMEM((width, length), low),
            pltpu.VMEM((width, length), low),
            pltpu.VMEM((width, length), low),
            pltpu.VMEM((width, length), low),
            pltpu.VMEM((hidden_units, length), low),
            pltpu.VMEM((2, key_end - key_at, query_end - query_at), full),
            pltpu.VMEM((length, width), full),
            pltpu.VMEM((length, width), low),
            pltpu.VMEM((length, width), full),
            pltpu.SemaphoreType.DMA((len(given),)),
            pltpu.SemaphoreType.DMA((len(made),)),
            pltpu.SemaphoreType.DMA((2 * 5 * half,)),
        ],
        compiler_params=compiler_params(),
        cost_estimate=cost(28),
        name="forward_step",
    )(here, sizes, matching, *given)


def loss_kernel(
    place_ref,
    sizes_ref,
    sharpness_ref,
    numbers_ref,
    gathered_hbm,
    pooled_hbm,
    normed_hbm,
    inv_hbm,
    gain_hbm,
    loss_ref,
    grad_hidden_hbm,
    grad_branch_hbm,
    sums_ref,
    gathered_ref,
    pooled_ref,
    normed_ref,
    inv_ref,
    gain_ref,
    grad_hidden_ref,
    grad_branch_ref,
    sems,
):
    given = [
        (gathered_hbm, gathered_ref),
        (pooled_hbm, pooled_ref),
        (normed_hbm, normed_ref),
        (inv_hbm, inv_ref),
        (gain_hbm, gain_ref),
    ]
    copies = [
        pltpu.make_async_copy(source, target, sems.at[i])
        for i, (source, target) in enumerate(given)
    ]
    start_all(copies)
    segments, width = pooled_ref.shape
    half = segments // 2
    devices = gathered_ref.shape[0]
    total = devices * half
    sharpness = sharpness_ref[0]
    row = lax.broadcasted_iota(jnp.int32, (total, devices * segments), 0)
    column = lax.broadcasted_iota(jnp.int32, (total, devices * segments), 1)
    source = jnp.bitwise_xor(row // half, place_ref[0]) * segments + row % half
    copies[0].wait()
    gathered = gathered_ref[...].reshape(devices * segments, width + LANES)
    pick = jnp.where(column == source, 1.0, 0.0).astype(jnp.bfloat16)
    picked = dot_nn(pick, gathered)
    questions = picked[:, :width].astype(jnp.bfloat16)
    digits = picked[:, width:]
    pick = jnp.where(column == source + half, 1.0, 0.0).astype(jnp.bfloat16)
    passages = dot_nn(pick, gathered[:, :width]).astype(jnp.bfloat16)
    matching = (digits[:, 0:1] + 256.0 * digits[:, 1:2]).astype(jnp.int32)
    table = dot_nt(questions, passages) / sharpness
    top = jnp.max(table, axis=1, keepdims=True)
    expo = jnp.exp(table - top)
    expo_total = jnp.sum(expo, axis=1, keepdims=True)
    chosen = matching == numbers_ref[...]
    positive = jnp.sum(jnp.where(chosen, table, 0.0), axis=1, keepdims=True)
    loss_ref[...] = (
        jnp.sum(top + jnp.log(expo_total) - positive, axis=0, keepdims=True) / total
    )
    slope = (expo / expo_total - chosen.astype(jnp.float32)) / total
    grad_dot = (slope / sharpness).astype(jnp.bfloat16)
    segment_at = lax.broadcasted_iota(jnp.int32, (segments, total), 0)
    column = lax.broadcasted_iota(jnp.int32, (segments, total), 1)
    mine = column == place_ref[0] * half + segment_at // 2
    is_query = segment_at % 2 == 0
    pick_query = jnp.where(mine & is_query, 1.0, 0.0).astype(jnp.bfloat16)
    pick_passage = jnp.where(mine & ~is_query, 1.0, 0.0).astype(jnp.bfloat16)
    row_terms = dot_nn(pick_query, grad_dot).astype(jnp.bfloat16)
    column_terms = dot_nt(pick_passage, grad_dot).astype(jnp.bfloat16)
    grad_units = dot_nn(row_terms, passages) + dot_nn(column_terms, questions)
    wait_all(copies[1:])
    pooled = pooled_ref[...]
    inv_norm = lax.rsqrt(jnp.sum(pooled * pooled, axis=1, keepdims=True) + EPS_UNIT)
    units = pooled * inv_norm
    along = jnp.sum(units * grad_units, axis=1, keepdims=True)
    grad_pooled = inv_norm * (grad_units - units * along) / counts_as_column(sizes_ref, segments)
    upper = grad_pooled.astype(jnp.bfloat16)
    lower = (grad_pooled - upper.astype(jnp.float32)).astype(jnp.bfloat16)
    both = jnp.concatenate([upper, lower], axis=0)
    start, end = lengths_as_row(sizes_ref, 2 * segments, segments)
    gain = as_row(gain_ref)
    outward = []
    tokens = normed_ref.shape[0]
    chunk = min(tokens, 128)
    gain_sum = jnp.zeros((1, width), jnp.float32)
    shift_sum = jnp.zeros((1, width), jnp.float32)
    bias_sum = jnp.zeros((1, width), jnp.float32)
    for at in range(0, tokens, chunk):
        token = at + lax.broadcasted_iota(jnp.int32, (chunk, 2 * segments), 0)
        member = jnp.where((token >= start) & (token < end), 1.0, 0.0).astype(jnp.bfloat16)
        grad_out = dot_nn(member, both)
        normed = normed_ref[at : at + chunk]
        gain_sum = gain_sum + jnp.sum(grad_out * normed, axis=0, keepdims=True)
        shift_sum = shift_sum + jnp.sum(grad_out, axis=0, keepdims=True)
        grad_hidden = standardize_back(normed, inv_ref[at : at + chunk], grad_out * gain)
        grad_hidden_ref[at : at + chunk] = grad_hidden
        low = grad_hidden.astype(jnp.bfloat16)
        grad_branch_ref[at : at + chunk] = low
        bias_sum = bias_sum + jnp.sum(low.astype(jnp.float32), axis=0, keepdims=True)
        for source_ref, target in (
            (grad_hidden_ref, grad_hidden_hbm),
            (grad_branch_ref, grad_branch_hbm),
        ):
            copy = pltpu.make_async_copy(
                source_ref.at[at : at + chunk],
                target.at[at : at + chunk],
                sems.at[len(copies) + len(outward)],
            )
            copy.start()
            outward.append(copy)
    sums_ref[...] = jnp.concatenate([bias_sum, gain_sum, shift_sum], axis=0)
    wait_all(outward)


def loss_step(place, sizes, sharpness, numbers, gathered, pooled, normed, inv, gain):
    tokens, width = normed.shape
    low, full = jnp.bfloat16, jnp.float32
    chunks = -(-tokens // 128)
    return pl.pallas_call(
        loss_kernel,
        in_specs=[smem_spec()] * 3 + [vmem_spec()] + [any_spec()] * 5,
        out_specs=[vmem_spec(), any_spec(), any_spec(), vmem_spec()],
        out_shape=[
            jax.ShapeDtypeStruct((1, 1), full),
            jax.ShapeDtypeStruct((tokens, width), full),
            jax.ShapeDtypeStruct((tokens, width), low),
            jax.ShapeDtypeStruct((3, width), full),
        ],
        scratch_shapes=[
            pltpu.VMEM(gathered.shape, low),
            pltpu.VMEM(pooled.shape, full),
            pltpu.VMEM(normed.shape, full),
            pltpu.VMEM(inv.shape, full),
            pltpu.VMEM(gain.shape, low),
            pltpu.VMEM((tokens, width), full),
            pltpu.VMEM((tokens, width), low),
            pltpu.SemaphoreType.DMA((5 + 2 * chunks,)),
        ],
        compiler_params=compiler_params(),
        cost_estimate=cost(4),
        name="loss_step",
    )(place, sizes, sharpness, numbers, gathered, pooled, normed, inv, gain)


def before_kernel(
    branch_hbm,
    slope_hbm,
    narrowing_hbm,
    widening_hbm,
    hidden_hbm,
    normed_hbm,
    inv_hbm,
    gain_hbm,
    mixing_hbm,
    grad_pre_hbm,
    bias_ref,
    grad_hidden_hbm,
    grad_branch_hbm,
    grad_attn_hbm,
    sums_ref,
    branch_ref,
    slope_ref,
    narrowing_ref,
    widening_ref,
    total,
    normed_ref,
    inv_ref,
    gain_ref,
    mixing_ref,
    grad_pre_ref,
    grad_hidden_ref,
    grad_branch_ref,
    grad_attn_ref,
    in_sems,
    part_sems,
    out_sems,
):
    tokens, width = branch_ref.shape
    parts = slope_ref.shape[1] // width
    given = [
        (branch_hbm, branch_ref),
        (hidden_hbm, total),
        (normed_hbm, normed_ref),
        (inv_hbm, inv_ref),
        (gain_hbm, gain_ref),
        (mixing_hbm, mixing_ref),
    ]
    copies = [
        pltpu.make_async_copy(source, target, in_sems.at[i])
        for i, (source, target) in enumerate(given)
    ]
    part_copies = []
    for part in range(parts):
        at = pl.ds(part * width, width)
        pairs = [
            (narrowing_hbm.at[at], narrowing_ref.at[at]),
            (slope_hbm.at[:, at], slope_ref.at[:, at]),
            (widening_hbm.at[:, at], widening_ref.at[:, at]),
        ]
        part_copies.append(
            [
                pltpu.make_async_copy(source, target, part_sems.at[part, i])
                for i, (source, target) in enumerate(pairs)
            ]
        )
    start_all(copies[:1] + part_copies[0] + part_copies[1] + copies[1:2])
    outward = []

    def write(source, target):
        copy = pltpu.make_async_copy(source, target, out_sems.at[len(outward)])
        copy.start()
        outward.append(copy)

    def columns_of(part):
        return slice(part * width, (part + 1) * width)

    def product(part):
        return dot_nt(branch_ref[...], narrowing_ref[columns_of(part)])

    wait_all(copies[:1] + part_copies[0][:1])
    waiting = product(0)
    for part in range(parts):
        if part + 2 < parts:
            start_all(part_copies[part + 2])
        elif part + 2 == parts:
            start_all(copies[2:])
        if part == 0:
            wait_all(copies[1:2])
        wait_all(part_copies[part][1:])
        grad_act = waiting
        if part + 1 < parts:
            wait_all(part_copies[part + 1][:1])
            waiting = product(part + 1)
        columns = columns_of(part)
        grad_pre = (grad_act * widen(slope_ref[:, columns])).astype(jnp.bfloat16)
        grad_pre_ref[:, columns] = grad_pre
        bias_ref[:, columns] = jnp.sum(widen(grad_pre), axis=0, keepdims=True)
        total[...] += dot_nt(grad_pre, widening_ref[:, columns])
        at = pl.ds(part * width, width)
        write(grad_pre_ref.at[:, at], grad_pre_hbm.at[:, at])
    wait_all(copies[2:])
    chunk = min(tokens, 128)
    gain = as_row(gain_ref)
    gain_sum = jnp.zeros((1, width), jnp.float32)
    shift_sum = jnp.zeros((1, width), jnp.float32)
    bias_sum = jnp.zeros((1, width), jnp.float32)
    for row in range(0, tokens, chunk):
        grad_out = total[row : row + chunk]
        normed = normed_ref[row : row + chunk]
        gain_sum = gain_sum + jnp.sum(grad_out * normed, axis=0, keepdims=True)
        shift_sum = shift_sum + jnp.sum(grad_out, axis=0, keepdims=True)
        grad_hidden = standardize_back(normed, inv_ref[row : row + chunk], grad_out * gain)
        grad_hidden_ref[row : row + chunk] = grad_hidden
        low = grad_hidden.astype(jnp.bfloat16)
        grad_branch_ref[row : row + chunk] = low
        bias_sum = bias_sum + jnp.sum(widen(low), axis=0, keepdims=True)
        grad_attn_ref[row : row + chunk] = dot_nt(low, mixing_ref[...]).astype(jnp.bfloat16)
    write(grad_branch_ref, grad_branch_hbm)
    write(grad_attn_ref, grad_attn_hbm)
    write(grad_hidden_ref, grad_hidden_hbm)
    sums_ref[...] = jnp.concatenate([bias_sum, gain_sum, shift_sum], axis=0)
    wait_all(outward)


def before_step(branch, slope, narrowing, widening, hidden, normed, inv, gain, mixing):
    tokens, hidden_units = slope.shape
    width = branch.shape[1]
    parts = hidden_units // width
    low, full = jnp.bfloat16, jnp.float32
    return pl.pallas_call(
        before_kernel,
        in_specs=[any_spec()] * 9,
        out_specs=[any_spec(), vmem_spec()] + [any_spec()] * 3 + [vmem_spec()],
        out_shape=[
            jax.ShapeDtypeStruct((tokens, hidden_units), low),
            jax.ShapeDtypeStruct((1, hidden_units), full),
            jax.ShapeDtypeStruct((tokens, width), full),
            jax.ShapeDtypeStruct((tokens, width), low),
            jax.ShapeDtypeStruct((tokens, width), low),
            jax.ShapeDtypeStruct((3, width), full),
        ],
        scratch_shapes=[
            pltpu.VMEM(branch.shape, low),
            pltpu.VMEM(slope.shape, low),
            pltpu.VMEM(narrowing.shape, low),
            pltpu.VMEM(widening.shape, low),
            pltpu.VMEM((tokens, width), full),
            pltpu.VMEM(normed.shape, full),
            pltpu.VMEM(inv.shape, full),
            pltpu.VMEM(gain.shape, low),
            pltpu.VMEM(mixing.shape, low),
            pltpu.VMEM(slope.shape, low),
            pltpu.VMEM((tokens, width), full),
            pltpu.VMEM((tokens, width), low),
            pltpu.VMEM((tokens, width), low),
            pltpu.SemaphoreType.DMA((6,)),
            pltpu.SemaphoreType.DMA((parts, 3)),
            pltpu.SemaphoreType.DMA((parts + 3,)),
        ],
        compiler_params=compiler_params(),
        cost_estimate=cost(11),
        name="before_step",
    )(branch, slope, narrowing, widening, hidden, normed, inv, gain, mixing)


def side_copies(own_ref, other_ref, at, count, target, sems):
    tokens = own_ref.shape[2]
    return [
        pltpu.make_async_copy(
            source.at[:, pl.ds(at, count)],
            target.at[:, :, pl.ds(i * tokens, tokens)],
            sems.at[i],
        )
        for i, source in enumerate((own_ref, other_ref))
    ]


def flat(ref):
    places, rows, tokens = ref.shape
    return ref[...].reshape(places * rows, tokens)


def store_places(product, first, parts, target):
    rows = target.shape[2]
    low = product.astype(jnp.bfloat16)
    for place in range(low.shape[0] // rows // parts):
        for tile in range(low.shape[1] // LANES):
            for part in range(parts):
                row = (place * parts + part) * rows
                target[first + place, tile * parts + part] = low[
                    row : row + rows, tile * LANES : (tile + 1) * LANES
                ]


def outer_kernel(
    own_ref,
    other_ref,
    branch_own_ref,
    branch_other_ref,
    keep_x,
    send_x,
    keep_z,
    send_z,
    left_x,
    left_z,
    right,
    made_x,
    made_z,
    left_sems,
    right_sems,
    out_sems,
):
    places, count, _ = left_x.shape
    tokens = branch_own_ref.shape[0]
    half = places // 2
    parts = count // made_x.shape[2]
    copies = [
        pltpu.make_async_copy(source, right.at[pl.ds(i * tokens, tokens)], right_sems.at[i])
        for i, source in enumerate((branch_own_ref, branch_other_ref))
    ]
    copies_x = side_copies(own_ref, other_ref, 0, count, left_x, left_sems.at[0])
    copies_z = side_copies(own_ref, other_ref, count, count, left_z, left_sems.at[1])
    start_all(copies + copies_x + copies_z)
    wait_all(copies + copies_x)
    units = [
        (left_x, made_x, half, send_x),
        (left_x, made_x, 0, keep_x),
        (left_z, made_z, half, send_z),
        (left_z, made_z, 0, keep_z),
    ]

    def product(n):
        left, _, first, _ = units[n]
        if n == 2:
            wait_all(copies_z)
        return dot_nn(
            left[first : first + half].reshape(half * count, 2 * tokens), right[...]
        )

    outward = []
    waiting = product(0)
    for n, (_, made, first, target) in enumerate(units):
        current = waiting
        if n + 1 < len(units):
            waiting = product(n + 1)
        store_places(current, first, parts, made)
        copy = pltpu.make_async_copy(made.at[pl.ds(first, half)], target, out_sems.at[n])
        copy.start()
        outward.append(copy)
    wait_all(outward)


def outer_step(own, other, branch_own, branch_other, count):
    places, _, tokens = own.shape
    width = branch_own.shape[1]
    parts = 2
    rows = count // parts
    low = jnp.bfloat16
    blocks = width // LANES * parts
    shape = jax.ShapeDtypeStruct((places // 2, blocks, rows, LANES), low)
    return pl.pallas_call(
        outer_kernel,
        in_specs=[any_spec(), got_spec(), any_spec(), got_spec()],
        out_specs=[any_spec()] * 4,
        out_shape=[shape] * 4,
        scratch_shapes=[
            pltpu.VMEM((places, count, 2 * tokens), low),
            pltpu.VMEM((places, count, 2 * tokens), low),
            pltpu.VMEM((2 * tokens, width), low),
            pltpu.VMEM((places, blocks, rows, LANES), low),
            pltpu.VMEM((places, blocks, rows, LANES), low),
            pltpu.SemaphoreType.DMA((2, 2)),
            pltpu.SemaphoreType.DMA((2,)),
            pltpu.SemaphoreType.DMA((4,)),
        ],
        compiler_params=compiler_params(),
        cost_estimate=cost(5),
        name="outer_step",
    )(own, other, branch_own, branch_other)


def inner_kernel(
    at,
    side_ref,
    own_ref,
    other_ref,
    grad_own_hbm,
    grad_other_hbm,
    keep_x,
    send_x,
    keep_y,
    send_y,
    left,
    right,
    made_x,
    made_y,
    left_sems,
    in_sems,
    out_sems,
):
    tokens, hidden_units = grad_own_hbm.shape
    places, rows, _ = left.shape
    half = places // 2
    parts = 4
    width = hidden_units // parts
    tiles = width // LANES
    side = side_ref[0]
    left_copies = side_copies(own_ref, other_ref, at, rows, left, left_sems)
    right_copies = []
    for part in range(parts):
        columns = pl.ds(part * width, width)
        right_copies.append(
            [
                pltpu.make_async_copy(
                    source.at[:, columns],
                    right.at[pl.ds(i * tokens, tokens), columns],
                    in_sems.at[part, i],
                )
                for i, source in enumerate((grad_own_hbm, grad_other_hbm))
            ]
        )
    start_all(left_copies)
    for copies in right_copies:
        start_all(copies)
    outward = []

    def write(source, target):
        copy = pltpu.make_async_copy(source, target, out_sems.at[len(outward)])
        copy.start()
        outward.append(copy)

    def weight(part):
        return dot_nn(flat(left), right[:, part * width : (part + 1) * width])

    def store_weight(part, product):
        low = product.astype(jnp.bfloat16)
        for place in range(places):
            for tile in range(tiles):
                block = low[place * rows : (place + 1) * rows, tile * LANES : (tile + 1) * LANES]
                if part < parts // 2:
                    made_x[place, part * tiles + tile] = block
                else:
                    made_y[jnp.bitwise_xor(side, part - parts // 2), place, tile] = block
        if part == parts // 2 - 1:
            write(made_x.at[pl.ds(half, half)], send_x)
            write(made_x.at[pl.ds(0, half)], keep_x)
        if part == parts - 1:
            write(made_y.at[1], send_y)
            write(made_y.at[0], keep_y)

    wait_all(left_copies)
    products = []
    for part in range(parts):
        wait_all(right_copies[part])
        products.append(weight(part))
        if part >= 1:
            store_weight(part - 1, products.pop(0))
    store_weight(parts - 1, products.pop(0))
    wait_all(outward)


def inner_step(side, own, other, at, rows, grad_own, grad_other):
    places, _, tokens = own.shape
    hidden_units = grad_own.shape[1]
    tiles = hidden_units // 4 // LANES
    half = places // 2
    low = jnp.bfloat16
    shape_x = jax.ShapeDtypeStruct((half, 2 * tiles, rows, LANES), low)
    shape_y = jax.ShapeDtypeStruct((places, tiles, rows, LANES), low)
    return pl.pallas_call(
        functools.partial(inner_kernel, at),
        in_specs=[smem_spec(), any_spec(), got_spec(), any_spec(), got_spec()],
        out_specs=[any_spec()] * 4,
        out_shape=[shape_x, shape_x, shape_y, shape_y],
        scratch_shapes=[
            pltpu.VMEM((places, rows, 2 * tokens), low),
            pltpu.VMEM((2 * tokens, hidden_units), low),
            pltpu.VMEM((places, 2 * tiles, rows, LANES), low),
            pltpu.VMEM((2, places, tiles, rows, LANES), low),
            pltpu.SemaphoreType.DMA((2,)),
            pltpu.SemaphoreType.DMA((4, 2)),
            pltpu.SemaphoreType.DMA((4,)),
        ],
        compiler_params=compiler_params(),
        cost_estimate=cost(5),
        name="inner_step",
    )(side, own, other, grad_own, grad_other)


def attend_back_kernel(
    segments,
    sizes_ref,
    query_ref,
    key_ref,
    key_t_ref,
    value_ref,
    lse_ref,
    grad_ref,
    grads_ref,
    sums_ref,
    fill,
    query_t,
    total_key,
    total_value,
):
    length, wide = query_ref.shape
    ranges = band(length)
    step = pl.program_id(0)

    @pl.when(step == 0)
    def _():
        for i, (query_at, query_end, key_at, key_end) in enumerate(ranges):
            fill[i] = mask_of(sizes_ref, segments, query_at, query_end, key_at, key_end)

    total_key[...] = jnp.zeros_like(total_key)
    total_value[...] = jnp.zeros_like(total_value)
    lane = lax.broadcasted_iota(jnp.int32, (1, LANES), 1)
    units = [(at, i) for at in range(wide // HD) for i in range(len(ranges))]

    def lanes_of(at):
        first = at * HD // LANES * LANES
        return slice(first, first + LANES), (lane // HD) == (at * HD - first) // HD

    def products(unit):
        at, i = unit
        query_at, query_end, key_at, key_end = ranges[i]
        lanes, head = lanes_of(at)
        query = jnp.where(head, query_ref[query_at:query_end, lanes], 0)
        grad = jnp.where(head, grad_ref[query_at:query_end, lanes], 0)
        scores = dot_nt(key_ref[key_at:key_end, lanes], query) + fill[i]
        return scores, dot_nt(value_ref[key_at:key_end, lanes], grad)

    def back(unit, scores, grad_probs):
        at, i = unit
        query_at, query_end, key_at, key_end = ranges[i]
        probs = jnp.exp(scores - lse_ref[0, at : at + 1, query_at:query_end])
        inner = jnp.sum(grad_probs * probs, axis=0, keepdims=True)
        return probs.astype(jnp.bfloat16), (probs * (grad_probs - inner)).astype(jnp.bfloat16)

    def finish(unit, probs, grad_scores):
        at, i = unit
        query_at, query_end, key_at, key_end = ranges[i]
        lanes, head = lanes_of(at)
        query = jnp.where(head, query_ref[query_at:query_end, lanes], 0)
        grad = jnp.where(head, grad_ref[query_at:query_end, lanes], 0)
        total_value[key_at:key_end, lanes] += dot_nn(probs, grad)
        total_key[key_at:key_end, lanes] += dot_nn(grad_scores, query)
        query_t[at * HD : (at + 1) * HD, query_at:query_end] = dot_nn(
            key_t_ref[at * HD : (at + 1) * HD, key_at:key_end], grad_scores
        )

    ahead = 2
    waiting = [products(unit) for unit in units[:ahead]]
    done = []
    for n, unit in enumerate(units):
        if n + ahead < len(units):
            waiting.append(products(units[n + ahead]))
        done.append((unit, *back(unit, *waiting.pop(0))))
        if len(done) > 1:
            finish(*done.pop(0))
    for item in done:
        finish(*item)
    grad_query = (query_t[...] * HD ** (-0.5)).T.astype(jnp.bfloat16)
    grad_value = total_value[...].astype(jnp.bfloat16)
    grads_ref[0] = grad_query
    grads_ref[1] = total_key[...].astype(jnp.bfloat16)
    grads_ref[2] = grad_value
    sums_ref[...] = jnp.concatenate(
        [
            jnp.sum(widen(grad_query), axis=0, keepdims=True),
            jnp.sum(widen(grad_value), axis=0, keepdims=True),
        ],
        axis=0,
    )


def attend_back_step(sizes, query, key, key_t, value, lse, grad):
    tokens, width = query.shape
    heads_here = lse.shape[1]
    wide = heads_here * HD
    columns = pl.BlockSpec((tokens, wide), lambda i: (0, i))
    query_at, query_end, key_at, key_end = band(tokens)[0]
    return pl.pallas_call(
        functools.partial(attend_back_kernel, sizes.shape[1]),
        grid=(width // wide,),
        in_specs=[
            smem_spec(),
            columns,
            columns,
            pl.BlockSpec((wide, tokens), lambda i: (i, 0)),
            columns,
            pl.BlockSpec((1, heads_here, tokens), lambda i: (i, 0, 0)),
            columns,
        ],
        out_specs=[
            pl.BlockSpec((3, tokens, wide), lambda i: (0, 0, i)),
            pl.BlockSpec((2, wide), lambda i: (0, i)),
        ],
        out_shape=[
            jax.ShapeDtypeStruct((3, tokens, width), jnp.bfloat16),
            jax.ShapeDtypeStruct((2, width), jnp.float32),
        ],
        scratch_shapes=[
            pltpu.VMEM((2, key_end - key_at, query_end - query_at), jnp.float32),
            pltpu.VMEM((wide, tokens), jnp.float32),
            pltpu.VMEM((tokens, wide), jnp.float32),
            pltpu.VMEM((tokens, wide), jnp.float32),
        ],
        compiler_params=compiler_params(),
        cost_estimate=cost(8),
        name="attend_back_step",
    )(sizes, query, key, key_t, value, lse, grad)


def add_kernel(shape_of, *refs):
    counts, last = shape_of
    pairs = sum(counts) + last
    given, refs = refs[: 2 * pairs], refs[2 * pairs :]
    outputs = 2 * len(counts) + (1 if last else 0)
    targets, refs = refs[:outputs], refs[outputs:]
    local, refs = refs[: 2 * pairs], refs[2 * pairs :]
    made, refs = refs[:outputs], refs[outputs:]
    in_sems, out_sems = refs
    copies = [
        pltpu.make_async_copy(source, target, in_sems.at[n])
        for n, (source, target) in enumerate(zip(given, local))
    ]
    start_all(copies)
    outward = []

    def write(n):
        copy = pltpu.make_async_copy(made[n], targets[n], out_sems.at[n])
        copy.start()
        outward.append(copy)

    at = 0
    for item, count in enumerate(counts):
        kept, sent = made[2 * item], made[2 * item + 1]
        half = kept.shape[0]
        block = 0
        for _ in range(count):
            wait_all(copies[2 * at : 2 * at + 2])
            keep, got = local[2 * at], local[2 * at + 1]
            blocks = slice(block, block + keep.shape[1])
            sent[:, blocks] = (widen(keep[half:]) + widen(got[half:])).astype(sent.dtype)
            kept[:, blocks] = widen(keep[:half]) + widen(got[:half])
            block += keep.shape[1]
            at += 1
        write(2 * item + 1)
        write(2 * item)
    if last:
        mine = made[-1]
        block = 0
        for _ in range(last):
            wait_all(copies[2 * at : 2 * at + 2])
            keep, got = local[2 * at], local[2 * at + 1]
            blocks = slice(block, block + keep.shape[1])
            mine[blocks] = (widen(keep[0]) + widen(got[0])).astype(mine.dtype)
            block += keep.shape[1]
            at += 1
        write(outputs - 1)
    wait_all(outward)


def add_step(items, last=(), name="add_step"):
    given, shapes = [], []
    for pairs in items:
        for pair in pairs:
            given.extend(pair)
        places, _, rows, lanes = pairs[0][0].shape
        blocks = sum(keep.shape[1] for keep, _ in pairs)
        shape = (places // 2, blocks, rows, lanes)
        shapes.append((shape, jnp.float32))
        shapes.append((shape, pairs[0][1].dtype))
    for pair in last:
        given.extend(pair)
    if last:
        _, _, rows, lanes = last[0][0].shape
        blocks = sum(keep.shape[1] for keep, _ in last)
        shapes.append(((blocks, rows, lanes), jnp.bfloat16))
    results = pl.pallas_call(
        functools.partial(add_kernel, ([len(pairs) for pairs in items], len(last))),
        in_specs=[got_spec()] * len(given),
        out_specs=[any_spec()] * len(shapes),
        out_shape=[jax.ShapeDtypeStruct(shape, kind) for shape, kind in shapes],
        scratch_shapes=[pltpu.VMEM(item.shape, item.dtype) for item in given]
        + [pltpu.VMEM(shape, kind) for shape, kind in shapes]
        + [pltpu.SemaphoreType.DMA((len(given),)), pltpu.SemaphoreType.DMA((len(shapes),))],
        compiler_params=compiler_params(),
        cost_estimate=cost(2),
        name=name,
    )(*given)
    halves = [(results[2 * n], results[2 * n + 1]) for n in range(len(items))]
    return halves + ([results[-1]] if last else [])


def split_vector(total, rows):
    places, _, count, lanes = total.shape
    parts = []
    for _ in range(3):
        low = total.astype(jnp.bfloat16)
        total = total - widen(low)
        parts.append(low)
    if rows > 3 * count:
        parts.append(jnp.zeros((places, 1, rows - 3 * count, lanes), jnp.bfloat16))
    return jnp.concatenate(parts, axis=2)


def join_vector(block, count):
    return sum(widen(block[..., i * count : (i + 1) * count, :]) for i in range(3))


def round_kernel(plan, passes, inputs, streams, *refs):
    given, refs = refs[:inputs], refs[inputs:]
    outputs = len(plan) - sum(1 for item in plan if item[5]) + streams
    targets, refs = refs[:outputs], refs[outputs:]
    local, refs = refs[:inputs], refs[inputs:]
    made, (in_sems, out_sems) = refs[:outputs], refs[outputs:]
    sent_to = made[outputs - streams :]
    copies = []
    passed = {}
    for n, source in enumerate(given):
        if n in passes:
            stream, at = passes[n]
            target = sent_to[stream].at[pl.ds(at, source.shape[0])]
            passed.setdefault(stream, []).append(n)
        else:
            target = local[n]
        copies.append(pltpu.make_async_copy(source, target, in_sems.at[n]))
    start_all(copies)
    wait_all(copies)
    outward = []

    def write(n):
        copy = pltpu.make_async_copy(made[n], targets[n], out_sems.at[n])
        copy.start()
        outward.append(copy)

    kept_at = 0
    for keep_at, got_at, begin, stream, at, whole, vector in plan:
        keep = local[keep_at]
        places, blocks, rows, lanes = keep.shape
        total = widen(keep[...])
        if vector and keep.dtype == jnp.bfloat16:
            total = join_vector(keep[...], 8)
        if got_at is not None:
            got = local[got_at][begin : begin + places * blocks]
            if vector:
                total = total + join_vector(got, 8)[:, None]
            else:
                total = total + widen(got.reshape(keep.shape))
        target = sent_to[stream]
        if not whole:
            made[kept_at][...] = total[: places // 2]
            write(kept_at)
            kept_at += 1
            total = total[places // 2 :]
        if vector:
            send = split_vector(total, target.shape[1])
        else:
            send = total.astype(jnp.bfloat16)
        count = send.shape[0] * blocks
        target[at : at + count] = send.reshape((count,) + target.shape[1:])
    for n in range(outputs - streams, outputs):
        write(n)
    wait_all(outward)


def round_step(chains, received, rows):
    given, kept, plan, passes = [], [], [], {}
    at_of, lengths = {}, {}
    stream_keys = list(received)
    given = [received[key] for key in stream_keys]
    hops = []
    for chain in chains.values():
        if chain["hops"] and chain["hops"][0] not in hops:
            hops.append(chain["hops"][0])
    shapes = []
    for name, chain in chains.items():
        if not chain["hops"]:
            continue
        hop = chain["hops"][0]
        at = lengths.get(hop, 0)
        at_of[name] = at
        if chain["send"] is not None:
            given.append(chain["send"].reshape((-1,) + chain["send"].shape[-2:]))
            passes[len(given) - 1] = (hops.index(hop), at)
            lengths[hop] = at + given[-1].shape[0]
            continue
        keep = chain["keep"]
        given.append(keep)
        keep_at = len(given) - 1
        got_at, begin = None, 0
        if chain["got"] is not None:
            got_at, begin = stream_keys.index(chain["got"][0]), chain["got"][1]
        places, blocks = keep.shape[:2]
        whole = places == 1
        plan.append((keep_at, got_at, begin, hops.index(hop), at, whole, chain["vector"]))
        lengths[hop] = at + (blocks if whole else places // 2 * blocks)
        if not whole:
            shapes.append(((places // 2,) + keep.shape[1:], jnp.float32))
            kept.append(name)
    shapes = shapes + [((lengths[hop], rows, LANES), jnp.bfloat16) for hop in hops]
    results = pl.pallas_call(
        functools.partial(round_kernel, plan, passes, len(given), len(hops)),
        in_specs=[got_spec()] * len(given),
        out_specs=[any_spec()] * len(shapes),
        out_shape=[jax.ShapeDtypeStruct(shape, kind) for shape, kind in shapes],
        scratch_shapes=[
            pltpu.VMEM((8, LANES) if n in passes else item.shape, item.dtype)
            for n, item in enumerate(given)
        ]
        + [pltpu.VMEM(shape, kind) for shape, kind in shapes]
        + [pltpu.SemaphoreType.DMA((len(given),)), pltpu.SemaphoreType.DMA((len(shapes),))],
        compiler_params=compiler_params(),
        cost_estimate=cost(3),
        name="round_step",
    )(*given)
    sent = dict(zip(hops, results[len(kept) :]))
    keeps = dict(zip(kept, results))
    for name, chain in chains.items():
        if not chain["hops"]:
            continue
        hop = chain["hops"].pop(0)
        at = at_of[name]
        if chain["send"] is not None:
            chain["send"] = None
        elif name in keeps:
            chain["keep"] = keeps[name]
        else:
            count = chain["keep"].shape[1]
            chain["keep"] = sent[hop][at : at + count][None]
        chain["got"] = (hop, at)
    return sent


def token_kernel(hidden_ref, grads_ref, question_ref, lookup_ref, content_ref, out_ref):
    out_ref[...] = (
        hidden_ref[...]
        + dot_nt(grads_ref[0], question_ref[...])
        + dot_nt(grads_ref[1], lookup_ref[...])
        + dot_nt(grads_ref[2], content_ref[...])
    )


def token_step(hidden, grads, question, lookup, content):
    tokens, width = hidden.shape
    wide = 2 * LANES
    weight = pl.BlockSpec((wide, width), lambda i: (i, 0))
    column = pl.BlockSpec((tokens, wide), lambda i: (0, i))
    return pl.pallas_call(
        token_kernel,
        grid=(width // wide,),
        in_specs=[column, pl.BlockSpec((3, tokens, width), lambda i: (0, 0, 0))] + [weight] * 3,
        out_specs=column,
        out_shape=jax.ShapeDtypeStruct((tokens, width), jnp.float32),
        compiler_params=compiler_params(),
        cost_estimate=cost(5),
        name="token_step",
    )(hidden, grads, question, lookup, content)


def attention_kernel(
    token_at,
    attn_at,
    places_z,
    side_ref,
    own_ref,
    other_ref,
    grads_own_ref,
    grads_other_ref,
    branch_own_ref,
    branch_other_ref,
    keep_x,
    send_x,
    keep_y,
    send_y,
    keep_z,
    send_z,
    token_left,
    attn_left,
    token_right,
    attn_right,
    made_x,
    made_y,
    made_z,
    left_sems,
    right_sems,
    out_sems,
):
    places, rows, _ = token_left.shape
    tokens = branch_own_ref.shape[0]
    wide = 2 * LANES
    left_copies = side_copies(own_ref, other_ref, token_at, rows, token_left, left_sems.at[0])
    attn_copies = side_copies(own_ref, other_ref, attn_at, rows, attn_left, left_sems.at[1])
    right_copies = []
    for chunk in range(3):
        columns = pl.ds(chunk * wide, wide)
        copies = []
        for core, (grads, branch) in enumerate(
            ((grads_own_ref, branch_own_ref), (grads_other_ref, branch_other_ref))
        ):
            token_rows = pl.ds(core * tokens, tokens)
            pairs = [
                (grads.at[i, :, columns], token_right.at[chunk, token_rows, pl.ds(i * wide, wide)])
                for i in range(3)
            ]
            pairs.append((branch.at[:, columns], attn_right.at[chunk, token_rows]))
            for i, (source, target) in enumerate(pairs):
                copies.append(
                    pltpu.make_async_copy(source, target, right_sems.at[chunk, 4 * core + i])
                )
        right_copies.append(copies)
    start_all(left_copies + right_copies[0][:3] + right_copies[0][4:7] + attn_copies)
    start_all(right_copies[0][3:4] + right_copies[0][7:] + right_copies[1] + right_copies[2])
    outward = []
    half = places // 2
    side = side_ref[0]
    for chunk in range(3):
        if chunk == 0:
            wait_all(left_copies + right_copies[0][:3] + right_copies[0][4:7])
        else:
            wait_all(right_copies[chunk])
        token_product = dot_nn(flat(token_left), token_right[chunk]).astype(jnp.bfloat16)
        if chunk == 0:
            wait_all(attn_copies + right_copies[0][3:4] + right_copies[0][7:])
        attn_product = dot_nn(flat(attn_left), attn_right[chunk]).astype(jnp.bfloat16)
        products = [
            token_product[:, :wide],
            attn_product,
            token_product[:, wide : 2 * wide],
            token_product[:, 2 * wide :],
        ]
        for which, product in enumerate(products):
            for place in range(places):
                for tile in range(2):
                    block = product[
                        place * rows : (place + 1) * rows, tile * LANES : (tile + 1) * LANES
                    ]
                    if chunk == 0:
                        made_x[place, which * 2 + tile] = block
                    elif chunk == 1:
                        where = jnp.bitwise_xor(side, which // 2)
                        made_y[where, place, which % 2 * 2 + tile] = block
                    else:
                        made_z[places_z[place], which * 2 + tile] = block
        if chunk == 0:
            pairs = [(made_x.at[:half], keep_x), (made_x.at[half:], send_x)]
        elif chunk == 1:
            pairs = [(made_y.at[0], keep_y), (made_y.at[1], send_y)]
        else:
            pairs = [(made_z.at[:half], keep_z), (made_z.at[half:], send_z)]
        for source, target in pairs:
            copy = pltpu.make_async_copy(source, target, out_sems.at[len(outward)])
            copy.start()
            outward.append(copy)
    wait_all(outward)


def attention_step(
    side, own, other, token_at, attn_at, rows, places_z, grads, grads_other, branch, branch_other
):
    places, _, tokens = own.shape
    wide = 2 * LANES
    low = jnp.bfloat16
    half = places // 2
    shape = jax.ShapeDtypeStruct((half, 8, rows, LANES), low)
    shape_y = jax.ShapeDtypeStruct((places, 4, rows, LANES), low)
    return pl.pallas_call(
        functools.partial(attention_kernel, token_at, attn_at, places_z),
        in_specs=[smem_spec()] + [any_spec(), got_spec()] * 3,
        out_specs=[any_spec()] * 6,
        out_shape=[shape, shape, shape_y, shape_y, shape, shape],
        scratch_shapes=[
            pltpu.VMEM((places, rows, 2 * tokens), low),
            pltpu.VMEM((places, rows, 2 * tokens), low),
            pltpu.VMEM((3, 2 * tokens, 3 * wide), low),
            pltpu.VMEM((3, 2 * tokens, wide), low),
            pltpu.VMEM((places, 8, rows, LANES), low),
            pltpu.VMEM((2, places, 4, rows, LANES), low),
            pltpu.VMEM((places, 8, rows, LANES), low),
            pltpu.SemaphoreType.DMA((2, 2)),
            pltpu.SemaphoreType.DMA((3, 8)),
            pltpu.SemaphoreType.DMA((6,)),
        ],
        compiler_params=compiler_params(),
        cost_estimate=cost(6),
        name="attention_step",
    )(side, own, other, grads, grads_other, branch, branch_other)


def body(
    hidden_states_in,
    piece_sizes,
    matching_passage_number,
    softmax_sharpness,
    question_projection,
    question_offset,
    lookup_projection,
    content_projection,
    content_offset,
    mixing_result_projection,
    mixing_result_offset,
    mixing_layernorm_scale,
    mixing_layernorm_offset,
    widening_projection,
    widening_offset,
    narrowing_projection,
    narrowing_offset,
    perceptron_layernorm_scale,
    perceptron_layernorm_offset,
):
    rows_here, length, width = hidden_states_in.shape
    segments = piece_sizes.shape[1]
    per_device = segments // 2
    groups_y = lax.axis_size("gy")
    rows = width // groups_y
    inner_rows = widening_offset.shape[0] // groups_y
    gy_bits = powers_below(groups_y)
    order_x = gy_bits[1:]
    order_z = gy_bits[2:3] + gy_bits[1:2] + gy_bits[3:]
    here = lax.axis_index("gy").astype(jnp.int32).reshape(1)
    side = (lax.axis_index("gx").astype(jnp.int32) & 1).reshape(1)
    (
        queries,
        keys,
        keys_t,
        values,
        lse,
        normed_one,
        inv_one,
        slope,
        normed_two,
        inv_two,
        pooled,
        message,
        side_own,
        side_send,
    ) = forward_step(
        here,
        piece_sizes,
        matching_passage_number,
        place_masks(order_x),
        place_masks(order_z),
        [
            hidden_states_in[0],
            question_projection,
            lookup_projection,
            content_projection,
            mixing_result_projection,
            widening_projection,
            narrowing_projection,
            question_offset,
            content_offset,
            mixing_result_offset,
            mixing_layernorm_scale,
            mixing_layernorm_offset,
            widening_offset,
            narrowing_offset,
            perceptron_layernorm_scale,
            perceptron_layernorm_offset,
        ],
    )
    gathered, numbers_of, place, side_other = gather_blocks(
        message, swap_with(side_send, "gy", 1)
    )
    numbers = (numbers_of[:, None] * per_device + np.arange(per_device)[None, :]).reshape(1, -1)
    loss_out, grad_hidden_two, branch_two, sums_two = loss_step(
        place.astype(jnp.int32).reshape(1),
        piece_sizes,
        softmax_sharpness,
        jnp.asarray(numbers, jnp.int32),
        gathered,
        pooled,
        normed_two,
        inv_two,
        perceptron_layernorm_scale,
    )
    branch_two_other = swap_with(branch_two, "gy", 1)
    outer_keep_x, outer_send_x, outer_keep_z, outer_send_z = outer_step(
        side_own, side_other, branch_two, branch_two_other, inner_rows // 2
    )
    outer_send_x, outer_send_z, branch_two = tie(outer_send_x, outer_send_z, branch_two)
    outer_got_x = swap_with(outer_send_x, "gy", order_x[0])
    outer_got_z = swap_with(outer_send_z, "gy", order_z[0])
    grad_pre, grad_b_inner, grad_hidden_one, branch_one, grad_attn, sums_one = before_step(
        branch_two,
        slope,
        narrowing_projection,
        widening_projection,
        grad_hidden_two,
        normed_one,
        inv_one,
        mixing_layernorm_scale,
        mixing_result_projection,
    )
    outer_got_x, outer_got_z, grad_pre, branch_one, grad_attn = tie(
        outer_got_x, outer_got_z, grad_pre, branch_one, grad_attn
    )
    grad_pre_other = swap_with(grad_pre, "gy", 1)
    branch_one_other = swap_with(branch_one, "gy", 1)
    (outer_keep_x, outer_send_x), (outer_keep_z, outer_send_z) = add_step(
        [[(outer_keep_x, outer_got_x)], [(outer_keep_z, outer_got_z)]]
    )
    outer_send_x, outer_send_z, grad_attn = tie(outer_send_x, outer_send_z, grad_attn)
    outer_got_x = swap_with(outer_send_x, "gy", order_x[1])
    outer_got_z = swap_with(outer_send_z, "gy", order_z[1])
    grads, sums_attn = attend_back_step(
        piece_sizes,
        queries,
        keys,
        keys_t,
        values,
        lse,
        grad_attn,
    )
    grads, grad_pre_other, branch_one_other, outer_got_x, outer_got_z = tie(
        grads, grad_pre_other, branch_one_other, outer_got_x, outer_got_z
    )
    grads_other = swap_with(grads, "gy", 1)
    (outer_keep_x, outer_send_x), (outer_keep_z, outer_send_z) = add_step(
        [[(outer_keep_x, outer_got_x)], [(outer_keep_z, outer_got_z)]]
    )
    outer_got_x = swap_with(outer_send_x, "gy", order_x[2])
    outer_got_z = swap_with(outer_send_z, "gy", order_z[2])
    vectors = jnp.concatenate([sums_attn, sums_one, sums_two], axis=0)
    vectors = vectors.reshape(8, groups_y, rows).transpose(1, 0, 2).reshape(groups_y, 8 * rows)
    vectors = jnp.concatenate([vectors, grad_b_inner.reshape(groups_y, -1)], axis=1)
    used = vectors.shape[1]
    vectors = jnp.pad(vectors, ((0, 0), (0, 8 * LANES - used)))
    vectors = vectors.reshape((2,) * len(gy_bits) + (8 * LANES,))
    for axis, bit in enumerate(reversed(gy_bits)):
        high = (lax.axis_index("gy") & bit) != 0
        vectors = jnp.where(high, jnp.flip(vectors, axis=axis), vectors)
    vectors = vectors.transpose(tuple(reversed(range(len(gy_bits)))) + (len(gy_bits),))
    vectors = vectors.reshape(2, groups_y // 2, 1, 8, LANES)
    vector_got = swap_with(vectors[1], "gy", gy_bits[0])
    inner_keep_x, inner_send_x, inner_keep_y, inner_send_y = inner_step(
        side, side_own, side_other, inner_rows, rows, grad_pre, grad_pre_other
    )
    gx_bits = powers_below(lax.axis_size("gx"))
    inner_send_x, inner_send_y, grads_other = tie(inner_send_x, inner_send_y, grads_other)
    inner_got_x = swap_with(inner_send_x, "gy", order_x[0])
    inner_got_y = swap_with(inner_send_y, "gx", 1)
    masks_x, masks_z = place_masks(order_x), place_masks(order_z)
    attn_keep_x, attn_send_x, attn_keep_y, attn_send_y, attn_keep_z, attn_send_z = attention_step(
        side,
        side_own,
        side_other,
        inner_rows + rows,
        inner_rows + 2 * rows,
        rows,
        [masks_z.index(mask) for mask in masks_x],
        grads,
        grads_other,
        branch_one,
        branch_one_other,
    )
    attn_got_x = swap_with(attn_send_x, "gy", order_x[0])
    attn_got_y = swap_with(attn_send_y, "gx", 1)
    attn_got_z = swap_with(attn_send_z, "gy", order_z[0])
    gx_hops = [("gx", bit) for bit in gx_bits]
    hops_x = [("gy", bit) for bit in order_x]
    hops_z = [("gy", bit) for bit in order_z]
    hops_y = gx_hops[:1] + hops_x + gx_hops[1:] + gx_hops[:1]
    vector_keep = vectors[0] + vector_got

    def chain(keep, got, send, hops, vector=False):
        return {
            "keep": keep,
            "got": got,
            "send": send,
            "hops": list(hops),
            "vector": vector,
        }

    chains = {
        "inner_x": chain(inner_keep_x, ("inner_x", 0), None, hops_x[1:] + gx_hops),
        "inner_y": chain(inner_keep_y, ("inner_y", 0), None, hops_y[1:]),
        "vector": chain(vector_keep, None, None, [("gy", b) for b in gy_bits[1:]] + gx_hops, True),
        "outer_x": chain(outer_keep_x, ("outer_x", 0), None, hops_x[3:] + gx_hops),
        "outer_z": chain(outer_keep_z, ("outer_z", 0), None, hops_z[3:] + gx_hops),
    }
    received = {
        "inner_x": inner_got_x,
        "inner_y": inner_got_y,
        "outer_x": outer_got_x,
        "outer_z": outer_got_z,
    }
    received = {key: item.reshape((-1,) + item.shape[-2:]) for key, item in received.items()}
    finals = {}

    def finish():
        for name, item in chains.items():
            if not item["hops"] and name not in finals:
                hop, at = item["got"]
                count = item["keep"].shape[1]
                finals[name] = (item["keep"][0], received[hop][at : at + count])

    sent = round_step(chains, received, rows)
    keys = list(sent)
    *items, grads = tie(*[sent[key] for key in keys], grads)
    items = [swap_with(item, key[0], key[1]) for item, key in zip(items, keys)]
    grad_tokens = token_step(
        grad_hidden_one, grads, question_projection, lookup_projection, content_projection
    )
    *items, attn_got_x, attn_got_y, attn_got_z, grad_tokens = tie(
        *items, attn_got_x, attn_got_y, attn_got_z, grad_tokens
    )
    received = dict(zip(keys, items))
    finish()
    begun = {"attn_x": attn_got_x, "attn_y": attn_got_y, "attn_z": attn_got_z}
    for name, item in begun.items():
        received[name] = item.reshape((-1,) + item.shape[-2:])
    chains["attn_x"] = chain(attn_keep_x, ("attn_x", 0), None, hops_x[1:] + gx_hops)
    chains["attn_y"] = chain(attn_keep_y, ("attn_y", 0), None, hops_y[1:])
    chains["attn_z"] = chain(attn_keep_z, ("attn_z", 0), None, hops_z[1:] + gx_hops)
    while any(item["hops"] for item in chains.values()):
        sent = round_step(chains, received, rows)
        keys = list(sent)
        items = tie(*[swap_with(sent[key], key[0], key[1]) for key in keys])
        received = dict(zip(keys, items))
        finish()

    def summed(name):
        mine, other = finals[name]
        return widen(mine) + widen(other)

    def side_by_side(name):
        mine, other = finals[name]
        high = (lax.axis_index("gx") & 1) != 0
        return widen(
            jnp.concatenate([jnp.where(high, other, mine), jnp.where(high, mine, other)], axis=0)
        )

    vectors = sum(join_vector(item, 8) for item in finals["vector"])
    vectors = vectors.reshape(1, 8 * LANES)[:, :used]
    outer_x, outer_z = summed("outer_x"), summed("outer_z")
    attn_x, attn_y, attn_z = summed("attn_x"), side_by_side("attn_y"), summed("attn_z")
    inner_sums = jnp.concatenate([summed("inner_x"), side_by_side("inner_y")], axis=0)
    vector_sums = vectors[0]
    b_query, b_value, b_output, gain_attn, shift_attn, b_outer, gain_ffn, shift_ffn = [
        vector_sums[i * rows : (i + 1) * rows] for i in range(8)
    ]
    grad_w_query, grad_w_output, grad_w_key, grad_w_value = [
        share_of(
            jnp.concatenate([part[2 * i : 2 * i + 2] for part in (attn_x, attn_y, attn_z)]), width
        )
        for i in range(4)
    ]
    grad_w_outer = jnp.concatenate([share_of(outer_x, width), share_of(outer_z, width)], axis=0)
    return (
        loss_out.reshape(1),
        pooled[None],
        grad_tokens.reshape(rows_here, length, width),
        grad_w_query,
        b_query,
        grad_w_key,
        grad_w_value,
        b_value,
        grad_w_output,
        b_output,
        gain_attn,
        shift_attn,
        share_of(inner_sums, widening_offset.shape[0]),
        vector_sums[8 * rows :],
        grad_w_outer,
        b_outer,
        gain_ffn,
        shift_ffn,
    )


def solution(mesh):
    return jax.shard_map(
        body,
        mesh=mesh,
        in_specs=(
            P(("gx", "gy"), None, None),
            P(("gx", "gy"), None),
            P(("gx", "gy")),
            P(),
            P(),
            P(),
            P(),
            P(),
            P(),
            P(),
            P(),
            P(),
            P(),
            P(),
            P(),
            P(),
            P(),
            P(),
            P(),
        ),
        out_specs=(
            P(),
            P(("gx", "gy"), None, None),
            P(("gx", "gy"), None, None),
            P("gy", None),
            P("gy"),
            P("gy", None),
            P("gy", None),
            P("gy"),
            P("gy", None),
            P("gy"),
            P("gy"),
            P("gy"),
            P("gy", None),
            P("gy"),
            P("gy", None),
            P("gy"),
            P("gy"),
            P("gy"),
        ),
        check_vma=False,
    )
```

```python
import functools

import jax
import jax.numpy as jnp
import numpy as np
from jax import lax
from jax.experimental import pallas as pl
from jax.experimental.pallas import tpu as pltpu
from jax.sharding import PartitionSpec as P

HEADS = 12
HD = 64
LANES = 128
VMEM_BYTES = 60 * 1024 * 1024
SMALL_BYTES = 24 * 1024 * 1024

EPS_NORM = 1e-12
EPS_UNIT = 1e-06
NEG_FILL = -1e30


def standardize(hidden):
    center = hidden - jnp.mean(hidden, axis=-1, keepdims=True)
    inv_scale = lax.rsqrt(jnp.mean(center * center, axis=-1, keepdims=True) + EPS_NORM)
    return (center * inv_scale, inv_scale)


def standardize_back(normed, inv_scale, grad_normed):
    mean_grad = jnp.mean(grad_normed, axis=-1, keepdims=True)
    mean_both = jnp.mean(grad_normed * normed, axis=-1, keepdims=True)
    return inv_scale * (grad_normed - mean_grad - normed * mean_both)


def widen(value):
    return value.astype(jnp.float32)


def powers_below(count):
    bits = []
    bit = 1
    while bit < count:
        bits.append(bit)
        bit *= 2
    return bits


def place_masks(bits):
    masks = [0]
    for bit in reversed(bits):
        masks = masks + [mask ^ bit for mask in masks]
    return masks


def swap_with(value, axis, bit):
    count = lax.axis_size(axis)
    return lax.ppermute(value, axis, [(i, i ^ bit) for i in range(count)])


def tie(*values):
    return lax.optimization_barrier(values)


def gather_steps():
    gy = powers_below(lax.axis_size("gy"))
    far = [("gy", bit) for bit in reversed(gy[2:])]
    near = [("gy", bit) for bit in reversed(gy[:2])]
    return far + [("gx", bit) for bit in powers_below(lax.axis_size("gx"))] + near


def gather_blocks(block, beside):
    groups_y = lax.axis_size("gy")
    devices = groups_y * lax.axis_size("gx")
    steps = gather_steps()
    numbers = [bit * (groups_y if axis == "gx" else 1) for axis, bit in steps]
    groups = [numbers[at : min(at + 2, len(steps) - 1)] for at in range(0, len(steps) - 1, 2)]
    groups.append(numbers[-1:])
    gathered = block[None]
    number = np.zeros((1,), np.int32)
    for group, bits in enumerate(groups):
        if group == 2:
            gathered, beside = tie(gathered, beside)
        masks = [0]
        for bit in bits:
            masks = masks + [mask ^ bit for mask in masks]
        parts = [gathered] + [
            lax.ppermute(gathered, ("gx", "gy"), [(i, i ^ mask) for i in range(devices)])
            for mask in masks[1:]
        ]
        gathered = jnp.concatenate(parts, axis=0)
        number = np.concatenate([number + mask for mask in masks])
    place = 0
    for step, (axis, bit) in enumerate(steps):
        place = place + jnp.where((lax.axis_index(axis) & bit) != 0, 1 << step, 0)
    return gathered, number, place, beside


def share_of(blocks, columns):
    tiles = columns // LANES
    count, rows, _ = blocks.shape
    parts = count // tiles
    view = blocks.reshape(tiles, parts, rows, LANES)
    return view.transpose(1, 2, 0, 3).reshape(parts * rows, columns)


def compiler_params(limit=VMEM_BYTES):
    return pltpu.CompilerParams(vmem_limit_bytes=limit)


def dot_nt(left, right):
    return lax.dot_general(
        left, right, (((1,), (1,)), ((), ())), preferred_element_type=jnp.float32
    )


def dot_nn(left, right):
    return jnp.dot(left, right, preferred_element_type=jnp.float32)


def start_all(copies):
    for copy in copies:
        copy.start()


def wait_all(copies):
    for copy in copies:
        copy.wait()


def as_row(ref):
    return ref[...].astype(jnp.float32).reshape(1, ref.shape[0])


def lengths_as_row(sizes_ref, lanes, segments):
    lane = lax.broadcasted_iota(jnp.int32, (1, lanes), 1) % segments
    start = jnp.zeros((1, lanes), jnp.int32)
    end = jnp.zeros((1, lanes), jnp.int32)
    at = jnp.int32(0)
    for segment in range(segments):
        size = sizes_ref[0, segment]
        start = jnp.where(lane == segment, at, start)
        at = at + size
        end = jnp.where(lane == segment, at, end)
    return start, end


def counts_as_column(sizes_ref, segments):
    row = lax.broadcasted_iota(jnp.int32, (segments, 1), 0)
    counts = jnp.zeros((segments, 1), jnp.float32)
    for segment in range(segments):
        counts = jnp.where(row == segment, sizes_ref[0, segment].astype(jnp.float32), counts)
    return counts


def starts_as_column(sizes_ref, segments):
    row = lax.broadcasted_iota(jnp.int32, (segments, 1), 0)
    start = jnp.zeros((segments, 1), jnp.int32)
    end = jnp.zeros((segments, 1), jnp.int32)
    at = jnp.int32(0)
    for segment in range(segments):
        size = sizes_ref[0, segment]
        start = jnp.where(row == segment, at, start)
        at = at + size
        end = jnp.where(row == segment, at, end)
    return start, end


def band(length):
    return [(0, length // 2, 0, 3 * length // 4), (length // 2, length, length // 4, length)]


def mask_of(sizes_ref, segments, query_at, query_end, key_at, key_end):
    query = query_at + lax.broadcasted_iota(jnp.int32, (1, query_end - query_at), 1)
    low = jnp.zeros_like(query)
    high = jnp.zeros_like(query)
    at = jnp.int32(0)
    for segment in range(segments):
        end = at + sizes_ref[0, segment]
        inside = (query >= at) & (query < end)
        low = jnp.where(inside, at, low)
        high = jnp.where(inside, end, high)
        at = end
    padding = query >= at
    low = jnp.where(padding, at, low)
    high = jnp.where(padding, key_end, high)
    key = key_at + lax.broadcasted_iota(jnp.int32, (key_end - key_at, query_end - query_at), 0)
    return jnp.where((key >= low) & (key < high), 0.0, NEG_FILL)


def got_spec():
    return pl.BlockSpec(memory_space=pl.ANY)


def vmem_spec():
    return pl.BlockSpec(memory_space=pltpu.VMEM)


def smem_spec():
    return pl.BlockSpec(memory_space=pltpu.SMEM)


def any_spec():
    return pl.BlockSpec(memory_space=pltpu.HBM)


def cost(microseconds):
    return pl.CostEstimate(
        flops=int(microseconds * 1.1e9), bytes_accessed=1000000, transcendentals=0
    )


def forward_kernel(segments, masks_x, masks_z, here_ref, sizes_ref, matching_ref, *refs):
    given, refs = refs[:16], refs[16:]
    results, refs = refs[:14], refs[14:]
    side_own, side_send = results[-2:]
    local, refs = refs[:16], refs[16:]
    made, refs = refs[:12], refs[12:]
    (
        tokens_ref,
        question_w,
        lookup_w,
        content_w,
        mixing_w,
        widening_w,
        narrowing_w,
        question_row,
        content_row,
        mixing_row,
        gain_one_row,
        shift_one_row,
        widening_row,
        narrowing_row,
        gain_two_row,
        shift_two_row,
    ) = local
    (
        query_ref,
        key_ref,
        key_t_ref,
        value_ref,
        lse_ref,
        normed_one_ref,
        inv_one_ref,
        slope_ref,
        normed_two_ref,
        inv_two_ref,
        pooled_ref,
        message_ref,
    ) = made
    value_t, token_t, attn_t, out_one_t, inner_t, fill = refs[:6]
    out_one, out_one_low, total, in_sems, out_sems, side_sems = refs[6:]
    length, width = tokens_ref.shape
    hidden_units = widening_w.shape[1]
    here = here_ref[0]
    share_rows = side_own.shape[1] // (hidden_units // width + 3)
    inner_rows = hidden_units // width * share_rows
    first_rows = inner_rows // 2
    copies = [
        pltpu.make_async_copy(source, target, in_sems.at[i])
        for i, (source, target) in enumerate(zip(given, local))
    ]
    outward = [
        pltpu.make_async_copy(source, target, out_sems.at[i])
        for i, (source, target) in enumerate(zip(made, results))
    ]
    side_copies = []

    def send_side(source, source_rows, offset, count, at, masks):
        for place, mask in enumerate(masks):
            for flip, target in enumerate((side_own, side_send)):
                share = jnp.bitwise_xor(here, mask ^ flip)
                first = pl.multiple_of(share * source_rows + offset, 8)
                copy = pltpu.make_async_copy(
                    source.at[pl.ds(first, count)],
                    target.at[place, pl.ds(at, count)],
                    side_sems.at[len(side_copies)],
                )
                copy.start()
                side_copies.append(copy)

    start_all(copies[:2] + copies[7:] + copies[2:4])
    ranges = band(length)
    for i, (query_at, query_end, key_at, key_end) in enumerate(ranges):
        fill[i] = mask_of(sizes_ref, segments, query_at, query_end, key_at, key_end)
    wait_all(copies[:2] + copies[7:])
    start_all(copies[4:7])
    product = dot_nn(tokens_ref[...], question_w[...]) + as_row(question_row)
    query_ref[...] = product.astype(jnp.bfloat16) * jnp.bfloat16(HD ** (-0.5))
    token_t[...] = tokens_ref[...].T
    copies[2].wait()
    product = dot_nn(tokens_ref[...], lookup_w[...]).astype(jnp.bfloat16)
    key_ref[...] = product
    key_t_ref[...] = product.T
    copies[3].wait()
    product = (dot_nn(tokens_ref[...], content_w[...]) + as_row(content_row)).astype(jnp.bfloat16)
    value_ref[...] = product
    value_t[...] = product.T
    start_all(outward[:4])
    send_side(token_t, share_rows, 0, share_rows, inner_rows + share_rows, masks_x)
    lane = lax.broadcasted_iota(jnp.int32, (1, LANES), 1)
    units = [(at, i) for at in range(HEADS) for i in range(len(ranges))]

    def scores_of(unit):
        at, i = unit
        query_at, query_end, key_at, key_end = ranges[i]
        first = at * HD // LANES * LANES
        lanes = slice(first, first + LANES)
        which = (at * HD - first) // HD
        query = jnp.where((lane // HD) == which, query_ref[query_at:query_end, lanes], 0)
        return dot_nt(key_ref[key_at:key_end, lanes], query) + fill[i]

    def attend(unit, scores):
        at, i = unit
        query_at, query_end, key_at, key_end = ranges[i]
        top = jnp.max(scores, axis=0, keepdims=True)
        expo = jnp.exp(scores - top)
        norm = jnp.sum(expo, axis=0, keepdims=True)
        probs = (expo * (1.0 / norm)).astype(jnp.bfloat16)
        lse_ref[at // 4, at % 4 : at % 4 + 1, query_at:query_end] = top + jnp.log(norm)
        mixed = dot_nn(value_t[at * HD : (at + 1) * HD, key_at:key_end], probs)
        attn_t[at * HD : (at + 1) * HD, query_at:query_end] = mixed.astype(jnp.bfloat16)

    ahead = 4
    waiting = [scores_of(unit) for unit in units[:ahead]]
    for n, unit in enumerate(units):
        if n + ahead < len(units):
            waiting.append(scores_of(units[n + ahead]))
        attend(unit, waiting.pop(0))
    outward[4].start()
    send_side(attn_t, share_rows, 0, share_rows, inner_rows + 2 * share_rows, masks_x)
    copies[4].wait()
    chunk = min(length, 128)
    for at in range(0, length, chunk):
        rows = slice(at, at + chunk)
        hidden = (
            tokens_ref[rows].astype(jnp.float32)
            + dot_nn(attn_t[:, rows].T, mixing_w[...])
            + as_row(mixing_row)
        )
        normed, inv = standardize(hidden)
        normed_one_ref[rows] = normed
        inv_one_ref[rows] = inv
        shifted = normed * as_row(gain_one_row) + as_row(shift_one_row)
        out_one[rows] = shifted
        low = shifted.astype(jnp.bfloat16)
        out_one_low[rows] = low
        out_one_t[:, rows] = low.T
        total[rows] = shifted + as_row(narrowing_row)
    start_all(outward[5:7])
    send_side(out_one_t, share_rows, 0, share_rows, inner_rows, masks_x)
    copies[5].wait()
    copies[6].wait()
    tile = hidden_units // 4
    taller = min(length, 256)
    units = [(at, row) for at in range(0, hidden_units, tile) for row in range(0, length, taller)]

    def widened(unit):
        at, row = unit
        return dot_nn(out_one_low[row : row + taller], widening_w[:, at : at + tile])

    def activate(unit, before):
        at, row = unit
        rows = slice(row, row + taller)
        before = before + widening_row[at : at + tile].astype(jnp.float32).reshape(1, tile)
        cdf = 0.5 * (1.0 + lax.erf(before * 0.7071067811865476))
        pdf = jnp.exp(-0.5 * before * before) * 0.3989422804014327
        inner = (before * cdf).astype(jnp.bfloat16)
        slope_ref[rows, at : at + tile] = (cdf + before * pdf).astype(jnp.bfloat16)
        inner_t[at : at + tile, rows] = inner.T
        total[rows] += dot_nn(inner, narrowing_w[at : at + tile, :])

    ahead = 1
    waiting = [widened(unit) for unit in units[:ahead]]
    for n, unit in enumerate(units):
        if n + ahead < len(units):
            waiting.append(widened(units[n + ahead]))
        activate(unit, waiting.pop(0))
    outward[7].start()
    send_side(inner_t, inner_rows, 0, first_rows, 0, masks_x)
    send_side(inner_t, inner_rows, first_rows, inner_rows - first_rows, first_rows, masks_z)
    start, end = starts_as_column(sizes_ref, segments)
    sums = jnp.zeros((segments, width), jnp.float32)
    for at in range(0, length, chunk):
        rows = slice(at, at + chunk)
        normed, inv = standardize(total[rows])
        normed_two_ref[rows] = normed
        inv_two_ref[rows] = inv
        out_two = normed * as_row(gain_two_row) + as_row(shift_two_row)
        upper = out_two.astype(jnp.bfloat16)
        lower = (out_two - upper.astype(jnp.float32)).astype(jnp.bfloat16)
        token = at + lax.broadcasted_iota(jnp.int32, (segments, chunk), 1)
        member = jnp.where((token >= start) & (token < end), 1.0, 0.0).astype(jnp.bfloat16)
        sums = sums + dot_nn(member, upper) + dot_nn(member, lower)
    pooled = sums / counts_as_column(sizes_ref, segments)
    pooled_ref[...] = pooled
    inv_norm = lax.rsqrt(jnp.sum(pooled * pooled, axis=1, keepdims=True) + EPS_UNIT)
    units = (pooled * inv_norm).astype(jnp.bfloat16)
    half = segments // 2
    place = lax.broadcasted_iota(jnp.int32, (segments, segments), 0)
    source = lax.broadcasted_iota(jnp.int32, (segments, segments), 1)
    wanted = jnp.where(place < half, 2 * place, 2 * (place - half) + 1)
    pick = jnp.where(source == wanted, 1.0, 0.0).astype(jnp.bfloat16)
    message_ref[:, :width] = dot_nn(pick, units).astype(jnp.bfloat16)
    row = lax.broadcasted_iota(jnp.int32, (segments, LANES), 0)
    column = lax.broadcasted_iota(jnp.int32, (segments, LANES), 1)
    digits = jnp.zeros((segments, LANES), jnp.float32)
    for i in range(half):
        number = matching_ref[i]
        digit = jnp.where(column == 0, number & 255, number >> 8).astype(jnp.float32)
        digits = jnp.where((row == i) & (column < 2), digit, digits)
    message_ref[:, width:] = digits.astype(jnp.bfloat16)
    start_all(outward[8:])
    wait_all(outward)
    wait_all(side_copies)


def forward_step(here, sizes, matching, masks_x, masks_z, given):
    tokens, hidden_units = given[0], given[5].shape[1]
    length, width = tokens.shape
    segments = sizes.shape[1]
    half = len(masks_x)
    query_at, query_end, key_at, key_end = band(length)[0]
    low, full = jnp.bfloat16, jnp.float32
    side = ((half, (hidden_units // width + 3) * (width // half // 2), length), low)
    made = [
        ((length, width), low),
        ((length, width), low),
        ((width, length), low),
        ((length, width), low),
        ((HEADS // 4, 4, length), full),
        ((length, width), full),
        ((length, 1), full),
        ((length, hidden_units), low),
        ((length, width), full),
        ((length, 1), full),
        ((segments, width), full),
        ((segments, width + LANES), low),
    ]
    return pl.pallas_call(
        functools.partial(forward_kernel, segments, masks_x, masks_z),
        in_specs=[smem_spec()] * 3 + [any_spec()] * len(given),
        out_specs=[any_spec()] * (len(made) + 2),
        out_shape=[jax.ShapeDtypeStruct(shape, kind) for shape, kind in made + [side, side]],
        scratch_shapes=[pltpu.VMEM(item.shape, item.dtype) for item in given]
        + [pltpu.VMEM(shape, kind) for shape, kind in made]
        + [
            pltpu.VMEM((width, length), low),
            pltpu.VMEM((width, length), low),
            pltpu.VMEM((width, length), low),
            pltpu.VMEM((width, length), low),
            pltpu.VMEM((hidden_units, length), low),
            pltpu.VMEM((2, key_end - key_at, query_end - query_at), full),
            pltpu.VMEM((length, width), full),
            pltpu.VMEM((length, width), low),
            pltpu.VMEM((length, width), full),
            pltpu.SemaphoreType.DMA((len(given),)),
            pltpu.SemaphoreType.DMA((len(made),)),
            pltpu.SemaphoreType.DMA((2 * 5 * half,)),
        ],
        compiler_params=compiler_params(),
        cost_estimate=cost(28),
        name="forward_step",
    )(here, sizes, matching, *given)


def loss_kernel(
    place_ref,
    sizes_ref,
    sharpness_ref,
    numbers_ref,
    gathered_hbm,
    pooled_hbm,
    normed_hbm,
    inv_hbm,
    gain_hbm,
    loss_ref,
    grad_hidden_hbm,
    grad_branch_hbm,
    sums_ref,
    gathered_ref,
    pooled_ref,
    normed_ref,
    inv_ref,
    gain_ref,
    grad_hidden_ref,
    grad_branch_ref,
    sems,
):
    given = [
        (gathered_hbm, gathered_ref),
        (pooled_hbm, pooled_ref),
        (normed_hbm, normed_ref),
        (inv_hbm, inv_ref),
        (gain_hbm, gain_ref),
    ]
    copies = [
        pltpu.make_async_copy(source, target, sems.at[i])
        for i, (source, target) in enumerate(given)
    ]
    start_all(copies)
    segments, width = pooled_ref.shape
    half = segments // 2
    devices = gathered_ref.shape[0]
    total = devices * half
    sharpness = sharpness_ref[0]
    row = lax.broadcasted_iota(jnp.int32, (total, devices * segments), 0)
    column = lax.broadcasted_iota(jnp.int32, (total, devices * segments), 1)
    source = jnp.bitwise_xor(row // half, place_ref[0]) * segments + row % half
    copies[0].wait()
    gathered = gathered_ref[...].reshape(devices * segments, width + LANES)
    pick = jnp.where(column == source, 1.0, 0.0).astype(jnp.bfloat16)
    picked = dot_nn(pick, gathered)
    questions = picked[:, :width].astype(jnp.bfloat16)
    digits = picked[:, width:]
    pick = jnp.where(column == source + half, 1.0, 0.0).astype(jnp.bfloat16)
    passages = dot_nn(pick, gathered[:, :width]).astype(jnp.bfloat16)
    matching = (digits[:, 0:1] + 256.0 * digits[:, 1:2]).astype(jnp.int32)
    table = dot_nt(questions, passages) / sharpness
    top = jnp.max(table, axis=1, keepdims=True)
    expo = jnp.exp(table - top)
    expo_total = jnp.sum(expo, axis=1, keepdims=True)
    chosen = matching == numbers_ref[...]
    positive = jnp.sum(jnp.where(chosen, table, 0.0), axis=1, keepdims=True)
    loss_ref[...] = (
        jnp.sum(top + jnp.log(expo_total) - positive, axis=0, keepdims=True) / total
    )
    slope = (expo / expo_total - chosen.astype(jnp.float32)) / total
    grad_dot = (slope / sharpness).astype(jnp.bfloat16)
    segment_at = lax.broadcasted_iota(jnp.int32, (segments, total), 0)
    column = lax.broadcasted_iota(jnp.int32, (segments, total), 1)
    mine = column == place_ref[0] * half + segment_at // 2
    is_query = segment_at % 2 == 0
    pick_query = jnp.where(mine & is_query, 1.0, 0.0).astype(jnp.bfloat16)
    pick_passage = jnp.where(mine & ~is_query, 1.0, 0.0).astype(jnp.bfloat16)
    row_terms = dot_nn(pick_query, grad_dot).astype(jnp.bfloat16)
    column_terms = dot_nt(pick_passage, grad_dot).astype(jnp.bfloat16)
    grad_units = dot_nn(row_terms, passages) + dot_nn(column_terms, questions)
    wait_all(copies[1:])
    pooled = pooled_ref[...]
    inv_norm = lax.rsqrt(jnp.sum(pooled * pooled, axis=1, keepdims=True) + EPS_UNIT)
    units = pooled * inv_norm
    along = jnp.sum(units * grad_units, axis=1, keepdims=True)
    grad_pooled = inv_norm * (grad_units - units * along) / counts_as_column(sizes_ref, segments)
    upper = grad_pooled.astype(jnp.bfloat16)
    lower = (grad_pooled - upper.astype(jnp.float32)).astype(jnp.bfloat16)
    both = jnp.concatenate([upper, lower], axis=0)
    start, end = lengths_as_row(sizes_ref, 2 * segments, segments)
    gain = as_row(gain_ref)
    outward = []
    tokens = normed_ref.shape[0]
    chunk = min(tokens, 128)
    gain_sum = jnp.zeros((1, width), jnp.float32)
    shift_sum = jnp.zeros((1, width), jnp.float32)
    bias_sum = jnp.zeros((1, width), jnp.float32)
    for at in range(0, tokens, chunk):
        token = at + lax.broadcasted_iota(jnp.int32, (chunk, 2 * segments), 0)
        member = jnp.where((token >= start) & (token < end), 1.0, 0.0).astype(jnp.bfloat16)
        grad_out = dot_nn(member, both)
        normed = normed_ref[at : at + chunk]
        gain_sum = gain_sum + jnp.sum(grad_out * normed, axis=0, keepdims=True)
        shift_sum = shift_sum + jnp.sum(grad_out, axis=0, keepdims=True)
        grad_hidden = standardize_back(normed, inv_ref[at : at + chunk], grad_out * gain)
        grad_hidden_ref[at : at + chunk] = grad_hidden
        low = grad_hidden.astype(jnp.bfloat16)
        grad_branch_ref[at : at + chunk] = low
        bias_sum = bias_sum + jnp.sum(low.astype(jnp.float32), axis=0, keepdims=True)
        for source_ref, target in (
            (grad_hidden_ref, grad_hidden_hbm),
            (grad_branch_ref, grad_branch_hbm),
        ):
            copy = pltpu.make_async_copy(
                source_ref.at[at : at + chunk],
                target.at[at : at + chunk],
                sems.at[len(copies) + len(outward)],
            )
            copy.start()
            outward.append(copy)
    sums_ref[...] = jnp.concatenate([bias_sum, gain_sum, shift_sum], axis=0)
    wait_all(outward)


def loss_step(place, sizes, sharpness, numbers, gathered, pooled, normed, inv, gain):
    tokens, width = normed.shape
    low, full = jnp.bfloat16, jnp.float32
    chunks = -(-tokens // 128)
    return pl.pallas_call(
        loss_kernel,
        in_specs=[smem_spec()] * 3 + [vmem_spec()] + [any_spec()] * 5,
        out_specs=[vmem_spec(), any_spec(), any_spec(), vmem_spec()],
        out_shape=[
            jax.ShapeDtypeStruct((1, 1), full),
            jax.ShapeDtypeStruct((tokens, width), full),
            jax.ShapeDtypeStruct((tokens, width), low),
            jax.ShapeDtypeStruct((3, width), full),
        ],
        scratch_shapes=[
            pltpu.VMEM(gathered.shape, low),
            pltpu.VMEM(pooled.shape, full),
            pltpu.VMEM(normed.shape, full),
            pltpu.VMEM(inv.shape, full),
            pltpu.VMEM(gain.shape, low),
            pltpu.VMEM((tokens, width), full),
            pltpu.VMEM((tokens, width), low),
            pltpu.SemaphoreType.DMA((5 + 2 * chunks,)),
        ],
        compiler_params=compiler_params(),
        cost_estimate=cost(4),
        name="loss_step",
    )(place, sizes, sharpness, numbers, gathered, pooled, normed, inv, gain)


def before_kernel(
    branch_hbm,
    slope_hbm,
    narrowing_hbm,
    widening_hbm,
    hidden_hbm,
    normed_hbm,
    inv_hbm,
    gain_hbm,
    mixing_hbm,
    grad_pre_hbm,
    bias_ref,
    grad_hidden_hbm,
    grad_branch_hbm,
    grad_attn_hbm,
    sums_ref,
    branch_ref,
    slope_ref,
    narrowing_ref,
    widening_ref,
    total,
    normed_ref,
    inv_ref,
    gain_ref,
    mixing_ref,
    grad_pre_ref,
    grad_hidden_ref,
    grad_branch_ref,
    grad_attn_ref,
    in_sems,
    part_sems,
    out_sems,
):
    tokens, width = branch_ref.shape
    parts = slope_ref.shape[1] // width
    given = [
        (branch_hbm, branch_ref),
        (hidden_hbm, total),
        (normed_hbm, normed_ref),
        (inv_hbm, inv_ref),
        (gain_hbm, gain_ref),
        (mixing_hbm, mixing_ref),
    ]
    copies = [
        pltpu.make_async_copy(source, target, in_sems.at[i])
        for i, (source, target) in enumerate(given)
    ]
    part_copies = []
    for part in range(parts):
        at = pl.ds(part * width, width)
        pairs = [
            (narrowing_hbm.at[at], narrowing_ref.at[at]),
            (slope_hbm.at[:, at], slope_ref.at[:, at]),
            (widening_hbm.at[:, at], widening_ref.at[:, at]),
        ]
        part_copies.append(
            [
                pltpu.make_async_copy(source, target, part_sems.at[part, i])
                for i, (source, target) in enumerate(pairs)
            ]
        )
    start_all(copies[:1] + part_copies[0] + part_copies[1] + copies[1:2])
    outward = []

    def write(source, target):
        copy = pltpu.make_async_copy(source, target, out_sems.at[len(outward)])
        copy.start()
        outward.append(copy)

    def columns_of(part):
        return slice(part * width, (part + 1) * width)

    def product(part):
        return dot_nt(branch_ref[...], narrowing_ref[columns_of(part)])

    wait_all(copies[:1] + part_copies[0][:1])
    waiting = product(0)
    for part in range(parts):
        if part + 2 < parts:
            start_all(part_copies[part + 2])
        elif part + 2 == parts:
            start_all(copies[2:])
        if part == 0:
            wait_all(copies[1:2])
        wait_all(part_copies[part][1:])
        grad_act = waiting
        if part + 1 < parts:
            wait_all(part_copies[part + 1][:1])
            waiting = product(part + 1)
        columns = columns_of(part)
        grad_pre = (grad_act * widen(slope_ref[:, columns])).astype(jnp.bfloat16)
        grad_pre_ref[:, columns] = grad_pre
        bias_ref[:, columns] = jnp.sum(widen(grad_pre), axis=0, keepdims=True)
        total[...] += dot_nt(grad_pre, widening_ref[:, columns])
        at = pl.ds(part * width, width)
        write(grad_pre_ref.at[:, at], grad_pre_hbm.at[:, at])
    wait_all(copies[2:])
    chunk = min(tokens, 128)
    gain = as_row(gain_ref)
    gain_sum = jnp.zeros((1, width), jnp.float32)
    shift_sum = jnp.zeros((1, width), jnp.float32)
    bias_sum = jnp.zeros((1, width), jnp.float32)
    for row in range(0, tokens, chunk):
        grad_out = total[row : row + chunk]
        normed = normed_ref[row : row + chunk]
        gain_sum = gain_sum + jnp.sum(grad_out * normed, axis=0, keepdims=True)
        shift_sum = shift_sum + jnp.sum(grad_out, axis=0, keepdims=True)
        grad_hidden = standardize_back(normed, inv_ref[row : row + chunk], grad_out * gain)
        grad_hidden_ref[row : row + chunk] = grad_hidden
        low = grad_hidden.astype(jnp.bfloat16)
        grad_branch_ref[row : row + chunk] = low
        bias_sum = bias_sum + jnp.sum(widen(low), axis=0, keepdims=True)
        grad_attn_ref[row : row + chunk] = dot_nt(low, mixing_ref[...]).astype(jnp.bfloat16)
    write(grad_branch_ref, grad_branch_hbm)
    write(grad_attn_ref, grad_attn_hbm)
    write(grad_hidden_ref, grad_hidden_hbm)
    sums_ref[...] = jnp.concatenate([bias_sum, gain_sum, shift_sum], axis=0)
    wait_all(outward)


def before_step(branch, slope, narrowing, widening, hidden, normed, inv, gain, mixing):
    tokens, hidden_units = slope.shape
    width = branch.shape[1]
    parts = hidden_units // width
    low, full = jnp.bfloat16, jnp.float32
    return pl.pallas_call(
        before_kernel,
        in_specs=[any_spec()] * 9,
        out_specs=[any_spec(), vmem_spec()] + [any_spec()] * 3 + [vmem_spec()],
        out_shape=[
            jax.ShapeDtypeStruct((tokens, hidden_units), low),
            jax.ShapeDtypeStruct((1, hidden_units), full),
            jax.ShapeDtypeStruct((tokens, width), full),
            jax.ShapeDtypeStruct((tokens, width), low),
            jax.ShapeDtypeStruct((tokens, width), low),
            jax.ShapeDtypeStruct((3, width), full),
        ],
        scratch_shapes=[
            pltpu.VMEM(branch.shape, low),
            pltpu.VMEM(slope.shape, low),
            pltpu.VMEM(narrowing.shape, low),
            pltpu.VMEM(widening.shape, low),
            pltpu.VMEM((tokens, width), full),
            pltpu.VMEM(normed.shape, full),
            pltpu.VMEM(inv.shape, full),
            pltpu.VMEM(gain.shape, low),
            pltpu.VMEM(mixing.shape, low),
            pltpu.VMEM(slope.shape, low),
            pltpu.VMEM((tokens, width), full),
            pltpu.VMEM((tokens, width), low),
            pltpu.VMEM((tokens, width), low),
            pltpu.SemaphoreType.DMA((6,)),
            pltpu.SemaphoreType.DMA((parts, 3)),
            pltpu.SemaphoreType.DMA((parts + 3,)),
        ],
        compiler_params=compiler_params(),
        cost_estimate=cost(11),
        name="before_step",
    )(branch, slope, narrowing, widening, hidden, normed, inv, gain, mixing)


def side_copies(own_ref, other_ref, at, count, target, sems):
    tokens = own_ref.shape[2]
    return [
        pltpu.make_async_copy(
            source.at[:, pl.ds(at, count)],
            target.at[:, :, pl.ds(i * tokens, tokens)],
            sems.at[i],
        )
        for i, source in enumerate((own_ref, other_ref))
    ]


def flat(ref):
    places, rows, tokens = ref.shape
    return ref[...].reshape(places * rows, tokens)


def store_places(product, first, parts, target):
    rows = target.shape[2]
    low = product.astype(jnp.bfloat16)
    for place in range(low.shape[0] // rows // parts):
        for tile in range(low.shape[1] // LANES):
            for part in range(parts):
                row = (place * parts + part) * rows
                target[first + place, tile * parts + part] = low[
                    row : row + rows, tile * LANES : (tile + 1) * LANES
                ]


def outer_kernel(
    own_ref,
    other_ref,
    branch_own_ref,
    branch_other_ref,
    keep_x,
    send_x,
    keep_z,
    send_z,
    left_x,
    left_z,
    right,
    made_x,
    made_z,
    left_sems,
    right_sems,
    out_sems,
):
    places, count, _ = left_x.shape
    tokens = branch_own_ref.shape[0]
    half = places // 2
    parts = count // made_x.shape[2]
    copies = [
        pltpu.make_async_copy(source, right.at[pl.ds(i * tokens, tokens)], right_sems.at[i])
        for i, source in enumerate((branch_own_ref, branch_other_ref))
    ]
    copies_x = side_copies(own_ref, other_ref, 0, count, left_x, left_sems.at[0])
    copies_z = side_copies(own_ref, other_ref, count, count, left_z, left_sems.at[1])
    start_all(copies + copies_x + copies_z)
    wait_all(copies + copies_x)
    units = [
        (left_x, made_x, half, send_x),
        (left_x, made_x, 0, keep_x),
        (left_z, made_z, half, send_z),
        (left_z, made_z, 0, keep_z),
    ]

    def product(n):
        left, _, first, _ = units[n]
        if n == 2:
            wait_all(copies_z)
        return dot_nn(
            left[first : first + half].reshape(half * count, 2 * tokens), right[...]
        )

    outward = []
    waiting = product(0)
    for n, (_, made, first, target) in enumerate(units):
        current = waiting
        if n + 1 < len(units):
            waiting = product(n + 1)
        store_places(current, first, parts, made)
        copy = pltpu.make_async_copy(made.at[pl.ds(first, half)], target, out_sems.at[n])
        copy.start()
        outward.append(copy)
    wait_all(outward)


def outer_step(own, other, branch_own, branch_other, count):
    places, _, tokens = own.shape
    width = branch_own.shape[1]
    parts = 2
    rows = count // parts
    low = jnp.bfloat16
    blocks = width // LANES * parts
    shape = jax.ShapeDtypeStruct((places // 2, blocks, rows, LANES), low)
    return pl.pallas_call(
        outer_kernel,
        in_specs=[any_spec(), got_spec(), any_spec(), got_spec()],
        out_specs=[any_spec()] * 4,
        out_shape=[shape] * 4,
        scratch_shapes=[
            pltpu.VMEM((places, count, 2 * tokens), low),
            pltpu.VMEM((places, count, 2 * tokens), low),
            pltpu.VMEM((2 * tokens, width), low),
            pltpu.VMEM((places, blocks, rows, LANES), low),
            pltpu.VMEM((places, blocks, rows, LANES), low),
            pltpu.SemaphoreType.DMA((2, 2)),
            pltpu.SemaphoreType.DMA((2,)),
            pltpu.SemaphoreType.DMA((4,)),
        ],
        compiler_params=compiler_params(),
        cost_estimate=cost(5),
        name="outer_step",
    )(own, other, branch_own, branch_other)


def inner_kernel(
    at,
    side_ref,
    own_ref,
    other_ref,
    grad_own_hbm,
    grad_other_hbm,
    keep_x,
    send_x,
    keep_y,
    send_y,
    left,
    right,
    made_x,
    made_y,
    left_sems,
    in_sems,
    out_sems,
):
    tokens, hidden_units = grad_own_hbm.shape
    places, rows, _ = left.shape
    half = places // 2
    parts = 4
    width = hidden_units // parts
    tiles = width // LANES
    side = side_ref[0]
    left_copies = side_copies(own_ref, other_ref, at, rows, left, left_sems)
    right_copies = []
    for part in range(parts):
        columns = pl.ds(part * width, width)
        right_copies.append(
            [
                pltpu.make_async_copy(
                    source.at[:, columns],
                    right.at[pl.ds(i * tokens, tokens), columns],
                    in_sems.at[part, i],
                )
                for i, source in enumerate((grad_own_hbm, grad_other_hbm))
            ]
        )
    start_all(left_copies)
    for copies in right_copies:
        start_all(copies)
    outward = []

    def write(source, target):
        copy = pltpu.make_async_copy(source, target, out_sems.at[len(outward)])
        copy.start()
        outward.append(copy)

    def weight(part):
        return dot_nn(flat(left), right[:, part * width : (part + 1) * width])

    def store_weight(part, product):
        low = product.astype(jnp.bfloat16)
        for place in range(places):
            for tile in range(tiles):
                block = low[place * rows : (place + 1) * rows, tile * LANES : (tile + 1) * LANES]
                if part < parts // 2:
                    made_x[place, part * tiles + tile] = block
                else:
                    made_y[jnp.bitwise_xor(side, part - parts // 2), place, tile] = block
        if part == parts // 2 - 1:
            write(made_x.at[pl.ds(half, half)], send_x)
            write(made_x.at[pl.ds(0, half)], keep_x)
        if part == parts - 1:
            write(made_y.at[1], send_y)
            write(made_y.at[0], keep_y)

    wait_all(left_copies)
    products = []
    for part in range(parts):
        wait_all(right_copies[part])
        products.append(weight(part))
        if part >= 1:
            store_weight(part - 1, products.pop(0))
    store_weight(parts - 1, products.pop(0))
    wait_all(outward)


def inner_step(side, own, other, at, rows, grad_own, grad_other):
    places, _, tokens = own.shape
    hidden_units = grad_own.shape[1]
    tiles = hidden_units // 4 // LANES
    half = places // 2
    low = jnp.bfloat16
    shape_x = jax.ShapeDtypeStruct((half, 2 * tiles, rows, LANES), low)
    shape_y = jax.ShapeDtypeStruct((places, tiles, rows, LANES), low)
    return pl.pallas_call(
        functools.partial(inner_kernel, at),
        in_specs=[smem_spec(), any_spec(), got_spec(), any_spec(), got_spec()],
        out_specs=[any_spec()] * 4,
        out_shape=[shape_x, shape_x, shape_y, shape_y],
        scratch_shapes=[
            pltpu.VMEM((places, rows, 2 * tokens), low),
            pltpu.VMEM((2 * tokens, hidden_units), low),
            pltpu.VMEM((places, 2 * tiles, rows, LANES), low),
            pltpu.VMEM((2, places, tiles, rows, LANES), low),
            pltpu.SemaphoreType.DMA((2,)),
            pltpu.SemaphoreType.DMA((4, 2)),
            pltpu.SemaphoreType.DMA((4,)),
        ],
        compiler_params=compiler_params(),
        cost_estimate=cost(5),
        name="inner_step",
    )(side, own, other, grad_own, grad_other)


def attend_back_kernel(
    segments,
    sizes_ref,
    query_ref,
    key_ref,
    key_t_ref,
    value_ref,
    lse_ref,
    grad_ref,
    grads_ref,
    sums_ref,
    fill,
    query_t,
    total_key,
    total_value,
):
    length, wide = query_ref.shape
    ranges = band(length)
    step = pl.program_id(0)

    @pl.when(step == 0)
    def _():
        for i, (query_at, query_end, key_at, key_end) in enumerate(ranges):
            fill[i] = mask_of(sizes_ref, segments, query_at, query_end, key_at, key_end)

    total_key[...] = jnp.zeros_like(total_key)
    total_value[...] = jnp.zeros_like(total_value)
    lane = lax.broadcasted_iota(jnp.int32, (1, LANES), 1)
    units = [(at, i) for at in range(wide // HD) for i in range(len(ranges))]

    def lanes_of(at):
        first = at * HD // LANES * LANES
        return slice(first, first + LANES), (lane // HD) == (at * HD - first) // HD

    def products(unit):
        at, i = unit
        query_at, query_end, key_at, key_end = ranges[i]
        lanes, head = lanes_of(at)
        query = jnp.where(head, query_ref[query_at:query_end, lanes], 0)
        grad = jnp.where(head, grad_ref[query_at:query_end, lanes], 0)
        scores = dot_nt(key_ref[key_at:key_end, lanes], query) + fill[i]
        return scores, dot_nt(value_ref[key_at:key_end, lanes], grad)

    def back(unit, scores, grad_probs):
        at, i = unit
        query_at, query_end, key_at, key_end = ranges[i]
        probs = jnp.exp(scores - lse_ref[0, at : at + 1, query_at:query_end])
        inner = jnp.sum(grad_probs * probs, axis=0, keepdims=True)
        return probs.astype(jnp.bfloat16), (probs * (grad_probs - inner)).astype(jnp.bfloat16)

    def finish(unit, probs, grad_scores):
        at, i = unit
        query_at, query_end, key_at, key_end = ranges[i]
        lanes, head = lanes_of(at)
        query = jnp.where(head, query_ref[query_at:query_end, lanes], 0)
        grad = jnp.where(head, grad_ref[query_at:query_end, lanes], 0)
        total_value[key_at:key_end, lanes] += dot_nn(probs, grad)
        total_key[key_at:key_end, lanes] += dot_nn(grad_scores, query)
        query_t[at * HD : (at + 1) * HD, query_at:query_end] = dot_nn(
            key_t_ref[at * HD : (at + 1) * HD, key_at:key_end], grad_scores
        )

    ahead = 2
    waiting = [products(unit) for unit in units[:ahead]]
    done = []
    for n, unit in enumerate(units):
        if n + ahead < len(units):
            waiting.append(products(units[n + ahead]))
        done.append((unit, *back(unit, *waiting.pop(0))))
        if len(done) > 1:
            finish(*done.pop(0))
    for item in done:
        finish(*item)
    grad_query = (query_t[...] * HD ** (-0.5)).T.astype(jnp.bfloat16)
    grad_value = total_value[...].astype(jnp.bfloat16)
    grads_ref[0] = grad_query
    grads_ref[1] = total_key[...].astype(jnp.bfloat16)
    grads_ref[2] = grad_value
    sums_ref[...] = jnp.concatenate(
        [
            jnp.sum(widen(grad_query), axis=0, keepdims=True),
            jnp.sum(widen(grad_value), axis=0, keepdims=True),
        ],
        axis=0,
    )


def attend_back_step(sizes, query, key, key_t, value, lse, grad):
    tokens, width = query.shape
    heads_here = lse.shape[1]
    wide = heads_here * HD
    columns = pl.BlockSpec((tokens, wide), lambda i: (0, i))
    query_at, query_end, key_at, key_end = band(tokens)[0]
    return pl.pallas_call(
        functools.partial(attend_back_kernel, sizes.shape[1]),
        grid=(width // wide,),
        in_specs=[
            smem_spec(),
            columns,
            columns,
            pl.BlockSpec((wide, tokens), lambda i: (i, 0)),
            columns,
            pl.BlockSpec((1, heads_here, tokens), lambda i: (i, 0, 0)),
            columns,
        ],
        out_specs=[
            pl.BlockSpec((3, tokens, wide), lambda i: (0, 0, i)),
            pl.BlockSpec((2, wide), lambda i: (0, i)),
        ],
        out_shape=[
            jax.ShapeDtypeStruct((3, tokens, width), jnp.bfloat16),
            jax.ShapeDtypeStruct((2, width), jnp.float32),
        ],
        scratch_shapes=[
            pltpu.VMEM((2, key_end - key_at, query_end - query_at), jnp.float32),
            pltpu.VMEM((wide, tokens), jnp.float32),
            pltpu.VMEM((tokens, wide), jnp.float32),
            pltpu.VMEM((tokens, wide), jnp.float32),
        ],
        compiler_params=compiler_params(),
        cost_estimate=cost(8),
        name="attend_back_step",
    )(sizes, query, key, key_t, value, lse, grad)


def add_kernel(shape_of, *refs):
    counts, last = shape_of
    pairs = sum(counts) + last
    given, refs = refs[: 2 * pairs], refs[2 * pairs :]
    outputs = 2 * len(counts) + (1 if last else 0)
    targets, refs = refs[:outputs], refs[outputs:]
    local, refs = refs[: 2 * pairs], refs[2 * pairs :]
    made, refs = refs[:outputs], refs[outputs:]
    in_sems, out_sems = refs
    copies = [
        pltpu.make_async_copy(source, target, in_sems.at[n])
        for n, (source, target) in enumerate(zip(given, local))
    ]
    start_all(copies)
    outward = []

    def write(n):
        copy = pltpu.make_async_copy(made[n], targets[n], out_sems.at[n])
        copy.start()
        outward.append(copy)

    at = 0
    for item, count in enumerate(counts):
        kept, sent = made[2 * item], made[2 * item + 1]
        half = kept.shape[0]
        block = 0
        for _ in range(count):
            wait_all(copies[2 * at : 2 * at + 2])
            keep, got = local[2 * at], local[2 * at + 1]
            blocks = slice(block, block + keep.shape[1])
            sent[:, blocks] = (widen(keep[half:]) + widen(got[half:])).astype(sent.dtype)
            kept[:, blocks] = widen(keep[:half]) + widen(got[:half])
            block += keep.shape[1]
            at += 1
        write(2 * item + 1)
        write(2 * item)
    if last:
        mine = made[-1]
        block = 0
        for _ in range(last):
            wait_all(copies[2 * at : 2 * at + 2])
            keep, got = local[2 * at], local[2 * at + 1]
            blocks = slice(block, block + keep.shape[1])
            mine[blocks] = (widen(keep[0]) + widen(got[0])).astype(mine.dtype)
            block += keep.shape[1]
            at += 1
        write(outputs - 1)
    wait_all(outward)


def add_step(items, last=(), name="add_step"):
    given, shapes = [], []
    for pairs in items:
        for pair in pairs:
            given.extend(pair)
        places, _, rows, lanes = pairs[0][0].shape
        blocks = sum(keep.shape[1] for keep, _ in pairs)
        shape = (places // 2, blocks, rows, lanes)
        shapes.append((shape, jnp.float32))
        shapes.append((shape, pairs[0][1].dtype))
    for pair in last:
        given.extend(pair)
    if last:
        _, _, rows, lanes = last[0][0].shape
        blocks = sum(keep.shape[1] for keep, _ in last)
        shapes.append(((blocks, rows, lanes), jnp.bfloat16))
    results = pl.pallas_call(
        functools.partial(add_kernel, ([len(pairs) for pairs in items], len(last))),
        in_specs=[got_spec()] * len(given),
        out_specs=[any_spec()] * len(shapes),
        out_shape=[jax.ShapeDtypeStruct(shape, kind) for shape, kind in shapes],
        scratch_shapes=[pltpu.VMEM(item.shape, item.dtype) for item in given]
        + [pltpu.VMEM(shape, kind) for shape, kind in shapes]
        + [pltpu.SemaphoreType.DMA((len(given),)), pltpu.SemaphoreType.DMA((len(shapes),))],
        compiler_params=compiler_params(SMALL_BYTES),
        cost_estimate=cost(2),
        name=name,
    )(*given)
    halves = [(results[2 * n], results[2 * n + 1]) for n in range(len(items))]
    return halves + ([results[-1]] if last else [])


def split_vector(total, rows):
    places, _, count, lanes = total.shape
    parts = []
    for _ in range(3):
        low = total.astype(jnp.bfloat16)
        total = total - widen(low)
        parts.append(low)
    if rows > 3 * count:
        parts.append(jnp.zeros((places, 1, rows - 3 * count, lanes), jnp.bfloat16))
    return jnp.concatenate(parts, axis=2)


def join_vector(block, count):
    return sum(widen(block[..., i * count : (i + 1) * count, :]) for i in range(3))


def round_kernel(plan, passes, inputs, streams, *refs):
    given, refs = refs[:inputs], refs[inputs:]
    outputs = len(plan) - sum(1 for item in plan if item[5]) + streams
    targets, refs = refs[:outputs], refs[outputs:]
    local, refs = refs[:inputs], refs[inputs:]
    made, (in_sems, out_sems) = refs[:outputs], refs[outputs:]
    sent_to = made[outputs - streams :]
    copies = []
    passed = {}
    for n, source in enumerate(given):
        if n in passes:
            stream, at = passes[n]
            target = sent_to[stream].at[pl.ds(at, source.shape[0])]
            passed.setdefault(stream, []).append(n)
        else:
            target = local[n]
        copies.append(pltpu.make_async_copy(source, target, in_sems.at[n]))
    start_all(copies)
    outward = []
    waited = set()

    def write(n):
        copy = pltpu.make_async_copy(made[n], targets[n], out_sems.at[n])
        copy.start()
        outward.append(copy)

    def need(n):
        if n not in waited:
            waited.add(n)
            copies[n].wait()

    kept_at = 0
    for keep_at, got_at, begin, stream, at, whole, vector in plan:
        keep = local[keep_at]
        places, blocks, rows, lanes = keep.shape
        need(keep_at)
        if got_at is not None:
            need(got_at)
        total = widen(keep[...])
        if vector and keep.dtype == jnp.bfloat16:
            total = join_vector(keep[...], 8)
        if got_at is not None:
            got = local[got_at][begin : begin + places * blocks]
            if vector:
                total = total + join_vector(got, 8)[:, None]
            else:
                total = total + widen(got.reshape(keep.shape))
        target = sent_to[stream]
        if not whole:
            made[kept_at][...] = total[: places // 2]
            write(kept_at)
            kept_at += 1
            total = total[places // 2 :]
        if vector:
            send = split_vector(total, target.shape[1])
        else:
            send = total.astype(jnp.bfloat16)
        count = send.shape[0] * blocks
        target[at : at + count] = send.reshape((count,) + target.shape[1:])
    for n in range(inputs):
        need(n)
    for n in range(outputs - streams, outputs):
        write(n)
    wait_all(outward)


def round_step(chains, received, rows, limit):
    given, kept, plan, passes = [], [], [], {}
    at_of, lengths = {}, {}
    stream_keys = list(received)
    given = [received[key] for key in stream_keys]
    hops = []
    for chain in chains.values():
        if chain["hops"] and chain["hops"][0] not in hops:
            hops.append(chain["hops"][0])
    shapes = []
    for name, chain in chains.items():
        if not chain["hops"]:
            continue
        hop = chain["hops"][0]
        at = lengths.get(hop, 0)
        at_of[name] = at
        if chain["send"] is not None:
            given.append(chain["send"].reshape((-1,) + chain["send"].shape[-2:]))
            passes[len(given) - 1] = (hops.index(hop), at)
            lengths[hop] = at + given[-1].shape[0]
            continue
        keep = chain["keep"]
        given.append(keep)
        keep_at = len(given) - 1
        got_at, begin = None, 0
        if chain["got"] is not None:
            got_at, begin = stream_keys.index(chain["got"][0]), chain["got"][1]
        places, blocks = keep.shape[:2]
        whole = places == 1
        plan.append((keep_at, got_at, begin, hops.index(hop), at, whole, chain["vector"]))
        lengths[hop] = at + (blocks if whole else places // 2 * blocks)
        if not whole:
            shapes.append(((places // 2,) + keep.shape[1:], jnp.float32))
            kept.append(name)
    shapes = shapes + [((lengths[hop], rows, LANES), jnp.bfloat16) for hop in hops]
    results = pl.pallas_call(
        functools.partial(round_kernel, plan, passes, len(given), len(hops)),
        in_specs=[got_spec()] * len(given),
        out_specs=[any_spec()] * len(shapes),
        out_shape=[jax.ShapeDtypeStruct(shape, kind) for shape, kind in shapes],
        scratch_shapes=[
            pltpu.VMEM((8, LANES) if n in passes else item.shape, item.dtype)
            for n, item in enumerate(given)
        ]
        + [pltpu.VMEM(shape, kind) for shape, kind in shapes]
        + [pltpu.SemaphoreType.DMA((len(given),)), pltpu.SemaphoreType.DMA((len(shapes),))],
        compiler_params=compiler_params(limit),
        cost_estimate=cost(3),
        name="round_step",
    )(*given)
    sent = dict(zip(hops, results[len(kept) :]))
    keeps = dict(zip(kept, results))
    for name, chain in chains.items():
        if not chain["hops"]:
            continue
        hop = chain["hops"].pop(0)
        at = at_of[name]
        if chain["send"] is not None:
            chain["send"] = None
        elif name in keeps:
            chain["keep"] = keeps[name]
        else:
            count = chain["keep"].shape[1]
            chain["keep"] = sent[hop][at : at + count][None]
        chain["got"] = (hop, at)
    return sent


def token_kernel(hidden_ref, grads_ref, question_ref, lookup_ref, content_ref, out_ref):
    out_ref[...] = (
        hidden_ref[...]
        + dot_nt(grads_ref[0], question_ref[...])
        + dot_nt(grads_ref[1], lookup_ref[...])
        + dot_nt(grads_ref[2], content_ref[...])
    )


def token_step(hidden, grads, question, lookup, content):
    tokens, width = hidden.shape
    wide = 2 * LANES
    weight = pl.BlockSpec((wide, width), lambda i: (i, 0))
    column = pl.BlockSpec((tokens, wide), lambda i: (0, i))
    return pl.pallas_call(
        token_kernel,
        grid=(width // wide,),
        in_specs=[column, pl.BlockSpec((3, tokens, width), lambda i: (0, 0, 0))] + [weight] * 3,
        out_specs=column,
        out_shape=jax.ShapeDtypeStruct((tokens, width), jnp.float32),
        compiler_params=compiler_params(),
        cost_estimate=cost(5),
        name="token_step",
    )(hidden, grads, question, lookup, content)


def attention_kernel(
    token_at,
    attn_at,
    places_z,
    side_ref,
    own_ref,
    other_ref,
    grads_own_ref,
    grads_other_ref,
    branch_own_ref,
    branch_other_ref,
    keep_x,
    send_x,
    keep_y,
    send_y,
    keep_z,
    send_z,
    token_left,
    attn_left,
    token_right,
    attn_right,
    made_x,
    made_y,
    made_z,
    left_sems,
    right_sems,
    out_sems,
):
    places, rows, _ = token_left.shape
    tokens = branch_own_ref.shape[0]
    wide = 2 * LANES
    left_copies = side_copies(own_ref, other_ref, token_at, rows, token_left, left_sems.at[0])
    attn_copies = side_copies(own_ref, other_ref, attn_at, rows, attn_left, left_sems.at[1])
    right_copies = []
    for chunk in range(3):
        columns = pl.ds(chunk * wide, wide)
        copies = []
        for core, (grads, branch) in enumerate(
            ((grads_own_ref, branch_own_ref), (grads_other_ref, branch_other_ref))
        ):
            token_rows = pl.ds(core * tokens, tokens)
            pairs = [
                (grads.at[i, :, columns], token_right.at[chunk, token_rows, pl.ds(i * wide, wide)])
                for i in range(3)
            ]
            pairs.append((branch.at[:, columns], attn_right.at[chunk, token_rows]))
            for i, (source, target) in enumerate(pairs):
                copies.append(
                    pltpu.make_async_copy(source, target, right_sems.at[chunk, 4 * core + i])
                )
        right_copies.append(copies)
    start_all(left_copies + right_copies[0][:3] + right_copies[0][4:7] + attn_copies)
    start_all(right_copies[0][3:4] + right_copies[0][7:] + right_copies[1] + right_copies[2])
    outward = []
    half = places // 2
    side = side_ref[0]
    for chunk in range(3):
        if chunk == 0:
            wait_all(left_copies + right_copies[0][:3] + right_copies[0][4:7])
        else:
            wait_all(right_copies[chunk])
        token_product = dot_nn(flat(token_left), token_right[chunk]).astype(jnp.bfloat16)
        if chunk == 0:
            wait_all(attn_copies + right_copies[0][3:4] + right_copies[0][7:])
        attn_product = dot_nn(flat(attn_left), attn_right[chunk]).astype(jnp.bfloat16)
        products = [
            token_product[:, :wide],
            attn_product,
            token_product[:, wide : 2 * wide],
            token_product[:, 2 * wide :],
        ]
        for which, product in enumerate(products):
            for place in range(places):
                for tile in range(2):
                    block = product[
                        place * rows : (place + 1) * rows, tile * LANES : (tile + 1) * LANES
                    ]
                    if chunk == 0:
                        made_x[place, which * 2 + tile] = block
                    elif chunk == 1:
                        where = jnp.bitwise_xor(side, which // 2)
                        made_y[where, place, which % 2 * 2 + tile] = block
                    else:
                        made_z[places_z[place], which * 2 + tile] = block
        if chunk == 0:
            pairs = [(made_x.at[:half], keep_x), (made_x.at[half:], send_x)]
        elif chunk == 1:
            pairs = [(made_y.at[0], keep_y), (made_y.at[1], send_y)]
        else:
            pairs = [(made_z.at[:half], keep_z), (made_z.at[half:], send_z)]
        for source, target in pairs:
            copy = pltpu.make_async_copy(source, target, out_sems.at[len(outward)])
            copy.start()
            outward.append(copy)
    wait_all(outward)


def attention_step(
    side, own, other, token_at, attn_at, rows, places_z, grads, grads_other, branch, branch_other
):
    places, _, tokens = own.shape
    wide = 2 * LANES
    low = jnp.bfloat16
    half = places // 2
    shape = jax.ShapeDtypeStruct((half, 8, rows, LANES), low)
    shape_y = jax.ShapeDtypeStruct((places, 4, rows, LANES), low)
    return pl.pallas_call(
        functools.partial(attention_kernel, token_at, attn_at, places_z),
        in_specs=[smem_spec()] + [any_spec(), got_spec()] * 3,
        out_specs=[any_spec()] * 6,
        out_shape=[shape, shape, shape_y, shape_y, shape, shape],
        scratch_shapes=[
            pltpu.VMEM((places, rows, 2 * tokens), low),
            pltpu.VMEM((places, rows, 2 * tokens), low),
            pltpu.VMEM((3, 2 * tokens, 3 * wide), low),
            pltpu.VMEM((3, 2 * tokens, wide), low),
            pltpu.VMEM((places, 8, rows, LANES), low),
            pltpu.VMEM((2, places, 4, rows, LANES), low),
            pltpu.VMEM((places, 8, rows, LANES), low),
            pltpu.SemaphoreType.DMA((2, 2)),
            pltpu.SemaphoreType.DMA((3, 8)),
            pltpu.SemaphoreType.DMA((6,)),
        ],
        compiler_params=compiler_params(),
        cost_estimate=cost(6),
        name="attention_step",
    )(side, own, other, grads, grads_other, branch, branch_other)


def body(
    hidden_states_in,
    piece_sizes,
    matching_passage_number,
    softmax_sharpness,
    question_projection,
    question_offset,
    lookup_projection,
    content_projection,
    content_offset,
    mixing_result_projection,
    mixing_result_offset,
    mixing_layernorm_scale,
    mixing_layernorm_offset,
    widening_projection,
    widening_offset,
    narrowing_projection,
    narrowing_offset,
    perceptron_layernorm_scale,
    perceptron_layernorm_offset,
):
    rows_here, length, width = hidden_states_in.shape
    segments = piece_sizes.shape[1]
    per_device = segments // 2
    groups_y = lax.axis_size("gy")
    rows = width // groups_y
    inner_rows = widening_offset.shape[0] // groups_y
    gy_bits = powers_below(groups_y)
    order_x = gy_bits[1:]
    order_z = gy_bits[2:3] + gy_bits[1:2] + gy_bits[3:]
    here = lax.axis_index("gy").astype(jnp.int32).reshape(1)
    side = (lax.axis_index("gx").astype(jnp.int32) & 1).reshape(1)
    (
        queries,
        keys,
        keys_t,
        values,
        lse,
        normed_one,
        inv_one,
        slope,
        normed_two,
        inv_two,
        pooled,
        message,
        side_own,
        side_send,
    ) = forward_step(
        here,
        piece_sizes,
        matching_passage_number,
        place_masks(order_x),
        place_masks(order_z),
        [
            hidden_states_in[0],
            question_projection,
            lookup_projection,
            content_projection,
            mixing_result_projection,
            widening_projection,
            narrowing_projection,
            question_offset,
            content_offset,
            mixing_result_offset,
            mixing_layernorm_scale,
            mixing_layernorm_offset,
            widening_offset,
            narrowing_offset,
            perceptron_layernorm_scale,
            perceptron_layernorm_offset,
        ],
    )
    gathered, numbers_of, place, side_other = gather_blocks(
        message, swap_with(side_send, "gy", 1)
    )
    numbers = (numbers_of[:, None] * per_device + np.arange(per_device)[None, :]).reshape(1, -1)
    loss_out, grad_hidden_two, branch_two, sums_two = loss_step(
        place.astype(jnp.int32).reshape(1),
        piece_sizes,
        softmax_sharpness,
        jnp.asarray(numbers, jnp.int32),
        gathered,
        pooled,
        normed_two,
        inv_two,
        perceptron_layernorm_scale,
    )
    branch_two_other = swap_with(branch_two, "gy", 1)
    outer_keep_x, outer_send_x, outer_keep_z, outer_send_z = outer_step(
        side_own, side_other, branch_two, branch_two_other, inner_rows // 2
    )
    outer_send_x, outer_send_z, branch_two = tie(outer_send_x, outer_send_z, branch_two)
    outer_got_x = swap_with(outer_send_x, "gy", order_x[0])
    outer_got_z = swap_with(outer_send_z, "gy", order_z[0])
    grad_pre, grad_b_inner, grad_hidden_one, branch_one, grad_attn, sums_one = before_step(
        branch_two,
        slope,
        narrowing_projection,
        widening_projection,
        grad_hidden_two,
        normed_one,
        inv_one,
        mixing_layernorm_scale,
        mixing_result_projection,
    )
    outer_got_x, outer_got_z, grad_pre, branch_one, grad_attn = tie(
        outer_got_x, outer_got_z, grad_pre, branch_one, grad_attn
    )
    grad_pre_other = swap_with(grad_pre, "gy", 1)
    branch_one_other = swap_with(branch_one, "gy", 1)
    (outer_keep_x, outer_send_x), (outer_keep_z, outer_send_z) = add_step(
        [[(outer_keep_x, outer_got_x)], [(outer_keep_z, outer_got_z)]]
    )
    outer_send_x, outer_send_z, grad_attn = tie(outer_send_x, outer_send_z, grad_attn)
    outer_got_x = swap_with(outer_send_x, "gy", order_x[1])
    outer_got_z = swap_with(outer_send_z, "gy", order_z[1])
    grads, sums_attn = attend_back_step(
        piece_sizes,
        queries,
        keys,
        keys_t,
        values,
        lse,
        grad_attn,
    )
    grads, grad_pre_other, branch_one_other, outer_got_x, outer_got_z = tie(
        grads, grad_pre_other, branch_one_other, outer_got_x, outer_got_z
    )
    grads_other = swap_with(grads, "gy", 1)
    (outer_keep_x, outer_send_x), (outer_keep_z, outer_send_z) = add_step(
        [[(outer_keep_x, outer_got_x)], [(outer_keep_z, outer_got_z)]]
    )
    outer_got_x = swap_with(outer_send_x, "gy", order_x[2])
    outer_got_z = swap_with(outer_send_z, "gy", order_z[2])
    inner_keep_x, inner_send_x, inner_keep_y, inner_send_y = inner_step(
        side, side_own, side_other, inner_rows, rows, grad_pre, grad_pre_other
    )
    gx_bits = powers_below(lax.axis_size("gx"))
    inner_send_x, inner_send_y, grads_other = tie(inner_send_x, inner_send_y, grads_other)
    inner_got_x = swap_with(inner_send_x, "gy", order_x[0])
    inner_got_y = swap_with(inner_send_y, "gx", 1)
    masks_x, masks_z = place_masks(order_x), place_masks(order_z)
    attn_keep_x, attn_send_x, attn_keep_y, attn_send_y, attn_keep_z, attn_send_z = attention_step(
        side,
        side_own,
        side_other,
        inner_rows + rows,
        inner_rows + 2 * rows,
        rows,
        [masks_z.index(mask) for mask in masks_x],
        grads,
        grads_other,
        branch_one,
        branch_one_other,
    )
    attn_got_x = swap_with(attn_send_x, "gy", order_x[0])
    attn_got_y = swap_with(attn_send_y, "gx", 1)
    attn_got_z = swap_with(attn_send_z, "gy", order_z[0])
    attn_keep_x, sums_attn = tie(attn_keep_x, sums_attn)
    vectors = jnp.concatenate([sums_attn, sums_one, sums_two], axis=0)
    vectors = vectors.reshape(8, groups_y, rows).transpose(1, 0, 2).reshape(groups_y, 8 * rows)
    vectors = jnp.concatenate([vectors, grad_b_inner.reshape(groups_y, -1)], axis=1)
    used = vectors.shape[1]
    vectors = jnp.pad(vectors, ((0, 0), (0, 8 * LANES - used)))
    vectors = vectors.reshape((2,) * len(gy_bits) + (8 * LANES,))
    for axis, bit in enumerate(reversed(gy_bits)):
        high = (lax.axis_index("gy") & bit) != 0
        vectors = jnp.where(high, jnp.flip(vectors, axis=axis), vectors)
    vectors = vectors.transpose(tuple(reversed(range(len(gy_bits)))) + (len(gy_bits),))
    vectors = vectors.reshape(2, groups_y // 2, 1, 8, LANES)
    vector_got = swap_with(vectors[1], "gy", gy_bits[0])
    gx_hops = [("gx", bit) for bit in gx_bits]
    hops_x = [("gy", bit) for bit in order_x]
    hops_z = [("gy", bit) for bit in order_z]
    hops_y = gx_hops[:1] + hops_x + gx_hops[1:] + gx_hops[:1]

    def chain(keep, got, send, hops, vector=False):
        return {
            "keep": keep,
            "got": got,
            "send": send,
            "hops": list(hops),
            "vector": vector,
        }

    chains = {
        "inner_x": chain(inner_keep_x, ("inner_x", 0), None, hops_x[1:] + gx_hops),
        "inner_y": chain(inner_keep_y, ("inner_y", 0), None, hops_y[1:]),
        "outer_x": chain(outer_keep_x, ("outer_x", 0), None, hops_x[3:] + gx_hops),
        "outer_z": chain(outer_keep_z, ("outer_z", 0), None, hops_z[3:] + gx_hops),
    }
    received = {
        "inner_x": inner_got_x,
        "inner_y": inner_got_y,
        "outer_x": outer_got_x,
        "outer_z": outer_got_z,
    }
    received = {key: item.reshape((-1,) + item.shape[-2:]) for key, item in received.items()}
    finals = {}

    def finish():
        for name, item in chains.items():
            if not item["hops"] and name not in finals:
                hop, at = item["got"]
                count = item["keep"].shape[1]
                finals[name] = (item["keep"][0], received[hop][at : at + count])

    sent = round_step(chains, received, rows, VMEM_BYTES)
    keys = list(sent)
    *items, grads = tie(*[sent[key] for key in keys], grads)
    items = [swap_with(item, key[0], key[1]) for item, key in zip(items, keys)]
    grad_tokens = token_step(
        grad_hidden_one, grads, question_projection, lookup_projection, content_projection
    )
    *items, attn_got_x, attn_got_y, attn_got_z, grad_tokens, vector_got = tie(
        *items, attn_got_x, attn_got_y, attn_got_z, grad_tokens, vector_got
    )
    received = dict(zip(keys, items))
    finish()
    begun = {"attn_x": attn_got_x, "attn_y": attn_got_y, "attn_z": attn_got_z}
    for name, item in begun.items():
        received[name] = item.reshape((-1,) + item.shape[-2:])
    vector_hops = [("gy", bit) for bit in gy_bits[1:]] + gx_hops
    chains["vector"] = chain(vectors[0] + vector_got, None, None, vector_hops, True)
    chains["attn_x"] = chain(attn_keep_x, ("attn_x", 0), None, hops_x[1:] + gx_hops)
    chains["attn_y"] = chain(attn_keep_y, ("attn_y", 0), None, hops_y[1:])
    chains["attn_z"] = chain(attn_keep_z, ("attn_z", 0), None, hops_z[1:] + gx_hops)
    limit = SMALL_BYTES
    while any(item["hops"] for item in chains.values()):
        sent = round_step(chains, received, rows, limit)
        limit = SMALL_BYTES
        keys = list(sent)
        items = tie(*[swap_with(sent[key], key[0], key[1]) for key in keys])
        received = dict(zip(keys, items))
        finish()

    def summed(name):
        mine, other = finals[name]
        return widen(mine) + widen(other)

    def side_by_side(name):
        mine, other = finals[name]
        high = (lax.axis_index("gx") & 1) != 0
        return widen(
            jnp.concatenate([jnp.where(high, other, mine), jnp.where(high, mine, other)], axis=0)
        )

    vectors = sum(join_vector(item, 8) for item in finals["vector"])
    vectors = vectors.reshape(1, 8 * LANES)[:, :used]
    outer_x, outer_z = summed("outer_x"), summed("outer_z")
    attn_x, attn_y, attn_z = summed("attn_x"), side_by_side("attn_y"), summed("attn_z")
    inner_sums = jnp.concatenate([summed("inner_x"), side_by_side("inner_y")], axis=0)
    vector_sums = vectors[0]
    b_query, b_value, b_output, gain_attn, shift_attn, b_outer, gain_ffn, shift_ffn = [
        vector_sums[i * rows : (i + 1) * rows] for i in range(8)
    ]
    grad_w_query, grad_w_output, grad_w_key, grad_w_value = [
        share_of(
            jnp.concatenate([part[2 * i : 2 * i + 2] for part in (attn_x, attn_y, attn_z)]), width
        )
        for i in range(4)
    ]
    grad_w_outer = jnp.concatenate([share_of(outer_x, width), share_of(outer_z, width)], axis=0)
    return (
        loss_out.reshape(1),
        pooled[None],
        grad_tokens.reshape(rows_here, length, width),
        grad_w_query,
        b_query,
        grad_w_key,
        grad_w_value,
        b_value,
        grad_w_output,
        b_output,
        gain_attn,
        shift_attn,
        share_of(inner_sums, widening_offset.shape[0]),
        vector_sums[8 * rows :],
        grad_w_outer,
        b_outer,
        gain_ffn,
        shift_ffn,
    )


def solution(mesh):
    return jax.shard_map(
        body,
        mesh=mesh,
        in_specs=(
            P(("gx", "gy"), None, None),
            P(("gx", "gy"), None),
            P(("gx", "gy")),
            P(),
            P(),
            P(),
            P(),
            P(),
            P(),
            P(),
            P(),
            P(),
            P(),
            P(),
            P(),
            P(),
            P(),
            P(),
            P(),
        ),
        out_specs=(
            P(),
            P(("gx", "gy"), None, None),
            P(("gx", "gy"), None, None),
            P("gy", None),
            P("gy"),
            P("gy", None),
            P("gy", None),
            P("gy"),
            P("gy", None),
            P("gy"),
            P("gy"),
            P("gy"),
            P("gy", None),
            P("gy"),
            P("gy", None),
            P("gy"),
            P("gy"),
            P("gy"),
        ),
        check_vma=False,
    )
```

```python
import functools

import jax
import jax.numpy as jnp
import numpy as np
from jax import lax
from jax.experimental import pallas as pl
from jax.experimental.pallas import tpu as pltpu
from jax.sharding import PartitionSpec as P

HEADS = 12
HD = 64
LANES = 128
VMEM_BYTES = 60 * 1024 * 1024
SMALL_BYTES = 24 * 1024 * 1024

EPS_NORM = 1e-12
EPS_UNIT = 1e-06
NEG_FILL = -1e30


def standardize(hidden):
    center = hidden - jnp.mean(hidden, axis=-1, keepdims=True)
    inv_scale = lax.rsqrt(jnp.mean(center * center, axis=-1, keepdims=True) + EPS_NORM)
    return (center * inv_scale, inv_scale)


def standardize_back(normed, inv_scale, grad_normed):
    mean_grad = jnp.mean(grad_normed, axis=-1, keepdims=True)
    mean_both = jnp.mean(grad_normed * normed, axis=-1, keepdims=True)
    return inv_scale * (grad_normed - mean_grad - normed * mean_both)


def widen(value):
    return value.astype(jnp.float32)


def powers_below(count):
    bits = []
    bit = 1
    while bit < count:
        bits.append(bit)
        bit *= 2
    return bits


def place_masks(bits):
    masks = [0]
    for bit in reversed(bits):
        masks = masks + [mask ^ bit for mask in masks]
    return masks


def swap_with(value, axis, bit):
    count = lax.axis_size(axis)
    return lax.ppermute(value, axis, [(i, i ^ bit) for i in range(count)])


def tie(*values):
    return lax.optimization_barrier(values)


def gather_steps():
    gy = powers_below(lax.axis_size("gy"))
    far = [("gy", bit) for bit in reversed(gy[2:])]
    near = [("gy", bit) for bit in reversed(gy[:2])]
    return far + [("gx", bit) for bit in powers_below(lax.axis_size("gx"))] + near


def gather_blocks(block, beside):
    groups_y = lax.axis_size("gy")
    devices = groups_y * lax.axis_size("gx")
    steps = gather_steps()
    numbers = [bit * (groups_y if axis == "gx" else 1) for axis, bit in steps]
    groups = [numbers[at : min(at + 2, len(steps) - 1)] for at in range(0, len(steps) - 1, 2)]
    groups.append(numbers[-1:])
    gathered = block[None]
    number = np.zeros((1,), np.int32)
    for group, bits in enumerate(groups):
        if group == 2:
            gathered, beside = tie(gathered, beside)
        masks = [0]
        for bit in bits:
            masks = masks + [mask ^ bit for mask in masks]
        parts = [gathered] + [
            lax.ppermute(gathered, ("gx", "gy"), [(i, i ^ mask) for i in range(devices)])
            for mask in masks[1:]
        ]
        gathered = jnp.concatenate(parts, axis=0)
        number = np.concatenate([number + mask for mask in masks])
    place = 0
    for step, (axis, bit) in enumerate(steps):
        place = place + jnp.where((lax.axis_index(axis) & bit) != 0, 1 << step, 0)
    return gathered, number, place, beside


def share_of(blocks, columns):
    tiles = columns // LANES
    count, rows, _ = blocks.shape
    parts = count // tiles
    view = blocks.reshape(tiles, parts, rows, LANES)
    return view.transpose(1, 2, 0, 3).reshape(parts * rows, columns)


def compiler_params(limit=VMEM_BYTES):
    return pltpu.CompilerParams(vmem_limit_bytes=limit)


def dot_nt(left, right):
    return lax.dot_general(
        left, right, (((1,), (1,)), ((), ())), preferred_element_type=jnp.float32
    )


def dot_nn(left, right):
    return jnp.dot(left, right, preferred_element_type=jnp.float32)


def start_all(copies):
    for copy in copies:
        copy.start()


def wait_all(copies):
    for copy in copies:
        copy.wait()


def as_row(ref):
    return ref[...].astype(jnp.float32).reshape(1, ref.shape[0])


def lengths_as_row(sizes_ref, lanes, segments):
    lane = lax.broadcasted_iota(jnp.int32, (1, lanes), 1) % segments
    start = jnp.zeros((1, lanes), jnp.int32)
    end = jnp.zeros((1, lanes), jnp.int32)
    at = jnp.int32(0)
    for segment in range(segments):
        size = sizes_ref[0, segment]
        start = jnp.where(lane == segment, at, start)
        at = at + size
        end = jnp.where(lane == segment, at, end)
    return start, end


def counts_as_column(sizes_ref, segments):
    row = lax.broadcasted_iota(jnp.int32, (segments, 1), 0)
    counts = jnp.zeros((segments, 1), jnp.float32)
    for segment in range(segments):
        counts = jnp.where(row == segment, sizes_ref[0, segment].astype(jnp.float32), counts)
    return counts


def starts_as_column(sizes_ref, segments):
    row = lax.broadcasted_iota(jnp.int32, (segments, 1), 0)
    start = jnp.zeros((segments, 1), jnp.int32)
    end = jnp.zeros((segments, 1), jnp.int32)
    at = jnp.int32(0)
    for segment in range(segments):
        size = sizes_ref[0, segment]
        start = jnp.where(row == segment, at, start)
        at = at + size
        end = jnp.where(row == segment, at, end)
    return start, end


def band(length):
    return [(0, length // 2, 0, 3 * length // 4), (length // 2, length, length // 4, length)]


def mask_of(sizes_ref, segments, query_at, query_end, key_at, key_end):
    query = query_at + lax.broadcasted_iota(jnp.int32, (1, query_end - query_at), 1)
    low = jnp.zeros_like(query)
    high = jnp.zeros_like(query)
    at = jnp.int32(0)
    for segment in range(segments):
        end = at + sizes_ref[0, segment]
        inside = (query >= at) & (query < end)
        low = jnp.where(inside, at, low)
        high = jnp.where(inside, end, high)
        at = end
    padding = query >= at
    low = jnp.where(padding, at, low)
    high = jnp.where(padding, key_end, high)
    key = key_at + lax.broadcasted_iota(jnp.int32, (key_end - key_at, query_end - query_at), 0)
    return jnp.where((key >= low) & (key < high), 0.0, NEG_FILL)


def got_spec():
    return pl.BlockSpec(memory_space=pl.ANY)


def vmem_spec():
    return pl.BlockSpec(memory_space=pltpu.VMEM)


def smem_spec():
    return pl.BlockSpec(memory_space=pltpu.SMEM)


def any_spec():
    return pl.BlockSpec(memory_space=pltpu.HBM)


def cost(microseconds):
    return pl.CostEstimate(
        flops=int(microseconds * 1.1e9), bytes_accessed=1000000, transcendentals=0
    )


def forward_kernel(segments, masks_x, masks_z, here_ref, sizes_ref, matching_ref, *refs):
    given, refs = refs[:16], refs[16:]
    results, refs = refs[:14], refs[14:]
    side_own, side_send = results[-2:]
    local, refs = refs[:16], refs[16:]
    made, refs = refs[:12], refs[12:]
    (
        tokens_ref,
        question_w,
        lookup_w,
        content_w,
        mixing_w,
        widening_w,
        narrowing_w,
        question_row,
        content_row,
        mixing_row,
        gain_one_row,
        shift_one_row,
        widening_row,
        narrowing_row,
        gain_two_row,
        shift_two_row,
    ) = local
    (
        query_ref,
        key_ref,
        key_t_ref,
        value_ref,
        lse_ref,
        normed_one_ref,
        inv_one_ref,
        slope_ref,
        normed_two_ref,
        inv_two_ref,
        pooled_ref,
        message_ref,
    ) = made
    value_t, token_t, attn_t, out_one_t, inner_t, fill = refs[:6]
    out_one, out_one_low, total, in_sems, out_sems, side_sems = refs[6:]
    length, width = tokens_ref.shape
    hidden_units = widening_w.shape[1]
    here = here_ref[0]
    share_rows = side_own.shape[1] // (hidden_units // width + 3)
    inner_rows = hidden_units // width * share_rows
    first_rows = inner_rows // 2
    copies = [
        pltpu.make_async_copy(source, target, in_sems.at[i])
        for i, (source, target) in enumerate(zip(given, local))
    ]
    outward = [
        pltpu.make_async_copy(source, target, out_sems.at[i])
        for i, (source, target) in enumerate(zip(made, results))
    ]
    side_copies = []

    def send_side(source, source_rows, offset, count, at, masks):
        for place, mask in enumerate(masks):
            for flip, target in enumerate((side_own, side_send)):
                share = jnp.bitwise_xor(here, mask ^ flip)
                first = pl.multiple_of(share * source_rows + offset, 8)
                copy = pltpu.make_async_copy(
                    source.at[pl.ds(first, count)],
                    target.at[place, pl.ds(at, count)],
                    side_sems.at[len(side_copies)],
                )
                copy.start()
                side_copies.append(copy)

    start_all(copies[:2] + copies[7:] + copies[2:4])
    ranges = band(length)
    for i, (query_at, query_end, key_at, key_end) in enumerate(ranges):
        fill[i] = mask_of(sizes_ref, segments, query_at, query_end, key_at, key_end)
    wait_all(copies[:2] + copies[7:])
    start_all(copies[4:7])
    product = dot_nn(tokens_ref[...], question_w[...]) + as_row(question_row)
    query_ref[...] = product.astype(jnp.bfloat16) * jnp.bfloat16(HD ** (-0.5))
    token_t[...] = tokens_ref[...].T
    copies[2].wait()
    product = dot_nn(tokens_ref[...], lookup_w[...]).astype(jnp.bfloat16)
    key_ref[...] = product
    key_t_ref[...] = product.T
    copies[3].wait()
    product = (dot_nn(tokens_ref[...], content_w[...]) + as_row(content_row)).astype(jnp.bfloat16)
    value_ref[...] = product
    value_t[...] = product.T
    start_all(outward[:4])
    send_side(token_t, share_rows, 0, share_rows, inner_rows + share_rows, masks_x)
    lane = lax.broadcasted_iota(jnp.int32, (1, LANES), 1)
    units = [(at, i) for at in range(HEADS) for i in range(len(ranges))]

    def scores_of(unit):
        at, i = unit
        query_at, query_end, key_at, key_end = ranges[i]
        first = at * HD // LANES * LANES
        lanes = slice(first, first + LANES)
        which = (at * HD - first) // HD
        query = jnp.where((lane // HD) == which, query_ref[query_at:query_end, lanes], 0)
        return dot_nt(key_ref[key_at:key_end, lanes], query) + fill[i]

    def attend(unit, scores):
        at, i = unit
        query_at, query_end, key_at, key_end = ranges[i]
        top = jnp.max(scores, axis=0, keepdims=True)
        expo = jnp.exp(scores - top)
        norm = jnp.sum(expo, axis=0, keepdims=True)
        probs = (expo * (1.0 / norm)).astype(jnp.bfloat16)
        lse_ref[at // 4, at % 4 : at % 4 + 1, query_at:query_end] = top + jnp.log(norm)
        mixed = dot_nn(value_t[at * HD : (at + 1) * HD, key_at:key_end], probs)
        attn_t[at * HD : (at + 1) * HD, query_at:query_end] = mixed.astype(jnp.bfloat16)

    ahead = 4
    waiting = [scores_of(unit) for unit in units[:ahead]]
    for n, unit in enumerate(units):
        if n + ahead < len(units):
            waiting.append(scores_of(units[n + ahead]))
        attend(unit, waiting.pop(0))
    outward[4].start()
    send_side(attn_t, share_rows, 0, share_rows, inner_rows + 2 * share_rows, masks_x)
    copies[4].wait()
    chunk = min(length, 128)
    for at in range(0, length, chunk):
        rows = slice(at, at + chunk)
        hidden = (
            tokens_ref[rows].astype(jnp.float32)
            + dot_nn(attn_t[:, rows].T, mixing_w[...])
            + as_row(mixing_row)
        )
        normed, inv = standardize(hidden)
        normed_one_ref[rows] = normed
        inv_one_ref[rows] = inv
        shifted = normed * as_row(gain_one_row) + as_row(shift_one_row)
        out_one[rows] = shifted
        low = shifted.astype(jnp.bfloat16)
        out_one_low[rows] = low
        out_one_t[:, rows] = low.T
        total[rows] = shifted + as_row(narrowing_row)
    start_all(outward[5:7])
    send_side(out_one_t, share_rows, 0, share_rows, inner_rows, masks_x)
    copies[5].wait()
    copies[6].wait()
    tile = hidden_units // 4
    taller = min(length, 256)
    units = [(at, row) for at in range(0, hidden_units, tile) for row in range(0, length, taller)]

    def widened(unit):
        at, row = unit
        return dot_nn(out_one_low[row : row + taller], widening_w[:, at : at + tile])

    def activate(unit, before):
        at, row = unit
        rows = slice(row, row + taller)
        before = before + widening_row[at : at + tile].astype(jnp.float32).reshape(1, tile)
        cdf = 0.5 * (1.0 + lax.erf(before * 0.7071067811865476))
        pdf = jnp.exp(-0.5 * before * before) * 0.3989422804014327
        inner = (before * cdf).astype(jnp.bfloat16)
        slope_ref[rows, at : at + tile] = (cdf + before * pdf).astype(jnp.bfloat16)
        inner_t[at : at + tile, rows] = inner.T
        total[rows] += dot_nn(inner, narrowing_w[at : at + tile, :])

    ahead = 1
    waiting = [widened(unit) for unit in units[:ahead]]
    for n, unit in enumerate(units):
        if n + ahead < len(units):
            waiting.append(widened(units[n + ahead]))
        activate(unit, waiting.pop(0))
    outward[7].start()
    send_side(inner_t, inner_rows, 0, first_rows, 0, masks_x)
    send_side(inner_t, inner_rows, first_rows, inner_rows - first_rows, first_rows, masks_z)
    start, end = starts_as_column(sizes_ref, segments)
    sums = jnp.zeros((segments, width), jnp.float32)
    for at in range(0, length, chunk):
        rows = slice(at, at + chunk)
        normed, inv = standardize(total[rows])
        normed_two_ref[rows] = normed
        inv_two_ref[rows] = inv
        out_two = normed * as_row(gain_two_row) + as_row(shift_two_row)
        upper = out_two.astype(jnp.bfloat16)
        lower = (out_two - upper.astype(jnp.float32)).astype(jnp.bfloat16)
        token = at + lax.broadcasted_iota(jnp.int32, (segments, chunk), 1)
        member = jnp.where((token >= start) & (token < end), 1.0, 0.0).astype(jnp.bfloat16)
        sums = sums + dot_nn(member, upper) + dot_nn(member, lower)
    pooled = sums / counts_as_column(sizes_ref, segments)
    pooled_ref[...] = pooled
    inv_norm = lax.rsqrt(jnp.sum(pooled * pooled, axis=1, keepdims=True) + EPS_UNIT)
    units = (pooled * inv_norm).astype(jnp.bfloat16)
    half = segments // 2
    place = lax.broadcasted_iota(jnp.int32, (segments, segments), 0)
    source = lax.broadcasted_iota(jnp.int32, (segments, segments), 1)
    wanted = jnp.where(place < half, 2 * place, 2 * (place - half) + 1)
    pick = jnp.where(source == wanted, 1.0, 0.0).astype(jnp.bfloat16)
    message_ref[:, :width] = dot_nn(pick, units).astype(jnp.bfloat16)
    row = lax.broadcasted_iota(jnp.int32, (segments, LANES), 0)
    column = lax.broadcasted_iota(jnp.int32, (segments, LANES), 1)
    digits = jnp.zeros((segments, LANES), jnp.float32)
    for i in range(half):
        number = matching_ref[i]
        digit = jnp.where(column == 0, number & 255, number >> 8).astype(jnp.float32)
        digits = jnp.where((row == i) & (column < 2), digit, digits)
    message_ref[:, width:] = digits.astype(jnp.bfloat16)
    start_all(outward[8:])
    wait_all(outward)
    wait_all(side_copies)


def forward_step(here, sizes, matching, masks_x, masks_z, given):
    tokens, hidden_units = given[0], given[5].shape[1]
    length, width = tokens.shape
    segments = sizes.shape[1]
    half = len(masks_x)
    query_at, query_end, key_at, key_end = band(length)[0]
    low, full = jnp.bfloat16, jnp.float32
    side = ((half, (hidden_units // width + 3) * (width // half // 2), length), low)
    made = [
        ((length, width), low),
        ((length, width), low),
        ((width, length), low),
        ((length, width), low),
        ((HEADS // 4, 4, length), full),
        ((length, width), full),
        ((length, 1), full),
        ((length, hidden_units), low),
        ((length, width), full),
        ((length, 1), full),
        ((segments, width), full),
        ((segments, width + LANES), low),
    ]
    return pl.pallas_call(
        functools.partial(forward_kernel, segments, masks_x, masks_z),
        in_specs=[smem_spec()] * 3 + [any_spec()] * len(given),
        out_specs=[any_spec()] * (len(made) + 2),
        out_shape=[jax.ShapeDtypeStruct(shape, kind) for shape, kind in made + [side, side]],
        scratch_shapes=[pltpu.VMEM(item.shape, item.dtype) for item in given]
        + [pltpu.VMEM(shape, kind) for shape, kind in made]
        + [
            pltpu.VMEM((width, length), low),
            pltpu.VMEM((width, length), low),
            pltpu.VMEM((width, length), low),
            pltpu.VMEM((width, length), low),
            pltpu.VMEM((hidden_units, length), low),
            pltpu.VMEM((2, key_end - key_at, query_end - query_at), full),
            pltpu.VMEM((length, width), full),
            pltpu.VMEM((length, width), low),
            pltpu.VMEM((length, width), full),
            pltpu.SemaphoreType.DMA((len(given),)),
            pltpu.SemaphoreType.DMA((len(made),)),
            pltpu.SemaphoreType.DMA((2 * 5 * half,)),
        ],
        compiler_params=compiler_params(),
        cost_estimate=cost(28),
        name="forward_step",
    )(here, sizes, matching, *given)


def loss_kernel(
    place_ref,
    sizes_ref,
    sharpness_ref,
    numbers_ref,
    gathered_hbm,
    pooled_hbm,
    normed_hbm,
    inv_hbm,
    gain_hbm,
    loss_ref,
    grad_hidden_hbm,
    grad_branch_hbm,
    sums_ref,
    gathered_ref,
    pooled_ref,
    normed_ref,
    inv_ref,
    gain_ref,
    grad_hidden_ref,
    grad_branch_ref,
    sems,
):
    given = [
        (gathered_hbm, gathered_ref),
        (pooled_hbm, pooled_ref),
        (normed_hbm, normed_ref),
        (inv_hbm, inv_ref),
        (gain_hbm, gain_ref),
    ]
    copies = [
        pltpu.make_async_copy(source, target, sems.at[i])
        for i, (source, target) in enumerate(given)
    ]
    start_all(copies)
    segments, width = pooled_ref.shape
    half = segments // 2
    devices = gathered_ref.shape[0]
    total = devices * half
    sharpness = sharpness_ref[0]
    row = lax.broadcasted_iota(jnp.int32, (total, devices * segments), 0)
    column = lax.broadcasted_iota(jnp.int32, (total, devices * segments), 1)
    source = jnp.bitwise_xor(row // half, place_ref[0]) * segments + row % half
    copies[0].wait()
    gathered = gathered_ref[...].reshape(devices * segments, width + LANES)
    pick = jnp.where(column == source, 1.0, 0.0).astype(jnp.bfloat16)
    picked = dot_nn(pick, gathered)
    questions = picked[:, :width].astype(jnp.bfloat16)
    digits = picked[:, width:]
    pick = jnp.where(column == source + half, 1.0, 0.0).astype(jnp.bfloat16)
    passages = dot_nn(pick, gathered[:, :width]).astype(jnp.bfloat16)
    matching = (digits[:, 0:1] + 256.0 * digits[:, 1:2]).astype(jnp.int32)
    table = dot_nt(questions, passages) / sharpness
    top = jnp.max(table, axis=1, keepdims=True)
    expo = jnp.exp(table - top)
    expo_total = jnp.sum(expo, axis=1, keepdims=True)
    chosen = matching == numbers_ref[...]
    positive = jnp.sum(jnp.where(chosen, table, 0.0), axis=1, keepdims=True)
    loss_ref[...] = (
        jnp.sum(top + jnp.log(expo_total) - positive, axis=0, keepdims=True) / total
    )
    slope = (expo / expo_total - chosen.astype(jnp.float32)) / total
    grad_dot = (slope / sharpness).astype(jnp.bfloat16)
    segment_at = lax.broadcasted_iota(jnp.int32, (segments, total), 0)
    column = lax.broadcasted_iota(jnp.int32, (segments, total), 1)
    mine = column == place_ref[0] * half + segment_at // 2
    is_query = segment_at % 2 == 0
    pick_query = jnp.where(mine & is_query, 1.0, 0.0).astype(jnp.bfloat16)
    pick_passage = jnp.where(mine & ~is_query, 1.0, 0.0).astype(jnp.bfloat16)
    row_terms = dot_nn(pick_query, grad_dot).astype(jnp.bfloat16)
    column_terms = dot_nt(pick_passage, grad_dot).astype(jnp.bfloat16)
    grad_units = dot_nn(row_terms, passages) + dot_nn(column_terms, questions)
    wait_all(copies[1:])
    pooled = pooled_ref[...]
    inv_norm = lax.rsqrt(jnp.sum(pooled * pooled, axis=1, keepdims=True) + EPS_UNIT)
    units = pooled * inv_norm
    along = jnp.sum(units * grad_units, axis=1, keepdims=True)
    grad_pooled = inv_norm * (grad_units - units * along) / counts_as_column(sizes_ref, segments)
    upper = grad_pooled.astype(jnp.bfloat16)
    lower = (grad_pooled - upper.astype(jnp.float32)).astype(jnp.bfloat16)
    both = jnp.concatenate([upper, lower], axis=0)
    start, end = lengths_as_row(sizes_ref, 2 * segments, segments)
    gain = as_row(gain_ref)
    outward = []
    tokens = normed_ref.shape[0]
    chunk = min(tokens, 128)
    gain_sum = jnp.zeros((1, width), jnp.float32)
    shift_sum = jnp.zeros((1, width), jnp.float32)
    bias_sum = jnp.zeros((1, width), jnp.float32)
    for at in range(0, tokens, chunk):
        token = at + lax.broadcasted_iota(jnp.int32, (chunk, 2 * segments), 0)
        member = jnp.where((token >= start) & (token < end), 1.0, 0.0).astype(jnp.bfloat16)
        grad_out = dot_nn(member, both)
        normed = normed_ref[at : at + chunk]
        gain_sum = gain_sum + jnp.sum(grad_out * normed, axis=0, keepdims=True)
        shift_sum = shift_sum + jnp.sum(grad_out, axis=0, keepdims=True)
        grad_hidden = standardize_back(normed, inv_ref[at : at + chunk], grad_out * gain)
        grad_hidden_ref[at : at + chunk] = grad_hidden
        low = grad_hidden.astype(jnp.bfloat16)
        grad_branch_ref[at : at + chunk] = low
        bias_sum = bias_sum + jnp.sum(low.astype(jnp.float32), axis=0, keepdims=True)
        for source_ref, target in (
            (grad_hidden_ref, grad_hidden_hbm),
            (grad_branch_ref, grad_branch_hbm),
        ):
            copy = pltpu.make_async_copy(
                source_ref.at[at : at + chunk],
                target.at[at : at + chunk],
                sems.at[len(copies) + len(outward)],
            )
            copy.start()
            outward.append(copy)
    sums_ref[...] = jnp.concatenate([bias_sum, gain_sum, shift_sum], axis=0)
    wait_all(outward)


def loss_step(place, sizes, sharpness, numbers, gathered, pooled, normed, inv, gain):
    tokens, width = normed.shape
    low, full = jnp.bfloat16, jnp.float32
    chunks = -(-tokens // 128)
    return pl.pallas_call(
        loss_kernel,
        in_specs=[smem_spec()] * 3 + [vmem_spec()] + [any_spec()] * 5,
        out_specs=[vmem_spec(), any_spec(), any_spec(), vmem_spec()],
        out_shape=[
            jax.ShapeDtypeStruct((1, 1), full),
            jax.ShapeDtypeStruct((tokens, width), full),
            jax.ShapeDtypeStruct((tokens, width), low),
            jax.ShapeDtypeStruct((3, width), full),
        ],
        scratch_shapes=[
            pltpu.VMEM(gathered.shape, low),
            pltpu.VMEM(pooled.shape, full),
            pltpu.VMEM(normed.shape, full),
            pltpu.VMEM(inv.shape, full),
            pltpu.VMEM(gain.shape, low),
            pltpu.VMEM((tokens, width), full),
            pltpu.VMEM((tokens, width), low),
            pltpu.SemaphoreType.DMA((5 + 2 * chunks,)),
        ],
        compiler_params=compiler_params(),
        cost_estimate=cost(4),
        name="loss_step",
    )(place, sizes, sharpness, numbers, gathered, pooled, normed, inv, gain)


def before_kernel(
    branch_hbm,
    slope_hbm,
    narrowing_hbm,
    widening_hbm,
    hidden_hbm,
    normed_hbm,
    inv_hbm,
    gain_hbm,
    mixing_hbm,
    grad_pre_hbm,
    bias_ref,
    grad_hidden_hbm,
    grad_branch_hbm,
    grad_attn_hbm,
    sums_ref,
    branch_ref,
    slope_ref,
    narrowing_ref,
    widening_ref,
    total,
    normed_ref,
    inv_ref,
    gain_ref,
    mixing_ref,
    grad_pre_ref,
    grad_hidden_ref,
    grad_branch_ref,
    grad_attn_ref,
    in_sems,
    part_sems,
    out_sems,
):
    tokens, width = branch_ref.shape
    parts = slope_ref.shape[1] // width
    given = [
        (branch_hbm, branch_ref),
        (hidden_hbm, total),
        (normed_hbm, normed_ref),
        (inv_hbm, inv_ref),
        (gain_hbm, gain_ref),
        (mixing_hbm, mixing_ref),
    ]
    copies = [
        pltpu.make_async_copy(source, target, in_sems.at[i])
        for i, (source, target) in enumerate(given)
    ]
    part_copies = []
    for part in range(parts):
        at = pl.ds(part * width, width)
        pairs = [
            (narrowing_hbm.at[at], narrowing_ref.at[at]),
            (slope_hbm.at[:, at], slope_ref.at[:, at]),
            (widening_hbm.at[:, at], widening_ref.at[:, at]),
        ]
        part_copies.append(
            [
                pltpu.make_async_copy(source, target, part_sems.at[part, i])
                for i, (source, target) in enumerate(pairs)
            ]
        )
    start_all(copies[:1] + part_copies[0] + part_copies[1] + copies[1:2])
    outward = []

    def write(source, target):
        copy = pltpu.make_async_copy(source, target, out_sems.at[len(outward)])
        copy.start()
        outward.append(copy)

    def columns_of(part):
        return slice(part * width, (part + 1) * width)

    def product(part):
        return dot_nt(branch_ref[...], narrowing_ref[columns_of(part)])

    wait_all(copies[:1] + part_copies[0][:1])
    waiting = product(0)
    for part in range(parts):
        if part + 2 < parts:
            start_all(part_copies[part + 2])
        elif part + 2 == parts:
            start_all(copies[2:])
        if part == 0:
            wait_all(copies[1:2])
        wait_all(part_copies[part][1:])
        grad_act = waiting
        if part + 1 < parts:
            wait_all(part_copies[part + 1][:1])
            waiting = product(part + 1)
        columns = columns_of(part)
        grad_pre = (grad_act * widen(slope_ref[:, columns])).astype(jnp.bfloat16)
        grad_pre_ref[:, columns] = grad_pre
        bias_ref[:, columns] = jnp.sum(widen(grad_pre), axis=0, keepdims=True)
        total[...] += dot_nt(grad_pre, widening_ref[:, columns])
        at = pl.ds(part * width, width)
        write(grad_pre_ref.at[:, at], grad_pre_hbm.at[:, at])
    wait_all(copies[2:])
    chunk = min(tokens, 128)
    gain = as_row(gain_ref)
    gain_sum = jnp.zeros((1, width), jnp.float32)
    shift_sum = jnp.zeros((1, width), jnp.float32)
    bias_sum = jnp.zeros((1, width), jnp.float32)
    for row in range(0, tokens, chunk):
        grad_out = total[row : row + chunk]
        normed = normed_ref[row : row + chunk]
        gain_sum = gain_sum + jnp.sum(grad_out * normed, axis=0, keepdims=True)
        shift_sum = shift_sum + jnp.sum(grad_out, axis=0, keepdims=True)
        grad_hidden = standardize_back(normed, inv_ref[row : row + chunk], grad_out * gain)
        grad_hidden_ref[row : row + chunk] = grad_hidden
        low = grad_hidden.astype(jnp.bfloat16)
        grad_branch_ref[row : row + chunk] = low
        bias_sum = bias_sum + jnp.sum(widen(low), axis=0, keepdims=True)
        grad_attn_ref[row : row + chunk] = dot_nt(low, mixing_ref[...]).astype(jnp.bfloat16)
    write(grad_branch_ref, grad_branch_hbm)
    write(grad_attn_ref, grad_attn_hbm)
    write(grad_hidden_ref, grad_hidden_hbm)
    sums_ref[...] = jnp.concatenate([bias_sum, gain_sum, shift_sum], axis=0)
    wait_all(outward)


def before_step(branch, slope, narrowing, widening, hidden, normed, inv, gain, mixing):
    tokens, hidden_units = slope.shape
    width = branch.shape[1]
    parts = hidden_units // width
    low, full = jnp.bfloat16, jnp.float32
    return pl.pallas_call(
        before_kernel,
        in_specs=[any_spec()] * 9,
        out_specs=[any_spec(), vmem_spec()] + [any_spec()] * 3 + [vmem_spec()],
        out_shape=[
            jax.ShapeDtypeStruct((tokens, hidden_units), low),
            jax.ShapeDtypeStruct((1, hidden_units), full),
            jax.ShapeDtypeStruct((tokens, width), full),
            jax.ShapeDtypeStruct((tokens, width), low),
            jax.ShapeDtypeStruct((tokens, width), low),
            jax.ShapeDtypeStruct((3, width), full),
        ],
        scratch_shapes=[
            pltpu.VMEM(branch.shape, low),
            pltpu.VMEM(slope.shape, low),
            pltpu.VMEM(narrowing.shape, low),
            pltpu.VMEM(widening.shape, low),
            pltpu.VMEM((tokens, width), full),
            pltpu.VMEM(normed.shape, full),
            pltpu.VMEM(inv.shape, full),
            pltpu.VMEM(gain.shape, low),
            pltpu.VMEM(mixing.shape, low),
            pltpu.VMEM(slope.shape, low),
            pltpu.VMEM((tokens, width), full),
            pltpu.VMEM((tokens, width), low),
            pltpu.VMEM((tokens, width), low),
            pltpu.SemaphoreType.DMA((6,)),
            pltpu.SemaphoreType.DMA((parts, 3)),
            pltpu.SemaphoreType.DMA((parts + 3,)),
        ],
        compiler_params=compiler_params(),
        cost_estimate=cost(11),
        name="before_step",
    )(branch, slope, narrowing, widening, hidden, normed, inv, gain, mixing)


def side_copies(own_ref, other_ref, at, count, target, sems):
    tokens = own_ref.shape[2]
    return [
        pltpu.make_async_copy(
            source.at[:, pl.ds(at, count)],
            target.at[:, :, pl.ds(i * tokens, tokens)],
            sems.at[i],
        )
        for i, source in enumerate((own_ref, other_ref))
    ]


def flat(ref):
    places, rows, tokens = ref.shape
    return ref[...].reshape(places * rows, tokens)


def store_places(product, first, parts, target):
    rows = target.shape[2]
    low = product.astype(jnp.bfloat16)
    for place in range(low.shape[0] // rows // parts):
        for tile in range(low.shape[1] // LANES):
            for part in range(parts):
                row = (place * parts + part) * rows
                target[first + place, tile * parts + part] = low[
                    row : row + rows, tile * LANES : (tile + 1) * LANES
                ]


def outer_kernel(
    own_ref,
    other_ref,
    branch_own_ref,
    branch_other_ref,
    keep_x,
    send_x,
    keep_z,
    send_z,
    left_x,
    left_z,
    right,
    made_x,
    made_z,
    left_sems,
    right_sems,
    out_sems,
):
    places, count, _ = left_x.shape
    tokens = branch_own_ref.shape[0]
    half = places // 2
    parts = count // made_x.shape[2]
    copies = [
        pltpu.make_async_copy(source, right.at[pl.ds(i * tokens, tokens)], right_sems.at[i])
        for i, source in enumerate((branch_own_ref, branch_other_ref))
    ]
    copies_x = side_copies(own_ref, other_ref, 0, count, left_x, left_sems.at[0])
    copies_z = side_copies(own_ref, other_ref, count, count, left_z, left_sems.at[1])
    start_all(copies + copies_x + copies_z)
    wait_all(copies + copies_x)
    units = [
        (left_x, made_x, half, send_x),
        (left_x, made_x, 0, keep_x),
        (left_z, made_z, half, send_z),
        (left_z, made_z, 0, keep_z),
    ]

    def product(n):
        left, _, first, _ = units[n]
        if n == 2:
            wait_all(copies_z)
        return dot_nn(
            left[first : first + half].reshape(half * count, 2 * tokens), right[...]
        )

    outward = []
    waiting = product(0)
    for n, (_, made, first, target) in enumerate(units):
        current = waiting
        if n + 1 < len(units):
            waiting = product(n + 1)
        store_places(current, first, parts, made)
        copy = pltpu.make_async_copy(made.at[pl.ds(first, half)], target, out_sems.at[n])
        copy.start()
        outward.append(copy)
    wait_all(outward)


def outer_step(own, other, branch_own, branch_other, count):
    places, _, tokens = own.shape
    width = branch_own.shape[1]
    parts = 2
    rows = count // parts
    low = jnp.bfloat16
    blocks = width // LANES * parts
    shape = jax.ShapeDtypeStruct((places // 2, blocks, rows, LANES), low)
    return pl.pallas_call(
        outer_kernel,
        in_specs=[any_spec(), got_spec(), any_spec(), got_spec()],
        out_specs=[any_spec()] * 4,
        out_shape=[shape] * 4,
        scratch_shapes=[
            pltpu.VMEM((places, count, 2 * tokens), low),
            pltpu.VMEM((places, count, 2 * tokens), low),
            pltpu.VMEM((2 * tokens, width), low),
            pltpu.VMEM((places, blocks, rows, LANES), low),
            pltpu.VMEM((places, blocks, rows, LANES), low),
            pltpu.SemaphoreType.DMA((2, 2)),
            pltpu.SemaphoreType.DMA((2,)),
            pltpu.SemaphoreType.DMA((4,)),
        ],
        compiler_params=compiler_params(),
        cost_estimate=cost(5),
        name="outer_step",
    )(own, other, branch_own, branch_other)


def inner_kernel(
    at,
    side_ref,
    own_ref,
    other_ref,
    grad_own_hbm,
    grad_other_hbm,
    keep_x,
    send_x,
    keep_y,
    send_y,
    left,
    right,
    made_x,
    made_y,
    left_sems,
    in_sems,
    out_sems,
):
    tokens, hidden_units = grad_own_hbm.shape
    places, rows, _ = left.shape
    half = places // 2
    parts = 4
    width = hidden_units // parts
    tiles = width // LANES
    side = side_ref[0]
    left_copies = side_copies(own_ref, other_ref, at, rows, left, left_sems)
    right_copies = []
    for part in range(parts):
        columns = pl.ds(part * width, width)
        right_copies.append(
            [
                pltpu.make_async_copy(
                    source.at[:, columns],
                    right.at[pl.ds(i * tokens, tokens), columns],
                    in_sems.at[part, i],
                )
                for i, source in enumerate((grad_own_hbm, grad_other_hbm))
            ]
        )
    start_all(left_copies)
    for copies in right_copies:
        start_all(copies)
    outward = []

    def write(source, target):
        copy = pltpu.make_async_copy(source, target, out_sems.at[len(outward)])
        copy.start()
        outward.append(copy)

    def weight(part):
        return dot_nn(flat(left), right[:, part * width : (part + 1) * width])

    def store_weight(part, product):
        low = product.astype(jnp.bfloat16)
        for place in range(places):
            for tile in range(tiles):
                block = low[place * rows : (place + 1) * rows, tile * LANES : (tile + 1) * LANES]
                if part < parts // 2:
                    made_x[place, part * tiles + tile] = block
                else:
                    made_y[jnp.bitwise_xor(side, part - parts // 2), place, tile] = block
        if part == parts // 2 - 1:
            write(made_x.at[pl.ds(half, half)], send_x)
            write(made_x.at[pl.ds(0, half)], keep_x)
        if part == parts - 1:
            write(made_y.at[1], send_y)
            write(made_y.at[0], keep_y)

    wait_all(left_copies)
    products = []
    for part in range(parts):
        wait_all(right_copies[part])
        products.append(weight(part))
        if part >= 1:
            store_weight(part - 1, products.pop(0))
    store_weight(parts - 1, products.pop(0))
    wait_all(outward)


def inner_step(side, own, other, at, rows, grad_own, grad_other):
    places, _, tokens = own.shape
    hidden_units = grad_own.shape[1]
    tiles = hidden_units // 4 // LANES
    half = places // 2
    low = jnp.bfloat16
    shape_x = jax.ShapeDtypeStruct((half, 2 * tiles, rows, LANES), low)
    shape_y = jax.ShapeDtypeStruct((places, tiles, rows, LANES), low)
    return pl.pallas_call(
        functools.partial(inner_kernel, at),
        in_specs=[smem_spec(), any_spec(), got_spec(), any_spec(), got_spec()],
        out_specs=[any_spec()] * 4,
        out_shape=[shape_x, shape_x, shape_y, shape_y],
        scratch_shapes=[
            pltpu.VMEM((places, rows, 2 * tokens), low),
            pltpu.VMEM((2 * tokens, hidden_units), low),
            pltpu.VMEM((places, 2 * tiles, rows, LANES), low),
            pltpu.VMEM((2, places, tiles, rows, LANES), low),
            pltpu.SemaphoreType.DMA((2,)),
            pltpu.SemaphoreType.DMA((4, 2)),
            pltpu.SemaphoreType.DMA((4,)),
        ],
        compiler_params=compiler_params(),
        cost_estimate=cost(5),
        name="inner_step",
    )(side, own, other, grad_own, grad_other)


def attend_back_kernel(
    segments,
    sizes_ref,
    query_ref,
    key_ref,
    key_t_ref,
    value_ref,
    lse_ref,
    grad_ref,
    grads_ref,
    sums_ref,
    fill,
    query_t,
    total_key,
    total_value,
):
    length, wide = query_ref.shape
    ranges = band(length)
    step = pl.program_id(0)

    @pl.when(step == 0)
    def _():
        for i, (query_at, query_end, key_at, key_end) in enumerate(ranges):
            fill[i] = mask_of(sizes_ref, segments, query_at, query_end, key_at, key_end)

    total_key[...] = jnp.zeros_like(total_key)
    total_value[...] = jnp.zeros_like(total_value)
    lane = lax.broadcasted_iota(jnp.int32, (1, LANES), 1)
    units = [(at, i) for at in range(wide // HD) for i in range(len(ranges))]

    def lanes_of(at):
        first = at * HD // LANES * LANES
        return slice(first, first + LANES), (lane // HD) == (at * HD - first) // HD

    def products(unit):
        at, i = unit
        query_at, query_end, key_at, key_end = ranges[i]
        lanes, head = lanes_of(at)
        query = jnp.where(head, query_ref[query_at:query_end, lanes], 0)
        grad = jnp.where(head, grad_ref[query_at:query_end, lanes], 0)
        scores = dot_nt(key_ref[key_at:key_end, lanes], query) + fill[i]
        return scores, dot_nt(value_ref[key_at:key_end, lanes], grad)

    def back(unit, scores, grad_probs):
        at, i = unit
        query_at, query_end, key_at, key_end = ranges[i]
        probs = jnp.exp(scores - lse_ref[0, at : at + 1, query_at:query_end])
        inner = jnp.sum(grad_probs * probs, axis=0, keepdims=True)
        return probs.astype(jnp.bfloat16), (probs * (grad_probs - inner)).astype(jnp.bfloat16)

    def finish(unit, probs, grad_scores):
        at, i = unit
        query_at, query_end, key_at, key_end = ranges[i]
        lanes, head = lanes_of(at)
        query = jnp.where(head, query_ref[query_at:query_end, lanes], 0)
        grad = jnp.where(head, grad_ref[query_at:query_end, lanes], 0)
        total_value[key_at:key_end, lanes] += dot_nn(probs, grad)
        total_key[key_at:key_end, lanes] += dot_nn(grad_scores, query)
        query_t[at * HD : (at + 1) * HD, query_at:query_end] = dot_nn(
            key_t_ref[at * HD : (at + 1) * HD, key_at:key_end], grad_scores
        )

    ahead = 2
    waiting = [products(unit) for unit in units[:ahead]]
    done = []
    for n, unit in enumerate(units):
        if n + ahead < len(units):
            waiting.append(products(units[n + ahead]))
        done.append((unit, *back(unit, *waiting.pop(0))))
        if len(done) > 1:
            finish(*done.pop(0))
    for item in done:
        finish(*item)
    grad_query = (query_t[...] * HD ** (-0.5)).T.astype(jnp.bfloat16)
    grad_value = total_value[...].astype(jnp.bfloat16)
    grads_ref[0] = grad_query
    grads_ref[1] = total_key[...].astype(jnp.bfloat16)
    grads_ref[2] = grad_value
    sums_ref[...] = jnp.concatenate(
        [
            jnp.sum(widen(grad_query), axis=0, keepdims=True),
            jnp.sum(widen(grad_value), axis=0, keepdims=True),
        ],
        axis=0,
    )


def attend_back_step(sizes, query, key, key_t, value, lse, grad):
    tokens, width = query.shape
    heads_here = lse.shape[1]
    wide = heads_here * HD
    columns = pl.BlockSpec((tokens, wide), lambda i: (0, i))
    query_at, query_end, key_at, key_end = band(tokens)[0]
    return pl.pallas_call(
        functools.partial(attend_back_kernel, sizes.shape[1]),
        grid=(width // wide,),
        in_specs=[
            smem_spec(),
            columns,
            columns,
            pl.BlockSpec((wide, tokens), lambda i: (i, 0)),
            columns,
            pl.BlockSpec((1, heads_here, tokens), lambda i: (i, 0, 0)),
            columns,
        ],
        out_specs=[
            pl.BlockSpec((3, tokens, wide), lambda i: (0, 0, i)),
            pl.BlockSpec((2, wide), lambda i: (0, i)),
        ],
        out_shape=[
            jax.ShapeDtypeStruct((3, tokens, width), jnp.bfloat16),
            jax.ShapeDtypeStruct((2, width), jnp.float32),
        ],
        scratch_shapes=[
            pltpu.VMEM((2, key_end - key_at, query_end - query_at), jnp.float32),
            pltpu.VMEM((wide, tokens), jnp.float32),
            pltpu.VMEM((tokens, wide), jnp.float32),
            pltpu.VMEM((tokens, wide), jnp.float32),
        ],
        compiler_params=compiler_params(),
        cost_estimate=cost(8),
        name="attend_back_step",
    )(sizes, query, key, key_t, value, lse, grad)


def add_kernel(shape_of, *refs):
    counts, last = shape_of
    pairs = sum(counts) + last
    given, refs = refs[: 2 * pairs], refs[2 * pairs :]
    outputs = 2 * len(counts) + (1 if last else 0)
    targets, refs = refs[:outputs], refs[outputs:]
    local, refs = refs[: 2 * pairs], refs[2 * pairs :]
    made, refs = refs[:outputs], refs[outputs:]
    in_sems, out_sems = refs
    copies = [
        pltpu.make_async_copy(source, target, in_sems.at[n])
        for n, (source, target) in enumerate(zip(given, local))
    ]
    start_all(copies)
    outward = []

    def write(n):
        copy = pltpu.make_async_copy(made[n], targets[n], out_sems.at[n])
        copy.start()
        outward.append(copy)

    at = 0
    for item, count in enumerate(counts):
        kept, sent = made[2 * item], made[2 * item + 1]
        half = kept.shape[0]
        block = 0
        for _ in range(count):
            wait_all(copies[2 * at : 2 * at + 2])
            keep, got = local[2 * at], local[2 * at + 1]
            blocks = slice(block, block + keep.shape[1])
            sent[:, blocks] = (widen(keep[half:]) + widen(got[half:])).astype(sent.dtype)
            kept[:, blocks] = widen(keep[:half]) + widen(got[:half])
            block += keep.shape[1]
            at += 1
        write(2 * item + 1)
        write(2 * item)
    if last:
        mine = made[-1]
        block = 0
        for _ in range(last):
            wait_all(copies[2 * at : 2 * at + 2])
            keep, got = local[2 * at], local[2 * at + 1]
            blocks = slice(block, block + keep.shape[1])
            mine[blocks] = (widen(keep[0]) + widen(got[0])).astype(mine.dtype)
            block += keep.shape[1]
            at += 1
        write(outputs - 1)
    wait_all(outward)


def add_step(items, last=(), name="add_step"):
    given, shapes = [], []
    for pairs in items:
        for pair in pairs:
            given.extend(pair)
        places, _, rows, lanes = pairs[0][0].shape
        blocks = sum(keep.shape[1] for keep, _ in pairs)
        shape = (places // 2, blocks, rows, lanes)
        shapes.append((shape, jnp.float32))
        shapes.append((shape, pairs[0][1].dtype))
    for pair in last:
        given.extend(pair)
    if last:
        _, _, rows, lanes = last[0][0].shape
        blocks = sum(keep.shape[1] for keep, _ in last)
        shapes.append(((blocks, rows, lanes), jnp.bfloat16))
    results = pl.pallas_call(
        functools.partial(add_kernel, ([len(pairs) for pairs in items], len(last))),
        in_specs=[got_spec()] * len(given),
        out_specs=[any_spec()] * len(shapes),
        out_shape=[jax.ShapeDtypeStruct(shape, kind) for shape, kind in shapes],
        scratch_shapes=[pltpu.VMEM(item.shape, item.dtype) for item in given]
        + [pltpu.VMEM(shape, kind) for shape, kind in shapes]
        + [pltpu.SemaphoreType.DMA((len(given),)), pltpu.SemaphoreType.DMA((len(shapes),))],
        compiler_params=compiler_params(SMALL_BYTES),
        cost_estimate=cost(2),
        name=name,
    )(*given)
    halves = [(results[2 * n], results[2 * n + 1]) for n in range(len(items))]
    return halves + ([results[-1]] if last else [])


def split_vector(total, rows):
    places, _, count, lanes = total.shape
    parts = []
    for _ in range(3):
        low = total.astype(jnp.bfloat16)
        total = total - widen(low)
        parts.append(low)
    if rows > 3 * count:
        parts.append(jnp.zeros((places, 1, rows - 3 * count, lanes), jnp.bfloat16))
    return jnp.concatenate(parts, axis=2)


def join_vector(block, count):
    return sum(widen(block[..., i * count : (i + 1) * count, :]) for i in range(3))


def round_kernel(plan, passes, inputs, streams, *refs):
    given, refs = refs[:inputs], refs[inputs:]
    outputs = len(plan) - sum(1 for item in plan if item[5]) + streams
    targets, refs = refs[:outputs], refs[outputs:]
    local, refs = refs[:inputs], refs[inputs:]
    made, (in_sems, out_sems) = refs[:outputs], refs[outputs:]
    sent_to = made[outputs - streams :]
    copies = []
    passed = {}
    for n, source in enumerate(given):
        if n in passes:
            stream, at = passes[n]
            target = sent_to[stream].at[pl.ds(at, source.shape[0])]
            passed.setdefault(stream, []).append(n)
        else:
            target = local[n]
        copies.append(pltpu.make_async_copy(source, target, in_sems.at[n]))
    start_all(copies)
    outward = []
    waited = set()

    def write(n):
        copy = pltpu.make_async_copy(made[n], targets[n], out_sems.at[n])
        copy.start()
        outward.append(copy)

    def need(n):
        if n not in waited:
            waited.add(n)
            copies[n].wait()

    kept_at = 0
    for keep_at, got_at, begin, stream, at, whole, vector in plan:
        keep = local[keep_at]
        places, blocks, rows, lanes = keep.shape
        need(keep_at)
        if got_at is not None:
            need(got_at)
        total = widen(keep[...])
        if vector and keep.dtype == jnp.bfloat16:
            total = join_vector(keep[...], 8)
        if got_at is not None:
            got = local[got_at][begin : begin + places * blocks]
            if vector:
                total = total + join_vector(got, 8)[:, None]
            else:
                total = total + widen(got.reshape(keep.shape))
        target = sent_to[stream]
        if not whole:
            made[kept_at][...] = total[: places // 2]
            write(kept_at)
            kept_at += 1
            total = total[places // 2 :]
        if vector:
            send = split_vector(total, target.shape[1])
        else:
            send = total.astype(jnp.bfloat16)
        count = send.shape[0] * blocks
        target[at : at + count] = send.reshape((count,) + target.shape[1:])
    for n in range(inputs):
        need(n)
    for n in range(outputs - streams, outputs):
        write(n)
    wait_all(outward)


def round_step(chains, received, rows, limit):
    given, kept, plan, passes = [], [], [], {}
    at_of, lengths = {}, {}
    stream_keys = list(received)
    given = [received[key] for key in stream_keys]
    hops = []
    for chain in chains.values():
        if chain["hops"] and chain["hops"][0] not in hops:
            hops.append(chain["hops"][0])
    shapes = []
    for name, chain in chains.items():
        if not chain["hops"]:
            continue
        hop = chain["hops"][0]
        at = lengths.get(hop, 0)
        at_of[name] = at
        if chain["send"] is not None:
            given.append(chain["send"].reshape((-1,) + chain["send"].shape[-2:]))
            passes[len(given) - 1] = (hops.index(hop), at)
            lengths[hop] = at + given[-1].shape[0]
            continue
        keep = chain["keep"]
        given.append(keep)
        keep_at = len(given) - 1
        got_at, begin = None, 0
        if chain["got"] is not None:
            got_at, begin = stream_keys.index(chain["got"][0]), chain["got"][1]
        places, blocks = keep.shape[:2]
        whole = places == 1
        plan.append((keep_at, got_at, begin, hops.index(hop), at, whole, chain["vector"]))
        lengths[hop] = at + (blocks if whole else places // 2 * blocks)
        if not whole:
            shapes.append(((places // 2,) + keep.shape[1:], jnp.float32))
            kept.append(name)
    shapes = shapes + [((lengths[hop], rows, LANES), jnp.bfloat16) for hop in hops]
    results = pl.pallas_call(
        functools.partial(round_kernel, plan, passes, len(given), len(hops)),
        in_specs=[got_spec()] * len(given),
        out_specs=[any_spec()] * len(shapes),
        out_shape=[jax.ShapeDtypeStruct(shape, kind) for shape, kind in shapes],
        scratch_shapes=[
            pltpu.VMEM((8, LANES) if n in passes else item.shape, item.dtype)
            for n, item in enumerate(given)
        ]
        + [pltpu.VMEM(shape, kind) for shape, kind in shapes]
        + [pltpu.SemaphoreType.DMA((len(given),)), pltpu.SemaphoreType.DMA((len(shapes),))],
        compiler_params=compiler_params(limit),
        cost_estimate=cost(3),
        name="round_step",
    )(*given)
    sent = dict(zip(hops, results[len(kept) :]))
    keeps = dict(zip(kept, results))
    for name, chain in chains.items():
        if not chain["hops"]:
            continue
        hop = chain["hops"].pop(0)
        at = at_of[name]
        if chain["send"] is not None:
            chain["send"] = None
        elif name in keeps:
            chain["keep"] = keeps[name]
        else:
            count = chain["keep"].shape[1]
            chain["keep"] = sent[hop][at : at + count][None]
        chain["got"] = (hop, at)
    return sent


def token_kernel(hidden_ref, grads_ref, question_ref, lookup_ref, content_ref, out_ref):
    out_ref[...] = (
        hidden_ref[...]
        + dot_nt(grads_ref[0], question_ref[...])
        + dot_nt(grads_ref[1], lookup_ref[...])
        + dot_nt(grads_ref[2], content_ref[...])
    )


def token_step(hidden, grads, question, lookup, content):
    tokens, width = hidden.shape
    wide = 2 * LANES
    weight = pl.BlockSpec((wide, width), lambda i: (i, 0))
    column = pl.BlockSpec((tokens, wide), lambda i: (0, i))
    return pl.pallas_call(
        token_kernel,
        grid=(width // wide,),
        in_specs=[column, pl.BlockSpec((3, tokens, width), lambda i: (0, 0, 0))] + [weight] * 3,
        out_specs=column,
        out_shape=jax.ShapeDtypeStruct((tokens, width), jnp.float32),
        compiler_params=compiler_params(),
        cost_estimate=cost(5),
        name="token_step",
    )(hidden, grads, question, lookup, content)


def attention_kernel(
    token_at,
    attn_at,
    places_z,
    side_ref,
    own_ref,
    other_ref,
    grads_own_ref,
    grads_other_ref,
    branch_own_ref,
    branch_other_ref,
    keep_x,
    send_x,
    keep_y,
    send_y,
    keep_z,
    send_z,
    token_left,
    attn_left,
    token_right,
    attn_right,
    made_x,
    made_y,
    made_z,
    left_sems,
    right_sems,
    out_sems,
):
    places, rows, _ = token_left.shape
    tokens = branch_own_ref.shape[0]
    wide = 2 * LANES
    left_copies = side_copies(own_ref, other_ref, token_at, rows, token_left, left_sems.at[0])
    attn_copies = side_copies(own_ref, other_ref, attn_at, rows, attn_left, left_sems.at[1])
    right_copies = []
    for chunk in range(3):
        columns = pl.ds(chunk * wide, wide)
        copies = []
        for core, (grads, branch) in enumerate(
            ((grads_own_ref, branch_own_ref), (grads_other_ref, branch_other_ref))
        ):
            token_rows = pl.ds(core * tokens, tokens)
            pairs = [
                (grads.at[i, :, columns], token_right.at[chunk, token_rows, pl.ds(i * wide, wide)])
                for i in range(3)
            ]
            pairs.append((branch.at[:, columns], attn_right.at[chunk, token_rows]))
            for i, (source, target) in enumerate(pairs):
                copies.append(
                    pltpu.make_async_copy(source, target, right_sems.at[chunk, 4 * core + i])
                )
        right_copies.append(copies)
    start_all(left_copies + right_copies[0][:3] + right_copies[0][4:7] + attn_copies)
    start_all(right_copies[0][3:4] + right_copies[0][7:] + right_copies[1] + right_copies[2])
    outward = []
    half = places // 2
    side = side_ref[0]
    for chunk in range(3):
        if chunk == 0:
            wait_all(left_copies + right_copies[0][:3] + right_copies[0][4:7])
        else:
            wait_all(right_copies[chunk])
        token_product = dot_nn(flat(token_left), token_right[chunk]).astype(jnp.bfloat16)
        if chunk == 0:
            wait_all(attn_copies + right_copies[0][3:4] + right_copies[0][7:])
        attn_product = dot_nn(flat(attn_left), attn_right[chunk]).astype(jnp.bfloat16)
        products = [
            token_product[:, :wide],
            attn_product,
            token_product[:, wide : 2 * wide],
            token_product[:, 2 * wide :],
        ]
        for which, product in enumerate(products):
            for place in range(places):
                for tile in range(2):
                    block = product[
                        place * rows : (place + 1) * rows, tile * LANES : (tile + 1) * LANES
                    ]
                    if chunk == 0:
                        made_x[place, which * 2 + tile] = block
                    elif chunk == 1:
                        where = jnp.bitwise_xor(side, which // 2)
                        made_y[where, place, which % 2 * 2 + tile] = block
                    else:
                        made_z[places_z[place], which * 2 + tile] = block
        if chunk == 0:
            pairs = [(made_x.at[:half], keep_x), (made_x.at[half:], send_x)]
        elif chunk == 1:
            pairs = [(made_y.at[0], keep_y), (made_y.at[1], send_y)]
        else:
            pairs = [(made_z.at[:half], keep_z), (made_z.at[half:], send_z)]
        for source, target in pairs:
            copy = pltpu.make_async_copy(source, target, out_sems.at[len(outward)])
            copy.start()
            outward.append(copy)
    wait_all(outward)


def attention_step(
    side, own, other, token_at, attn_at, rows, places_z, grads, grads_other, branch, branch_other
):
    places, _, tokens = own.shape
    wide = 2 * LANES
    low = jnp.bfloat16
    half = places // 2
    shape = jax.ShapeDtypeStruct((half, 8, rows, LANES), low)
    shape_y = jax.ShapeDtypeStruct((places, 4, rows, LANES), low)
    return pl.pallas_call(
        functools.partial(attention_kernel, token_at, attn_at, places_z),
        in_specs=[smem_spec()] + [any_spec(), got_spec()] * 3,
        out_specs=[any_spec()] * 6,
        out_shape=[shape, shape, shape_y, shape_y, shape, shape],
        scratch_shapes=[
            pltpu.VMEM((places, rows, 2 * tokens), low),
            pltpu.VMEM((places, rows, 2 * tokens), low),
            pltpu.VMEM((3, 2 * tokens, 3 * wide), low),
            pltpu.VMEM((3, 2 * tokens, wide), low),
            pltpu.VMEM((places, 8, rows, LANES), low),
            pltpu.VMEM((2, places, 4, rows, LANES), low),
            pltpu.VMEM((places, 8, rows, LANES), low),
            pltpu.SemaphoreType.DMA((2, 2)),
            pltpu.SemaphoreType.DMA((3, 8)),
            pltpu.SemaphoreType.DMA((6,)),
        ],
        compiler_params=compiler_params(),
        cost_estimate=cost(6),
        name="attention_step",
    )(side, own, other, grads, grads_other, branch, branch_other)


def body(
    hidden_states_in,
    piece_sizes,
    matching_passage_number,
    softmax_sharpness,
    question_projection,
    question_offset,
    lookup_projection,
    content_projection,
    content_offset,
    mixing_result_projection,
    mixing_result_offset,
    mixing_layernorm_scale,
    mixing_layernorm_offset,
    widening_projection,
    widening_offset,
    narrowing_projection,
    narrowing_offset,
    perceptron_layernorm_scale,
    perceptron_layernorm_offset,
):
    rows_here, length, width = hidden_states_in.shape
    segments = piece_sizes.shape[1]
    per_device = segments // 2
    groups_y = lax.axis_size("gy")
    rows = width // groups_y
    inner_rows = widening_offset.shape[0] // groups_y
    gy_bits = powers_below(groups_y)
    order_x = gy_bits[1:]
    order_z = gy_bits[2:3] + gy_bits[1:2] + gy_bits[3:]
    here = lax.axis_index("gy").astype(jnp.int32).reshape(1)
    side = (lax.axis_index("gx").astype(jnp.int32) & 1).reshape(1)
    (
        queries,
        keys,
        keys_t,
        values,
        lse,
        normed_one,
        inv_one,
        slope,
        normed_two,
        inv_two,
        pooled,
        message,
        side_own,
        side_send,
    ) = forward_step(
        here,
        piece_sizes,
        matching_passage_number,
        place_masks(order_x),
        place_masks(order_z),
        [
            hidden_states_in[0],
            question_projection,
            lookup_projection,
            content_projection,
            mixing_result_projection,
            widening_projection,
            narrowing_projection,
            question_offset,
            content_offset,
            mixing_result_offset,
            mixing_layernorm_scale,
            mixing_layernorm_offset,
            widening_offset,
            narrowing_offset,
            perceptron_layernorm_scale,
            perceptron_layernorm_offset,
        ],
    )
    gathered, numbers_of, place, side_other = gather_blocks(
        message, swap_with(side_send, "gy", 1)
    )
    numbers = (numbers_of[:, None] * per_device + np.arange(per_device)[None, :]).reshape(1, -1)
    loss_out, grad_hidden_two, branch_two, sums_two = loss_step(
        place.astype(jnp.int32).reshape(1),
        piece_sizes,
        softmax_sharpness,
        jnp.asarray(numbers, jnp.int32),
        gathered,
        pooled,
        normed_two,
        inv_two,
        perceptron_layernorm_scale,
    )
    branch_two_other = swap_with(branch_two, "gy", 1)
    outer_keep_x, outer_send_x, outer_keep_z, outer_send_z = outer_step(
        side_own, side_other, branch_two, branch_two_other, inner_rows // 2
    )
    outer_send_x, outer_send_z, branch_two = tie(outer_send_x, outer_send_z, branch_two)
    outer_got_x = swap_with(outer_send_x, "gy", order_x[0])
    outer_got_z = swap_with(outer_send_z, "gy", order_z[0])
    grad_pre, grad_b_inner, grad_hidden_one, branch_one, grad_attn, sums_one = before_step(
        branch_two,
        slope,
        narrowing_projection,
        widening_projection,
        grad_hidden_two,
        normed_one,
        inv_one,
        mixing_layernorm_scale,
        mixing_result_projection,
    )
    outer_got_x, outer_got_z, grad_pre, branch_one, grad_attn = tie(
        outer_got_x, outer_got_z, grad_pre, branch_one, grad_attn
    )
    grad_pre_other = swap_with(grad_pre, "gy", 1)
    branch_one_other = swap_with(branch_one, "gy", 1)
    (outer_keep_x, outer_send_x), (outer_keep_z, outer_send_z) = add_step(
        [[(outer_keep_x, outer_got_x)], [(outer_keep_z, outer_got_z)]]
    )
    outer_send_x, outer_send_z, grad_attn = tie(outer_send_x, outer_send_z, grad_attn)
    outer_got_x = swap_with(outer_send_x, "gy", order_x[1])
    outer_got_z = swap_with(outer_send_z, "gy", order_z[1])
    grads, sums_attn = attend_back_step(
        piece_sizes,
        queries,
        keys,
        keys_t,
        values,
        lse,
        grad_attn,
    )
    grads, grad_pre_other, branch_one_other, outer_got_x, outer_got_z = tie(
        grads, grad_pre_other, branch_one_other, outer_got_x, outer_got_z
    )
    grads_other = swap_with(grads, "gy", 1)
    (outer_keep_x, outer_send_x), (outer_keep_z, outer_send_z) = add_step(
        [[(outer_keep_x, outer_got_x)], [(outer_keep_z, outer_got_z)]]
    )
    outer_got_x = swap_with(outer_send_x, "gy", order_x[2])
    outer_got_z = swap_with(outer_send_z, "gy", order_z[2])
    inner_keep_x, inner_send_x, inner_keep_y, inner_send_y = inner_step(
        side, side_own, side_other, inner_rows, rows, grad_pre, grad_pre_other
    )
    gx_bits = powers_below(lax.axis_size("gx"))
    inner_send_x, inner_send_y, grads_other = tie(inner_send_x, inner_send_y, grads_other)
    inner_got_x = swap_with(inner_send_x, "gy", order_x[0])
    inner_got_y = swap_with(inner_send_y, "gx", 1)
    masks_x, masks_z = place_masks(order_x), place_masks(order_z)
    attn_keep_x, attn_send_x, attn_keep_y, attn_send_y, attn_keep_z, attn_send_z = attention_step(
        side,
        side_own,
        side_other,
        inner_rows + rows,
        inner_rows + 2 * rows,
        rows,
        [masks_z.index(mask) for mask in masks_x],
        grads,
        grads_other,
        branch_one,
        branch_one_other,
    )
    attn_got_x = swap_with(attn_send_x, "gy", order_x[0])
    attn_got_y = swap_with(attn_send_y, "gx", 1)
    attn_got_z = swap_with(attn_send_z, "gy", order_z[0])
    attn_keep_x, sums_attn = tie(attn_keep_x, sums_attn)
    vectors = jnp.concatenate([sums_attn, sums_one, sums_two], axis=0)
    vectors = vectors.reshape(8, groups_y, rows).transpose(1, 0, 2).reshape(groups_y, 8 * rows)
    vectors = jnp.concatenate([vectors, grad_b_inner.reshape(groups_y, -1)], axis=1)
    used = vectors.shape[1]
    vectors = jnp.pad(vectors, ((0, 0), (0, 8 * LANES - used)))
    vectors = vectors.reshape((2,) * len(gy_bits) + (8 * LANES,))
    for axis, bit in enumerate(reversed(gy_bits)):
        high = (lax.axis_index("gy") & bit) != 0
        vectors = jnp.where(high, jnp.flip(vectors, axis=axis), vectors)
    vectors = vectors.transpose(tuple(reversed(range(len(gy_bits)))) + (len(gy_bits),))
    vectors = vectors.reshape(2, groups_y // 2, 1, 8, LANES)
    vector_got = swap_with(vectors[1], "gy", gy_bits[0])
    gx_hops = [("gx", bit) for bit in gx_bits]
    hops_x = [("gy", bit) for bit in order_x]
    hops_z = [("gy", bit) for bit in order_z]
    hops_y = gx_hops[:1] + hops_x + gx_hops[1:] + gx_hops[:1]

    def chain(keep, got, send, hops, vector=False):
        return {
            "keep": keep,
            "got": got,
            "send": send,
            "hops": list(hops),
            "vector": vector,
        }

    chains = {
        "inner_x": chain(inner_keep_x, ("inner_x", 0), None, hops_x[1:] + gx_hops),
        "inner_y": chain(inner_keep_y, ("inner_y", 0), None, hops_y[1:]),
        "outer_x": chain(outer_keep_x, ("outer_x", 0), None, hops_x[3:] + gx_hops),
        "outer_z": chain(outer_keep_z, ("outer_z", 0), None, hops_z[3:] + gx_hops),
    }
    received = {
        "inner_x": inner_got_x,
        "inner_y": inner_got_y,
        "outer_x": outer_got_x,
        "outer_z": outer_got_z,
    }
    received = {key: item.reshape((-1,) + item.shape[-2:]) for key, item in received.items()}
    finals = {}

    def finish():
        for name, item in chains.items():
            if not item["hops"] and name not in finals:
                hop, at = item["got"]
                count = item["keep"].shape[1]
                finals[name] = (item["keep"][0], received[hop][at : at + count])

    sent = round_step(chains, received, rows, VMEM_BYTES)
    keys = list(sent)
    *items, grads = tie(*[sent[key] for key in keys], grads)
    items = [swap_with(item, key[0], key[1]) for item, key in zip(items, keys)]
    grad_tokens = token_step(
        grad_hidden_one, grads, question_projection, lookup_projection, content_projection
    )
    *items, attn_got_x, attn_got_y, attn_got_z, grad_tokens, vector_got = tie(
        *items, attn_got_x, attn_got_y, attn_got_z, grad_tokens, vector_got
    )
    received = dict(zip(keys, items))
    finish()
    begun = {"attn_x": attn_got_x, "attn_y": attn_got_y, "attn_z": attn_got_z}
    for name, item in begun.items():
        received[name] = item.reshape((-1,) + item.shape[-2:])
    vector_hops = [("gy", bit) for bit in gy_bits[1:]] + gx_hops
    chains["vector"] = chain(vectors[0] + vector_got, None, None, vector_hops, True)
    chains["attn_x"] = chain(attn_keep_x, ("attn_x", 0), None, hops_x[1:] + gx_hops)
    chains["attn_y"] = chain(attn_keep_y, ("attn_y", 0), None, hops_y[1:])
    chains["attn_z"] = chain(attn_keep_z, ("attn_z", 0), None, hops_z[1:] + gx_hops)
    limit = SMALL_BYTES
    while any(item["hops"] for item in chains.values()):
        sent = round_step(chains, received, rows, limit)
        limit = SMALL_BYTES
        keys = list(sent)
        items = tie(*[swap_with(sent[key], key[0], key[1]) for key in keys])
        received = dict(zip(keys, items))
        finish()

    def summed(name):
        mine, other = finals[name]
        return widen(mine) + widen(other)

    def side_by_side(name):
        mine, other = finals[name]
        high = (lax.axis_index("gx") & 1) != 0
        return widen(
            jnp.concatenate([jnp.where(high, other, mine), jnp.where(high, mine, other)], axis=0)
        )

    vectors = sum(join_vector(item, 8) for item in finals["vector"])
    vectors = vectors.reshape(1, 8 * LANES)[:, :used]
    outer_x, outer_z = summed("outer_x"), summed("outer_z")
    attn_x, attn_y, attn_z = summed("attn_x"), side_by_side("attn_y"), summed("attn_z")
    inner_sums = jnp.concatenate([summed("inner_x"), side_by_side("inner_y")], axis=0)
    vector_sums = vectors[0]
    b_query, b_value, b_output, gain_attn, shift_attn, b_outer, gain_ffn, shift_ffn = [
        vector_sums[i * rows : (i + 1) * rows] for i in range(8)
    ]
    grad_w_query, grad_w_output, grad_w_key, grad_w_value = [
        jnp.concatenate(
            [part[2 * i + tile] for part in (attn_x, attn_y, attn_z) for tile in range(2)], axis=1
        )
        for i in range(4)
    ]
    grad_w_outer = jnp.concatenate([share_of(outer_x, width), share_of(outer_z, width)], axis=0)
    return (
        loss_out.reshape(1),
        pooled[None],
        grad_tokens.reshape(rows_here, length, width),
        grad_w_query,
        b_query,
        grad_w_key,
        grad_w_value,
        b_value,
        grad_w_output,
        b_output,
        gain_attn,
        shift_attn,
        share_of(inner_sums, widening_offset.shape[0]),
        vector_sums[8 * rows :],
        grad_w_outer,
        b_outer,
        gain_ffn,
        shift_ffn,
    )


def solution(mesh):
    return jax.shard_map(
        body,
        mesh=mesh,
        in_specs=(
            P(("gx", "gy"), None, None),
            P(("gx", "gy"), None),
            P(("gx", "gy")),
            P(),
            P(),
            P(),
            P(),
            P(),
            P(),
            P(),
            P(),
            P(),
            P(),
            P(),
            P(),
            P(),
            P(),
            P(),
            P(),
        ),
        out_specs=(
            P(),
            P(("gx", "gy"), None, None),
            P(("gx", "gy"), None, None),
            P("gy", None),
            P("gy"),
            P("gy", None),
            P("gy", None),
            P("gy"),
            P("gy", None),
            P("gy"),
            P("gy"),
            P("gy"),
            P("gy", None),
            P("gy"),
            P("gy", None),
            P("gy"),
            P("gy"),
            P("gy"),
        ),
        check_vma=False,
    )
```

```python
import functools

import jax
import jax.numpy as jnp
import numpy as np
from jax import lax
from jax.experimental import pallas as pl
from jax.experimental.pallas import tpu as pltpu
from jax.sharding import PartitionSpec as P

HEADS = 12
HD = 64
LANES = 128
VMEM_BYTES = 60 * 1024 * 1024
SMALL_BYTES = 24 * 1024 * 1024

EPS_NORM = 1e-12
EPS_UNIT = 1e-06
NEG_FILL = -1e30


def standardize(hidden):
    center = hidden - jnp.mean(hidden, axis=-1, keepdims=True)
    inv_scale = lax.rsqrt(jnp.mean(center * center, axis=-1, keepdims=True) + EPS_NORM)
    return (center * inv_scale, inv_scale)


def standardize_back(normed, inv_scale, grad_normed):
    mean_grad = jnp.mean(grad_normed, axis=-1, keepdims=True)
    mean_both = jnp.mean(grad_normed * normed, axis=-1, keepdims=True)
    return inv_scale * (grad_normed - mean_grad - normed * mean_both)


def widen(value):
    return value.astype(jnp.float32)


def powers_below(count):
    bits = []
    bit = 1
    while bit < count:
        bits.append(bit)
        bit *= 2
    return bits


def place_masks(bits):
    masks = [0]
    for bit in reversed(bits):
        masks = masks + [mask ^ bit for mask in masks]
    return masks


def swap_with(value, axis, bit):
    count = lax.axis_size(axis)
    return lax.ppermute(value, axis, [(i, i ^ bit) for i in range(count)])


def tie(*values):
    return lax.optimization_barrier(values)


def gather_steps():
    gy = powers_below(lax.axis_size("gy"))
    far = [("gy", bit) for bit in reversed(gy[2:])]
    near = [("gy", bit) for bit in reversed(gy[:2])]
    return far + [("gx", bit) for bit in powers_below(lax.axis_size("gx"))] + near


def gather_blocks(block, beside):
    groups_y = lax.axis_size("gy")
    devices = groups_y * lax.axis_size("gx")
    steps = gather_steps()
    numbers = [bit * (groups_y if axis == "gx" else 1) for axis, bit in steps]
    groups = [numbers[at : min(at + 2, len(steps) - 1)] for at in range(0, len(steps) - 1, 2)]
    groups.append(numbers[-1:])
    gathered = block[None]
    number = np.zeros((1,), np.int32)
    for group, bits in enumerate(groups):
        if group == 2:
            gathered, beside = tie(gathered, beside)
        masks = [0]
        for bit in bits:
            masks = masks + [mask ^ bit for mask in masks]
        parts = [gathered] + [
            lax.ppermute(gathered, ("gx", "gy"), [(i, i ^ mask) for i in range(devices)])
            for mask in masks[1:]
        ]
        gathered = jnp.concatenate(parts, axis=0)
        number = np.concatenate([number + mask for mask in masks])
    place = 0
    for step, (axis, bit) in enumerate(steps):
        place = place + jnp.where((lax.axis_index(axis) & bit) != 0, 1 << step, 0)
    return gathered, number, place, beside


def share_of(blocks, columns):
    tiles = columns // LANES
    parts = blocks.shape[0] // tiles
    return jnp.concatenate(
        [
            jnp.concatenate([blocks[tile * parts + part] for tile in range(tiles)], axis=1)
            for part in range(parts)
        ],
        axis=0,
    )


def compiler_params(limit=VMEM_BYTES):
    return pltpu.CompilerParams(vmem_limit_bytes=limit)


def dot_nt(left, right):
    return lax.dot_general(
        left, right, (((1,), (1,)), ((), ())), preferred_element_type=jnp.float32
    )


def dot_nn(left, right):
    return jnp.dot(left, right, preferred_element_type=jnp.float32)


def start_all(copies):
    for copy in copies:
        copy.start()


def wait_all(copies):
    for copy in copies:
        copy.wait()


def as_row(ref):
    return ref[...].astype(jnp.float32).reshape(1, ref.shape[0])


def lengths_as_row(sizes_ref, lanes, segments):
    lane = lax.broadcasted_iota(jnp.int32, (1, lanes), 1) % segments
    start = jnp.zeros((1, lanes), jnp.int32)
    end = jnp.zeros((1, lanes), jnp.int32)
    at = jnp.int32(0)
    for segment in range(segments):
        size = sizes_ref[0, segment]
        start = jnp.where(lane == segment, at, start)
        at = at + size
        end = jnp.where(lane == segment, at, end)
    return start, end


def counts_as_column(sizes_ref, segments):
    row = lax.broadcasted_iota(jnp.int32, (segments, 1), 0)
    counts = jnp.zeros((segments, 1), jnp.float32)
    for segment in range(segments):
        counts = jnp.where(row == segment, sizes_ref[0, segment].astype(jnp.float32), counts)
    return counts


def starts_as_column(sizes_ref, segments):
    row = lax.broadcasted_iota(jnp.int32, (segments, 1), 0)
    start = jnp.zeros((segments, 1), jnp.int32)
    end = jnp.zeros((segments, 1), jnp.int32)
    at = jnp.int32(0)
    for segment in range(segments):
        size = sizes_ref[0, segment]
        start = jnp.where(row == segment, at, start)
        at = at + size
        end = jnp.where(row == segment, at, end)
    return start, end


def band(length):
    return [(0, length // 2, 0, 3 * length // 4), (length // 2, length, length // 4, length)]


def mask_of(sizes_ref, segments, query_at, query_end, key_at, key_end):
    query = query_at + lax.broadcasted_iota(jnp.int32, (1, query_end - query_at), 1)
    low = jnp.zeros_like(query)
    high = jnp.zeros_like(query)
    at = jnp.int32(0)
    for segment in range(segments):
        end = at + sizes_ref[0, segment]
        inside = (query >= at) & (query < end)
        low = jnp.where(inside, at, low)
        high = jnp.where(inside, end, high)
        at = end
    padding = query >= at
    low = jnp.where(padding, at, low)
    high = jnp.where(padding, key_end, high)
    key = key_at + lax.broadcasted_iota(jnp.int32, (key_end - key_at, query_end - query_at), 0)
    return jnp.where((key >= low) & (key < high), 0.0, NEG_FILL)


def got_spec():
    return pl.BlockSpec(memory_space=pl.ANY)


def vmem_spec():
    return pl.BlockSpec(memory_space=pltpu.VMEM)


def smem_spec():
    return pl.BlockSpec(memory_space=pltpu.SMEM)


def any_spec():
    return pl.BlockSpec(memory_space=pltpu.HBM)


def cost(microseconds):
    return pl.CostEstimate(
        flops=int(microseconds * 1.1e9), bytes_accessed=1000000, transcendentals=0
    )


def forward_kernel(segments, masks_x, masks_z, here_ref, sizes_ref, matching_ref, *refs):
    given, refs = refs[:16], refs[16:]
    results, refs = refs[:14], refs[14:]
    side_own, side_send = results[-2:]
    local, refs = refs[:16], refs[16:]
    made, refs = refs[:12], refs[12:]
    (
        tokens_ref,
        question_w,
        lookup_w,
        content_w,
        mixing_w,
        widening_w,
        narrowing_w,
        question_row,
        content_row,
        mixing_row,
        gain_one_row,
        shift_one_row,
        widening_row,
        narrowing_row,
        gain_two_row,
        shift_two_row,
    ) = local
    (
        query_ref,
        key_ref,
        key_t_ref,
        value_ref,
        lse_ref,
        normed_one_ref,
        inv_one_ref,
        slope_ref,
        normed_two_ref,
        inv_two_ref,
        pooled_ref,
        message_ref,
    ) = made
    value_t, token_t, attn_t, out_one_t, inner_t, fill = refs[:6]
    out_one, out_one_low, total, in_sems, out_sems, side_sems = refs[6:]
    length, width = tokens_ref.shape
    hidden_units = widening_w.shape[1]
    here = here_ref[0]
    share_rows = side_own.shape[1] // (hidden_units // width + 3)
    inner_rows = hidden_units // width * share_rows
    first_rows = inner_rows // 2
    copies = [
        pltpu.make_async_copy(source, target, in_sems.at[i])
        for i, (source, target) in enumerate(zip(given, local))
    ]
    outward = [
        pltpu.make_async_copy(source, target, out_sems.at[i])
        for i, (source, target) in enumerate(zip(made, results))
    ]
    side_copies = []

    def send_side(source, source_rows, offset, count, at, masks):
        for place, mask in enumerate(masks):
            for flip, target in enumerate((side_own, side_send)):
                share = jnp.bitwise_xor(here, mask ^ flip)
                first = pl.multiple_of(share * source_rows + offset, 8)
                copy = pltpu.make_async_copy(
                    source.at[pl.ds(first, count)],
                    target.at[place, pl.ds(at, count)],
                    side_sems.at[len(side_copies)],
                )
                copy.start()
                side_copies.append(copy)

    start_all(copies[:2] + copies[7:] + copies[2:4])
    ranges = band(length)
    for i, (query_at, query_end, key_at, key_end) in enumerate(ranges):
        fill[i] = mask_of(sizes_ref, segments, query_at, query_end, key_at, key_end)
    wait_all(copies[:2] + copies[7:])
    start_all(copies[4:7])
    product = dot_nn(tokens_ref[...], question_w[...]) + as_row(question_row)
    query_ref[...] = product.astype(jnp.bfloat16) * jnp.bfloat16(HD ** (-0.5))
    token_t[...] = tokens_ref[...].T
    copies[2].wait()
    product = dot_nn(tokens_ref[...], lookup_w[...]).astype(jnp.bfloat16)
    key_ref[...] = product
    key_t_ref[...] = product.T
    copies[3].wait()
    product = (dot_nn(tokens_ref[...], content_w[...]) + as_row(content_row)).astype(jnp.bfloat16)
    value_ref[...] = product
    value_t[...] = product.T
    start_all(outward[:4])
    send_side(token_t, share_rows, 0, share_rows, inner_rows + share_rows, masks_x)
    lane = lax.broadcasted_iota(jnp.int32, (1, LANES), 1)
    units = [(at, i) for at in range(HEADS) for i in range(len(ranges))]

    def scores_of(unit):
        at, i = unit
        query_at, query_end, key_at, key_end = ranges[i]
        first = at * HD // LANES * LANES
        lanes = slice(first, first + LANES)
        which = (at * HD - first) // HD
        query = jnp.where((lane // HD) == which, query_ref[query_at:query_end, lanes], 0)
        return dot_nt(key_ref[key_at:key_end, lanes], query) + fill[i]

    def attend(unit, scores):
        at, i = unit
        query_at, query_end, key_at, key_end = ranges[i]
        top = jnp.max(scores, axis=0, keepdims=True)
        expo = jnp.exp(scores - top)
        norm = jnp.sum(expo, axis=0, keepdims=True)
        probs = (expo * (1.0 / norm)).astype(jnp.bfloat16)
        lse_ref[at // 4, at % 4 : at % 4 + 1, query_at:query_end] = top + jnp.log(norm)
        mixed = dot_nn(value_t[at * HD : (at + 1) * HD, key_at:key_end], probs)
        attn_t[at * HD : (at + 1) * HD, query_at:query_end] = mixed.astype(jnp.bfloat16)

    ahead = 4
    waiting = [scores_of(unit) for unit in units[:ahead]]
    for n, unit in enumerate(units):
        if n + ahead < len(units):
            waiting.append(scores_of(units[n + ahead]))
        attend(unit, waiting.pop(0))
    outward[4].start()
    send_side(attn_t, share_rows, 0, share_rows, inner_rows + 2 * share_rows, masks_x)
    copies[4].wait()
    chunk = min(length, 128)
    for at in range(0, length, chunk):
        rows = slice(at, at + chunk)
        hidden = (
            tokens_ref[rows].astype(jnp.float32)
            + dot_nn(attn_t[:, rows].T, mixing_w[...])
            + as_row(mixing_row)
        )
        normed, inv = standardize(hidden)
        normed_one_ref[rows] = normed
        inv_one_ref[rows] = inv
        shifted = normed * as_row(gain_one_row) + as_row(shift_one_row)
        out_one[rows] = shifted
        low = shifted.astype(jnp.bfloat16)
        out_one_low[rows] = low
        out_one_t[:, rows] = low.T
        total[rows] = shifted + as_row(narrowing_row)
    start_all(outward[5:7])
    send_side(out_one_t, share_rows, 0, share_rows, inner_rows, masks_x)
    copies[5].wait()
    copies[6].wait()
    tile = hidden_units // 4
    taller = min(length, 256)
    units = [(at, row) for at in range(0, hidden_units, tile) for row in range(0, length, taller)]

    def widened(unit):
        at, row = unit
        return dot_nn(out_one_low[row : row + taller], widening_w[:, at : at + tile])

    def activate(unit, before):
        at, row = unit
        rows = slice(row, row + taller)
        before = before + widening_row[at : at + tile].astype(jnp.float32).reshape(1, tile)
        cdf = 0.5 * (1.0 + lax.erf(before * 0.7071067811865476))
        pdf = jnp.exp(-0.5 * before * before) * 0.3989422804014327
        inner = (before * cdf).astype(jnp.bfloat16)
        slope_ref[rows, at : at + tile] = (cdf + before * pdf).astype(jnp.bfloat16)
        inner_t[at : at + tile, rows] = inner.T
        total[rows] += dot_nn(inner, narrowing_w[at : at + tile, :])

    ahead = 1
    waiting = [widened(unit) for unit in units[:ahead]]
    for n, unit in enumerate(units):
        if n + ahead < len(units):
            waiting.append(widened(units[n + ahead]))
        activate(unit, waiting.pop(0))
    outward[7].start()
    send_side(inner_t, inner_rows, 0, first_rows, 0, masks_x)
    send_side(inner_t, inner_rows, first_rows, inner_rows - first_rows, first_rows, masks_z)
    start, end = starts_as_column(sizes_ref, segments)
    sums = jnp.zeros((segments, width), jnp.float32)
    for at in range(0, length, chunk):
        rows = slice(at, at + chunk)
        normed, inv = standardize(total[rows])
        normed_two_ref[rows] = normed
        inv_two_ref[rows] = inv
        out_two = normed * as_row(gain_two_row) + as_row(shift_two_row)
        upper = out_two.astype(jnp.bfloat16)
        lower = (out_two - upper.astype(jnp.float32)).astype(jnp.bfloat16)
        token = at + lax.broadcasted_iota(jnp.int32, (segments, chunk), 1)
        member = jnp.where((token >= start) & (token < end), 1.0, 0.0).astype(jnp.bfloat16)
        sums = sums + dot_nn(member, upper) + dot_nn(member, lower)
    pooled = sums / counts_as_column(sizes_ref, segments)
    pooled_ref[...] = pooled
    inv_norm = lax.rsqrt(jnp.sum(pooled * pooled, axis=1, keepdims=True) + EPS_UNIT)
    units = (pooled * inv_norm).astype(jnp.bfloat16)
    half = segments // 2
    place = lax.broadcasted_iota(jnp.int32, (segments, segments), 0)
    source = lax.broadcasted_iota(jnp.int32, (segments, segments), 1)
    wanted = jnp.where(place < half, 2 * place, 2 * (place - half) + 1)
    pick = jnp.where(source == wanted, 1.0, 0.0).astype(jnp.bfloat16)
    message_ref[:, :width] = dot_nn(pick, units).astype(jnp.bfloat16)
    row = lax.broadcasted_iota(jnp.int32, (segments, LANES), 0)
    column = lax.broadcasted_iota(jnp.int32, (segments, LANES), 1)
    digits = jnp.zeros((segments, LANES), jnp.float32)
    for i in range(half):
        number = matching_ref[i]
        digit = jnp.where(column == 0, number & 255, number >> 8).astype(jnp.float32)
        digits = jnp.where((row == i) & (column < 2), digit, digits)
    message_ref[:, width:] = digits.astype(jnp.bfloat16)
    start_all(outward[8:])
    wait_all(outward)
    wait_all(side_copies)


def forward_step(here, sizes, matching, masks_x, masks_z, given):
    tokens, hidden_units = given[0], given[5].shape[1]
    length, width = tokens.shape
    segments = sizes.shape[1]
    half = len(masks_x)
    query_at, query_end, key_at, key_end = band(length)[0]
    low, full = jnp.bfloat16, jnp.float32
    side = ((half, (hidden_units // width + 3) * (width // half // 2), length), low)
    made = [
        ((length, width), low),
        ((length, width), low),
        ((width, length), low),
        ((length, width), low),
        ((HEADS // 4, 4, length), full),
        ((length, width), full),
        ((length, 1), full),
        ((length, hidden_units), low),
        ((length, width), full),
        ((length, 1), full),
        ((segments, width), full),
        ((segments, width + LANES), low),
    ]
    return pl.pallas_call(
        functools.partial(forward_kernel, segments, masks_x, masks_z),
        in_specs=[smem_spec()] * 3 + [any_spec()] * len(given),
        out_specs=[any_spec()] * (len(made) + 2),
        out_shape=[jax.ShapeDtypeStruct(shape, kind) for shape, kind in made + [side, side]],
        scratch_shapes=[pltpu.VMEM(item.shape, item.dtype) for item in given]
        + [pltpu.VMEM(shape, kind) for shape, kind in made]
        + [
            pltpu.VMEM((width, length), low),
            pltpu.VMEM((width, length), low),
            pltpu.VMEM((width, length), low),
            pltpu.VMEM((width, length), low),
            pltpu.VMEM((hidden_units, length), low),
            pltpu.VMEM((2, key_end - key_at, query_end - query_at), full),
            pltpu.VMEM((length, width), full),
            pltpu.VMEM((length, width), low),
            pltpu.VMEM((length, width), full),
            pltpu.SemaphoreType.DMA((len(given),)),
            pltpu.SemaphoreType.DMA((len(made),)),
            pltpu.SemaphoreType.DMA((2 * 5 * half,)),
        ],
        compiler_params=compiler_params(),
        cost_estimate=cost(28),
        name="forward_step",
    )(here, sizes, matching, *given)


def loss_kernel(
    place_ref,
    sizes_ref,
    sharpness_ref,
    numbers_ref,
    gathered_hbm,
    pooled_hbm,
    normed_hbm,
    inv_hbm,
    gain_hbm,
    loss_ref,
    grad_hidden_hbm,
    grad_branch_hbm,
    sums_ref,
    gathered_ref,
    pooled_ref,
    normed_ref,
    inv_ref,
    gain_ref,
    grad_hidden_ref,
    grad_branch_ref,
    sems,
):
    given = [
        (gathered_hbm, gathered_ref),
        (pooled_hbm, pooled_ref),
        (normed_hbm, normed_ref),
        (inv_hbm, inv_ref),
        (gain_hbm, gain_ref),
    ]
    copies = [
        pltpu.make_async_copy(source, target, sems.at[i])
        for i, (source, target) in enumerate(given)
    ]
    start_all(copies)
    segments, width = pooled_ref.shape
    half = segments // 2
    devices = gathered_ref.shape[0]
    total = devices * half
    sharpness = sharpness_ref[0]
    row = lax.broadcasted_iota(jnp.int32, (total, devices * segments), 0)
    column = lax.broadcasted_iota(jnp.int32, (total, devices * segments), 1)
    source = jnp.bitwise_xor(row // half, place_ref[0]) * segments + row % half
    copies[0].wait()
    gathered = gathered_ref[...].reshape(devices * segments, width + LANES)
    pick = jnp.where(column == source, 1.0, 0.0).astype(jnp.bfloat16)
    picked = dot_nn(pick, gathered)
    questions = picked[:, :width].astype(jnp.bfloat16)
    digits = picked[:, width:]
    pick = jnp.where(column == source + half, 1.0, 0.0).astype(jnp.bfloat16)
    passages = dot_nn(pick, gathered[:, :width]).astype(jnp.bfloat16)
    matching = (digits[:, 0:1] + 256.0 * digits[:, 1:2]).astype(jnp.int32)
    table = dot_nt(questions, passages) / sharpness
    top = jnp.max(table, axis=1, keepdims=True)
    expo = jnp.exp(table - top)
    expo_total = jnp.sum(expo, axis=1, keepdims=True)
    chosen = matching == numbers_ref[...]
    positive = jnp.sum(jnp.where(chosen, table, 0.0), axis=1, keepdims=True)
    loss_ref[...] = (
        jnp.sum(top + jnp.log(expo_total) - positive, axis=0, keepdims=True) / total
    )
    slope = (expo / expo_total - chosen.astype(jnp.float32)) / total
    grad_dot = (slope / sharpness).astype(jnp.bfloat16)
    segment_at = lax.broadcasted_iota(jnp.int32, (segments, total), 0)
    column = lax.broadcasted_iota(jnp.int32, (segments, total), 1)
    mine = column == place_ref[0] * half + segment_at // 2
    is_query = segment_at % 2 == 0
    pick_query = jnp.where(mine & is_query, 1.0, 0.0).astype(jnp.bfloat16)
    pick_passage = jnp.where(mine & ~is_query, 1.0, 0.0).astype(jnp.bfloat16)
    row_terms = dot_nn(pick_query, grad_dot).astype(jnp.bfloat16)
    column_terms = dot_nt(pick_passage, grad_dot).astype(jnp.bfloat16)
    grad_units = dot_nn(row_terms, passages) + dot_nn(column_terms, questions)
    wait_all(copies[1:])
    pooled = pooled_ref[...]
    inv_norm = lax.rsqrt(jnp.sum(pooled * pooled, axis=1, keepdims=True) + EPS_UNIT)
    units = pooled * inv_norm
    along = jnp.sum(units * grad_units, axis=1, keepdims=True)
    grad_pooled = inv_norm * (grad_units - units * along) / counts_as_column(sizes_ref, segments)
    upper = grad_pooled.astype(jnp.bfloat16)
    lower = (grad_pooled - upper.astype(jnp.float32)).astype(jnp.bfloat16)
    both = jnp.concatenate([upper, lower], axis=0)
    start, end = lengths_as_row(sizes_ref, 2 * segments, segments)
    gain = as_row(gain_ref)
    outward = []
    tokens = normed_ref.shape[0]
    chunk = min(tokens, 128)
    gain_sum = jnp.zeros((1, width), jnp.float32)
    shift_sum = jnp.zeros((1, width), jnp.float32)
    bias_sum = jnp.zeros((1, width), jnp.float32)
    for at in range(0, tokens, chunk):
        token = at + lax.broadcasted_iota(jnp.int32, (chunk, 2 * segments), 0)
        member = jnp.where((token >= start) & (token < end), 1.0, 0.0).astype(jnp.bfloat16)
        grad_out = dot_nn(member, both)
        normed = normed_ref[at : at + chunk]
        gain_sum = gain_sum + jnp.sum(grad_out * normed, axis=0, keepdims=True)
        shift_sum = shift_sum + jnp.sum(grad_out, axis=0, keepdims=True)
        grad_hidden = standardize_back(normed, inv_ref[at : at + chunk], grad_out * gain)
        grad_hidden_ref[at : at + chunk] = grad_hidden
        low = grad_hidden.astype(jnp.bfloat16)
        grad_branch_ref[at : at + chunk] = low
        bias_sum = bias_sum + jnp.sum(low.astype(jnp.float32), axis=0, keepdims=True)
        for source_ref, target in (
            (grad_hidden_ref, grad_hidden_hbm),
            (grad_branch_ref, grad_branch_hbm),
        ):
            copy = pltpu.make_async_copy(
                source_ref.at[at : at + chunk],
                target.at[at : at + chunk],
                sems.at[len(copies) + len(outward)],
            )
            copy.start()
            outward.append(copy)
    sums_ref[...] = jnp.concatenate([bias_sum, gain_sum, shift_sum], axis=0)
    wait_all(outward)


def loss_step(place, sizes, sharpness, numbers, gathered, pooled, normed, inv, gain):
    tokens, width = normed.shape
    low, full = jnp.bfloat16, jnp.float32
    chunks = -(-tokens // 128)
    return pl.pallas_call(
        loss_kernel,
        in_specs=[smem_spec()] * 3 + [vmem_spec()] + [any_spec()] * 5,
        out_specs=[vmem_spec(), any_spec(), any_spec(), vmem_spec()],
        out_shape=[
            jax.ShapeDtypeStruct((1, 1), full),
            jax.ShapeDtypeStruct((tokens, width), full),
            jax.ShapeDtypeStruct((tokens, width), low),
            jax.ShapeDtypeStruct((3, width), full),
        ],
        scratch_shapes=[
            pltpu.VMEM(gathered.shape, low),
            pltpu.VMEM(pooled.shape, full),
            pltpu.VMEM(normed.shape, full),
            pltpu.VMEM(inv.shape, full),
            pltpu.VMEM(gain.shape, low),
            pltpu.VMEM((tokens, width), full),
            pltpu.VMEM((tokens, width), low),
            pltpu.SemaphoreType.DMA((5 + 2 * chunks,)),
        ],
        compiler_params=compiler_params(),
        cost_estimate=cost(4),
        name="loss_step",
    )(place, sizes, sharpness, numbers, gathered, pooled, normed, inv, gain)


def before_kernel(
    branch_hbm,
    slope_hbm,
    narrowing_hbm,
    widening_hbm,
    hidden_hbm,
    normed_hbm,
    inv_hbm,
    gain_hbm,
    mixing_hbm,
    grad_pre_hbm,
    bias_ref,
    grad_hidden_hbm,
    grad_branch_hbm,
    grad_attn_hbm,
    sums_ref,
    branch_ref,
    slope_ref,
    narrowing_ref,
    widening_ref,
    total,
    normed_ref,
    inv_ref,
    gain_ref,
    mixing_ref,
    grad_pre_ref,
    grad_hidden_ref,
    grad_branch_ref,
    grad_attn_ref,
    in_sems,
    part_sems,
    out_sems,
):
    tokens, width = branch_ref.shape
    parts = slope_ref.shape[1] // width
    given = [
        (branch_hbm, branch_ref),
        (hidden_hbm, total),
        (normed_hbm, normed_ref),
        (inv_hbm, inv_ref),
        (gain_hbm, gain_ref),
        (mixing_hbm, mixing_ref),
    ]
    copies = [
        pltpu.make_async_copy(source, target, in_sems.at[i])
        for i, (source, target) in enumerate(given)
    ]
    part_copies = []
    for part in range(parts):
        at = pl.ds(part * width, width)
        pairs = [
            (narrowing_hbm.at[at], narrowing_ref.at[at]),
            (slope_hbm.at[:, at], slope_ref.at[:, at]),
            (widening_hbm.at[:, at], widening_ref.at[:, at]),
        ]
        part_copies.append(
            [
                pltpu.make_async_copy(source, target, part_sems.at[part, i])
                for i, (source, target) in enumerate(pairs)
            ]
        )
    start_all(copies[:1] + part_copies[0] + part_copies[1] + copies[1:2])
    outward = []

    def write(source, target):
        copy = pltpu.make_async_copy(source, target, out_sems.at[len(outward)])
        copy.start()
        outward.append(copy)

    def columns_of(part):
        return slice(part * width, (part + 1) * width)

    def product(part):
        return dot_nt(branch_ref[...], narrowing_ref[columns_of(part)])

    wait_all(copies[:1] + part_copies[0][:1])
    waiting = product(0)
    for part in range(parts):
        if part + 2 < parts:
            start_all(part_copies[part + 2])
        elif part + 2 == parts:
            start_all(copies[2:])
        if part == 0:
            wait_all(copies[1:2])
        wait_all(part_copies[part][1:])
        grad_act = waiting
        if part + 1 < parts:
            wait_all(part_copies[part + 1][:1])
            waiting = product(part + 1)
        columns = columns_of(part)
        grad_pre = (grad_act * widen(slope_ref[:, columns])).astype(jnp.bfloat16)
        grad_pre_ref[:, columns] = grad_pre
        bias_ref[:, columns] = jnp.sum(widen(grad_pre), axis=0, keepdims=True)
        total[...] += dot_nt(grad_pre, widening_ref[:, columns])
        at = pl.ds(part * width, width)
        write(grad_pre_ref.at[:, at], grad_pre_hbm.at[:, at])
    wait_all(copies[2:])
    chunk = min(tokens, 128)
    gain = as_row(gain_ref)
    gain_sum = jnp.zeros((1, width), jnp.float32)
    shift_sum = jnp.zeros((1, width), jnp.float32)
    bias_sum = jnp.zeros((1, width), jnp.float32)
    for row in range(0, tokens, chunk):
        grad_out = total[row : row + chunk]
        normed = normed_ref[row : row + chunk]
        gain_sum = gain_sum + jnp.sum(grad_out * normed, axis=0, keepdims=True)
        shift_sum = shift_sum + jnp.sum(grad_out, axis=0, keepdims=True)
        grad_hidden = standardize_back(normed, inv_ref[row : row + chunk], grad_out * gain)
        grad_hidden_ref[row : row + chunk] = grad_hidden
        low = grad_hidden.astype(jnp.bfloat16)
        grad_branch_ref[row : row + chunk] = low
        bias_sum = bias_sum + jnp.sum(widen(low), axis=0, keepdims=True)
        grad_attn_ref[row : row + chunk] = dot_nt(low, mixing_ref[...]).astype(jnp.bfloat16)
    write(grad_branch_ref, grad_branch_hbm)
    write(grad_attn_ref, grad_attn_hbm)
    write(grad_hidden_ref, grad_hidden_hbm)
    sums_ref[...] = jnp.concatenate([bias_sum, gain_sum, shift_sum], axis=0)
    wait_all(outward)


def before_step(branch, slope, narrowing, widening, hidden, normed, inv, gain, mixing):
    tokens, hidden_units = slope.shape
    width = branch.shape[1]
    parts = hidden_units // width
    low, full = jnp.bfloat16, jnp.float32
    return pl.pallas_call(
        before_kernel,
        in_specs=[any_spec()] * 9,
        out_specs=[any_spec(), vmem_spec()] + [any_spec()] * 3 + [vmem_spec()],
        out_shape=[
            jax.ShapeDtypeStruct((tokens, hidden_units), low),
            jax.ShapeDtypeStruct((1, hidden_units), full),
            jax.ShapeDtypeStruct((tokens, width), full),
            jax.ShapeDtypeStruct((tokens, width), low),
            jax.ShapeDtypeStruct((tokens, width), low),
            jax.ShapeDtypeStruct((3, width), full),
        ],
        scratch_shapes=[
            pltpu.VMEM(branch.shape, low),
            pltpu.VMEM(slope.shape, low),
            pltpu.VMEM(narrowing.shape, low),
            pltpu.VMEM(widening.shape, low),
            pltpu.VMEM((tokens, width), full),
            pltpu.VMEM(normed.shape, full),
            pltpu.VMEM(inv.shape, full),
            pltpu.VMEM(gain.shape, low),
            pltpu.VMEM(mixing.shape, low),
            pltpu.VMEM(slope.shape, low),
            pltpu.VMEM((tokens, width), full),
            pltpu.VMEM((tokens, width), low),
            pltpu.VMEM((tokens, width), low),
            pltpu.SemaphoreType.DMA((6,)),
            pltpu.SemaphoreType.DMA((parts, 3)),
            pltpu.SemaphoreType.DMA((parts + 3,)),
        ],
        compiler_params=compiler_params(),
        cost_estimate=cost(11),
        name="before_step",
    )(branch, slope, narrowing, widening, hidden, normed, inv, gain, mixing)


def side_copies(own_ref, other_ref, at, count, target, sems):
    tokens = own_ref.shape[2]
    return [
        pltpu.make_async_copy(
            source.at[:, pl.ds(at, count)],
            target.at[:, :, pl.ds(i * tokens, tokens)],
            sems.at[i],
        )
        for i, source in enumerate((own_ref, other_ref))
    ]


def flat(ref):
    places, rows, tokens = ref.shape
    return ref[...].reshape(places * rows, tokens)


def store_places(product, first, parts, target):
    rows = target.shape[2]
    low = product.astype(jnp.bfloat16)
    for place in range(low.shape[0] // rows // parts):
        for tile in range(low.shape[1] // LANES):
            for part in range(parts):
                row = (place * parts + part) * rows
                target[first + place, tile * parts + part] = low[
                    row : row + rows, tile * LANES : (tile + 1) * LANES
                ]


def outer_kernel(
    own_ref,
    other_ref,
    branch_own_ref,
    branch_other_ref,
    keep_x,
    send_x,
    keep_z,
    send_z,
    left_x,
    left_z,
    right,
    made_x,
    made_z,
    left_sems,
    right_sems,
    out_sems,
):
    places, count, _ = left_x.shape
    tokens = branch_own_ref.shape[0]
    half = places // 2
    parts = count // made_x.shape[2]
    copies = [
        pltpu.make_async_copy(source, right.at[pl.ds(i * tokens, tokens)], right_sems.at[i])
        for i, source in enumerate((branch_own_ref, branch_other_ref))
    ]
    copies_x = side_copies(own_ref, other_ref, 0, count, left_x, left_sems.at[0])
    copies_z = side_copies(own_ref, other_ref, count, count, left_z, left_sems.at[1])
    start_all(copies + copies_x + copies_z)
    wait_all(copies + copies_x)
    units = [
        (left_x, made_x, half, send_x),
        (left_x, made_x, 0, keep_x),
        (left_z, made_z, half, send_z),
        (left_z, made_z, 0, keep_z),
    ]

    def product(n):
        left, _, first, _ = units[n]
        if n == 2:
            wait_all(copies_z)
        return dot_nn(
            left[first : first + half].reshape(half * count, 2 * tokens), right[...]
        )

    outward = []
    waiting = product(0)
    for n, (_, made, first, target) in enumerate(units):
        current = waiting
        if n + 1 < len(units):
            waiting = product(n + 1)
        store_places(current, first, parts, made)
        copy = pltpu.make_async_copy(made.at[pl.ds(first, half)], target, out_sems.at[n])
        copy.start()
        outward.append(copy)
    wait_all(outward)


def outer_step(own, other, branch_own, branch_other, count):
    places, _, tokens = own.shape
    width = branch_own.shape[1]
    parts = 2
    rows = count // parts
    low = jnp.bfloat16
    blocks = width // LANES * parts
    shape = jax.ShapeDtypeStruct((places // 2, blocks, rows, LANES), low)
    return pl.pallas_call(
        outer_kernel,
        in_specs=[any_spec(), got_spec(), any_spec(), got_spec()],
        out_specs=[any_spec()] * 4,
        out_shape=[shape] * 4,
        scratch_shapes=[
            pltpu.VMEM((places, count, 2 * tokens), low),
            pltpu.VMEM((places, count, 2 * tokens), low),
            pltpu.VMEM((2 * tokens, width), low),
            pltpu.VMEM((places, blocks, rows, LANES), low),
            pltpu.VMEM((places, blocks, rows, LANES), low),
            pltpu.SemaphoreType.DMA((2, 2)),
            pltpu.SemaphoreType.DMA((2,)),
            pltpu.SemaphoreType.DMA((4,)),
        ],
        compiler_params=compiler_params(),
        cost_estimate=cost(5),
        name="outer_step",
    )(own, other, branch_own, branch_other)


def inner_kernel(
    at,
    side_ref,
    own_ref,
    other_ref,
    grad_own_hbm,
    grad_other_hbm,
    keep_x,
    send_x,
    keep_y,
    send_y,
    left,
    right,
    made_x,
    made_y,
    left_sems,
    in_sems,
    out_sems,
):
    tokens, hidden_units = grad_own_hbm.shape
    places, rows, _ = left.shape
    half = places // 2
    parts = 4
    width = hidden_units // parts
    tiles = width // LANES
    side = side_ref[0]
    left_copies = side_copies(own_ref, other_ref, at, rows, left, left_sems)
    right_copies = []
    for part in range(parts):
        columns = pl.ds(part * width, width)
        right_copies.append(
            [
                pltpu.make_async_copy(
                    source.at[:, columns],
                    right.at[pl.ds(i * tokens, tokens), columns],
                    in_sems.at[part, i],
                )
                for i, source in enumerate((grad_own_hbm, grad_other_hbm))
            ]
        )
    start_all(left_copies)
    for copies in right_copies:
        start_all(copies)
    outward = []

    def write(source, target):
        copy = pltpu.make_async_copy(source, target, out_sems.at[len(outward)])
        copy.start()
        outward.append(copy)

    def weight(part):
        return dot_nn(flat(left), right[:, part * width : (part + 1) * width])

    def store_weight(part, product):
        low = product.astype(jnp.bfloat16)
        for place in range(places):
            for tile in range(tiles):
                block = low[place * rows : (place + 1) * rows, tile * LANES : (tile + 1) * LANES]
                if part < parts // 2:
                    made_x[place, part * tiles + tile] = block
                else:
                    made_y[jnp.bitwise_xor(side, part - parts // 2), place, tile] = block
        if part == parts // 2 - 1:
            write(made_x.at[pl.ds(half, half)], send_x)
            write(made_x.at[pl.ds(0, half)], keep_x)
        if part == parts - 1:
            write(made_y.at[1], send_y)
            write(made_y.at[0], keep_y)

    wait_all(left_copies)
    products = []
    for part in range(parts):
        wait_all(right_copies[part])
        products.append(weight(part))
        if part >= 1:
            store_weight(part - 1, products.pop(0))
    store_weight(parts - 1, products.pop(0))
    wait_all(outward)


def inner_step(side, own, other, at, rows, grad_own, grad_other):
    places, _, tokens = own.shape
    hidden_units = grad_own.shape[1]
    tiles = hidden_units // 4 // LANES
    half = places // 2
    low = jnp.bfloat16
    shape_x = jax.ShapeDtypeStruct((half, 2 * tiles, rows, LANES), low)
    shape_y = jax.ShapeDtypeStruct((places, tiles, rows, LANES), low)
    return pl.pallas_call(
        functools.partial(inner_kernel, at),
        in_specs=[smem_spec(), any_spec(), got_spec(), any_spec(), got_spec()],
        out_specs=[any_spec()] * 4,
        out_shape=[shape_x, shape_x, shape_y, shape_y],
        scratch_shapes=[
            pltpu.VMEM((places, rows, 2 * tokens), low),
            pltpu.VMEM((2 * tokens, hidden_units), low),
            pltpu.VMEM((places, 2 * tiles, rows, LANES), low),
            pltpu.VMEM((2, places, tiles, rows, LANES), low),
            pltpu.SemaphoreType.DMA((2,)),
            pltpu.SemaphoreType.DMA((4, 2)),
            pltpu.SemaphoreType.DMA((4,)),
        ],
        compiler_params=compiler_params(),
        cost_estimate=cost(5),
        name="inner_step",
    )(side, own, other, grad_own, grad_other)


def attend_back_kernel(
    segments,
    sizes_ref,
    query_ref,
    key_ref,
    key_t_ref,
    value_ref,
    lse_ref,
    grad_ref,
    grads_ref,
    sums_ref,
    fill,
    query_t,
    total_key,
    total_value,
):
    length, wide = query_ref.shape
    ranges = band(length)
    step = pl.program_id(0)

    @pl.when(step == 0)
    def _():
        for i, (query_at, query_end, key_at, key_end) in enumerate(ranges):
            fill[i] = mask_of(sizes_ref, segments, query_at, query_end, key_at, key_end)

    total_key[...] = jnp.zeros_like(total_key)
    total_value[...] = jnp.zeros_like(total_value)
    lane = lax.broadcasted_iota(jnp.int32, (1, LANES), 1)
    units = [(at, i) for at in range(wide // HD) for i in range(len(ranges))]

    def lanes_of(at):
        first = at * HD // LANES * LANES
        return slice(first, first + LANES), (lane // HD) == (at * HD - first) // HD

    def products(unit):
        at, i = unit
        query_at, query_end, key_at, key_end = ranges[i]
        lanes, head = lanes_of(at)
        query = jnp.where(head, query_ref[query_at:query_end, lanes], 0)
        grad = jnp.where(head, grad_ref[query_at:query_end, lanes], 0)
        scores = dot_nt(key_ref[key_at:key_end, lanes], query) + fill[i]
        return scores, dot_nt(value_ref[key_at:key_end, lanes], grad)

    def back(unit, scores, grad_probs):
        at, i = unit
        query_at, query_end, key_at, key_end = ranges[i]
        probs = jnp.exp(scores - lse_ref[0, at : at + 1, query_at:query_end])
        inner = jnp.sum(grad_probs * probs, axis=0, keepdims=True)
        return probs.astype(jnp.bfloat16), (probs * (grad_probs - inner)).astype(jnp.bfloat16)

    def finish(unit, probs, grad_scores):
        at, i = unit
        query_at, query_end, key_at, key_end = ranges[i]
        lanes, head = lanes_of(at)
        query = jnp.where(head, query_ref[query_at:query_end, lanes], 0)
        grad = jnp.where(head, grad_ref[query_at:query_end, lanes], 0)
        total_value[key_at:key_end, lanes] += dot_nn(probs, grad)
        total_key[key_at:key_end, lanes] += dot_nn(grad_scores, query)
        query_t[at * HD : (at + 1) * HD, query_at:query_end] = dot_nn(
            key_t_ref[at * HD : (at + 1) * HD, key_at:key_end], grad_scores
        )

    ahead = 2
    waiting = [products(unit) for unit in units[:ahead]]
    done = []
    for n, unit in enumerate(units):
        if n + ahead < len(units):
            waiting.append(products(units[n + ahead]))
        done.append((unit, *back(unit, *waiting.pop(0))))
        if len(done) > 1:
            finish(*done.pop(0))
    for item in done:
        finish(*item)
    grad_query = (query_t[...] * HD ** (-0.5)).T.astype(jnp.bfloat16)
    grad_value = total_value[...].astype(jnp.bfloat16)
    grads_ref[0] = grad_query
    grads_ref[1] = total_key[...].astype(jnp.bfloat16)
    grads_ref[2] = grad_value
    sums_ref[...] = jnp.concatenate(
        [
            jnp.sum(widen(grad_query), axis=0, keepdims=True),
            jnp.sum(widen(grad_value), axis=0, keepdims=True),
        ],
        axis=0,
    )


def attend_back_step(sizes, query, key, key_t, value, lse, grad):
    tokens, width = query.shape
    heads_here = lse.shape[1]
    wide = heads_here * HD
    columns = pl.BlockSpec((tokens, wide), lambda i: (0, i))
    query_at, query_end, key_at, key_end = band(tokens)[0]
    return pl.pallas_call(
        functools.partial(attend_back_kernel, sizes.shape[1]),
        grid=(width // wide,),
        in_specs=[
            smem_spec(),
            columns,
            columns,
            pl.BlockSpec((wide, tokens), lambda i: (i, 0)),
            columns,
            pl.BlockSpec((1, heads_here, tokens), lambda i: (i, 0, 0)),
            columns,
        ],
        out_specs=[
            pl.BlockSpec((3, tokens, wide), lambda i: (0, 0, i)),
            pl.BlockSpec((2, wide), lambda i: (0, i)),
        ],
        out_shape=[
            jax.ShapeDtypeStruct((3, tokens, width), jnp.bfloat16),
            jax.ShapeDtypeStruct((2, width), jnp.float32),
        ],
        scratch_shapes=[
            pltpu.VMEM((2, key_end - key_at, query_end - query_at), jnp.float32),
            pltpu.VMEM((wide, tokens), jnp.float32),
            pltpu.VMEM((tokens, wide), jnp.float32),
            pltpu.VMEM((tokens, wide), jnp.float32),
        ],
        compiler_params=compiler_params(),
        cost_estimate=cost(8),
        name="attend_back_step",
    )(sizes, query, key, key_t, value, lse, grad)


def add_kernel(shape_of, *refs):
    counts, last = shape_of
    pairs = sum(counts) + last
    given, refs = refs[: 2 * pairs], refs[2 * pairs :]
    outputs = 2 * len(counts) + (1 if last else 0)
    targets, refs = refs[:outputs], refs[outputs:]
    local, refs = refs[: 2 * pairs], refs[2 * pairs :]
    made, refs = refs[:outputs], refs[outputs:]
    in_sems, out_sems = refs
    copies = [
        pltpu.make_async_copy(source, target, in_sems.at[n])
        for n, (source, target) in enumerate(zip(given, local))
    ]
    start_all(copies)
    outward = []

    def write(n):
        copy = pltpu.make_async_copy(made[n], targets[n], out_sems.at[n])
        copy.start()
        outward.append(copy)

    at = 0
    for item, count in enumerate(counts):
        kept, sent = made[2 * item], made[2 * item + 1]
        half = kept.shape[0]
        block = 0
        for _ in range(count):
            wait_all(copies[2 * at : 2 * at + 2])
            keep, got = local[2 * at], local[2 * at + 1]
            blocks = slice(block, block + keep.shape[1])
            sent[:, blocks] = (widen(keep[half:]) + widen(got[half:])).astype(sent.dtype)
            kept[:, blocks] = widen(keep[:half]) + widen(got[:half])
            block += keep.shape[1]
            at += 1
        write(2 * item + 1)
        write(2 * item)
    if last:
        mine = made[-1]
        block = 0
        for _ in range(last):
            wait_all(copies[2 * at : 2 * at + 2])
            keep, got = local[2 * at], local[2 * at + 1]
            blocks = slice(block, block + keep.shape[1])
            mine[blocks] = (widen(keep[0]) + widen(got[0])).astype(mine.dtype)
            block += keep.shape[1]
            at += 1
        write(outputs - 1)
    wait_all(outward)


def add_step(items, last=(), name="add_step"):
    given, shapes = [], []
    for pairs in items:
        for pair in pairs:
            given.extend(pair)
        places, _, rows, lanes = pairs[0][0].shape
        blocks = sum(keep.shape[1] for keep, _ in pairs)
        shape = (places // 2, blocks, rows, lanes)
        shapes.append((shape, jnp.float32))
        shapes.append((shape, pairs[0][1].dtype))
    for pair in last:
        given.extend(pair)
    if last:
        _, _, rows, lanes = last[0][0].shape
        blocks = sum(keep.shape[1] for keep, _ in last)
        shapes.append(((blocks, rows, lanes), jnp.bfloat16))
    results = pl.pallas_call(
        functools.partial(add_kernel, ([len(pairs) for pairs in items], len(last))),
        in_specs=[got_spec()] * len(given),
        out_specs=[any_spec()] * len(shapes),
        out_shape=[jax.ShapeDtypeStruct(shape, kind) for shape, kind in shapes],
        scratch_shapes=[pltpu.VMEM(item.shape, item.dtype) for item in given]
        + [pltpu.VMEM(shape, kind) for shape, kind in shapes]
        + [pltpu.SemaphoreType.DMA((len(given),)), pltpu.SemaphoreType.DMA((len(shapes),))],
        compiler_params=compiler_params(SMALL_BYTES),
        cost_estimate=cost(2),
        name=name,
    )(*given)
    halves = [(results[2 * n], results[2 * n + 1]) for n in range(len(items))]
    return halves + ([results[-1]] if last else [])


def split_vector(total, rows):
    places, _, count, lanes = total.shape
    parts = []
    for _ in range(3):
        low = total.astype(jnp.bfloat16)
        total = total - widen(low)
        parts.append(low)
    if rows > 3 * count:
        parts.append(jnp.zeros((places, 1, rows - 3 * count, lanes), jnp.bfloat16))
    return jnp.concatenate(parts, axis=2)


def join_vector(block, count):
    return sum(widen(block[..., i * count : (i + 1) * count, :]) for i in range(3))


def round_kernel(plan, passes, inputs, streams, *refs):
    given, refs = refs[:inputs], refs[inputs:]
    outputs = len(plan) - sum(1 for item in plan if item[5]) + streams
    targets, refs = refs[:outputs], refs[outputs:]
    local, refs = refs[:inputs], refs[inputs:]
    made, (in_sems, out_sems) = refs[:outputs], refs[outputs:]
    sent_to = made[outputs - streams :]
    copies = []
    passed = {}
    for n, source in enumerate(given):
        if n in passes:
            stream, at = passes[n]
            target = sent_to[stream].at[pl.ds(at, source.shape[0])]
            passed.setdefault(stream, []).append(n)
        else:
            target = local[n]
        copies.append(pltpu.make_async_copy(source, target, in_sems.at[n]))
    start_all(copies)
    outward = []
    waited = set()

    def write(n):
        copy = pltpu.make_async_copy(made[n], targets[n], out_sems.at[n])
        copy.start()
        outward.append(copy)

    def need(n):
        if n not in waited:
            waited.add(n)
            copies[n].wait()

    kept_at = 0
    for keep_at, got_at, begin, stream, at, whole, vector in plan:
        keep = local[keep_at]
        places, blocks, rows, lanes = keep.shape
        need(keep_at)
        if got_at is not None:
            need(got_at)
        total = widen(keep[...])
        if vector and keep.dtype == jnp.bfloat16:
            total = join_vector(keep[...], 8)
        if got_at is not None:
            got = local[got_at][begin : begin + places * blocks]
            if vector:
                total = total + join_vector(got, 8)[:, None]
            else:
                total = total + widen(got.reshape(keep.shape))
        target = sent_to[stream]
        if not whole:
            made[kept_at][...] = total[: places // 2]
            write(kept_at)
            kept_at += 1
            total = total[places // 2 :]
        if vector:
            send = split_vector(total, target.shape[1])
        else:
            send = total.astype(jnp.bfloat16)
        count = send.shape[0] * blocks
        target[at : at + count] = send.reshape((count,) + target.shape[1:])
    for n in range(inputs):
        need(n)
    for n in range(outputs - streams, outputs):
        write(n)
    wait_all(outward)


def round_step(chains, received, rows, limit):
    given, kept, plan, passes = [], [], [], {}
    at_of, lengths = {}, {}
    stream_keys = list(received)
    given = [received[key] for key in stream_keys]
    hops = []
    for chain in chains.values():
        if chain["hops"] and chain["hops"][0] not in hops:
            hops.append(chain["hops"][0])
    shapes = []
    for name, chain in chains.items():
        if not chain["hops"]:
            continue
        hop = chain["hops"][0]
        at = lengths.get(hop, 0)
        at_of[name] = at
        if chain["send"] is not None:
            given.append(chain["send"].reshape((-1,) + chain["send"].shape[-2:]))
            passes[len(given) - 1] = (hops.index(hop), at)
            lengths[hop] = at + given[-1].shape[0]
            continue
        keep = chain["keep"]
        given.append(keep)
        keep_at = len(given) - 1
        got_at, begin = None, 0
        if chain["got"] is not None:
            got_at, begin = stream_keys.index(chain["got"][0]), chain["got"][1]
        places, blocks = keep.shape[:2]
        whole = places == 1
        plan.append((keep_at, got_at, begin, hops.index(hop), at, whole, chain["vector"]))
        lengths[hop] = at + (blocks if whole else places // 2 * blocks)
        if not whole:
            shapes.append(((places // 2,) + keep.shape[1:], jnp.float32))
            kept.append(name)
    shapes = shapes + [((lengths[hop], rows, LANES), jnp.bfloat16) for hop in hops]
    results = pl.pallas_call(
        functools.partial(round_kernel, plan, passes, len(given), len(hops)),
        in_specs=[got_spec()] * len(given),
        out_specs=[any_spec()] * len(shapes),
        out_shape=[jax.ShapeDtypeStruct(shape, kind) for shape, kind in shapes],
        scratch_shapes=[
            pltpu.VMEM((8, LANES) if n in passes else item.shape, item.dtype)
            for n, item in enumerate(given)
        ]
        + [pltpu.VMEM(shape, kind) for shape, kind in shapes]
        + [pltpu.SemaphoreType.DMA((len(given),)), pltpu.SemaphoreType.DMA((len(shapes),))],
        compiler_params=compiler_params(limit),
        cost_estimate=cost(3),
        name="round_step",
    )(*given)
    sent = dict(zip(hops, results[len(kept) :]))
    keeps = dict(zip(kept, results))
    for name, chain in chains.items():
        if not chain["hops"]:
            continue
        hop = chain["hops"].pop(0)
        at = at_of[name]
        if chain["send"] is not None:
            chain["send"] = None
        elif name in keeps:
            chain["keep"] = keeps[name]
        else:
            count = chain["keep"].shape[1]
            chain["keep"] = sent[hop][at : at + count][None]
        chain["got"] = (hop, at)
    return sent


def token_kernel(hidden_ref, grads_ref, question_ref, lookup_ref, content_ref, out_ref):
    out_ref[...] = (
        hidden_ref[...]
        + dot_nt(grads_ref[0], question_ref[...])
        + dot_nt(grads_ref[1], lookup_ref[...])
        + dot_nt(grads_ref[2], content_ref[...])
    )


def token_step(hidden, grads, question, lookup, content):
    tokens, width = hidden.shape
    wide = 2 * LANES
    weight = pl.BlockSpec((wide, width), lambda i: (i, 0))
    column = pl.BlockSpec((tokens, wide), lambda i: (0, i))
    return pl.pallas_call(
        token_kernel,
        grid=(width // wide,),
        in_specs=[column, pl.BlockSpec((3, tokens, width), lambda i: (0, 0, 0))] + [weight] * 3,
        out_specs=column,
        out_shape=jax.ShapeDtypeStruct((tokens, width), jnp.float32),
        compiler_params=compiler_params(),
        cost_estimate=cost(5),
        name="token_step",
    )(hidden, grads, question, lookup, content)


def attention_kernel(
    token_at,
    attn_at,
    places_z,
    side_ref,
    own_ref,
    other_ref,
    grads_own_ref,
    grads_other_ref,
    branch_own_ref,
    branch_other_ref,
    keep_x,
    send_x,
    keep_y,
    send_y,
    keep_z,
    send_z,
    token_left,
    attn_left,
    token_right,
    attn_right,
    made_x,
    made_y,
    made_z,
    left_sems,
    right_sems,
    out_sems,
):
    places, rows, _ = token_left.shape
    tokens = branch_own_ref.shape[0]
    wide = 2 * LANES
    left_copies = side_copies(own_ref, other_ref, token_at, rows, token_left, left_sems.at[0])
    attn_copies = side_copies(own_ref, other_ref, attn_at, rows, attn_left, left_sems.at[1])
    right_copies = []
    for chunk in range(3):
        columns = pl.ds(chunk * wide, wide)
        copies = []
        for core, (grads, branch) in enumerate(
            ((grads_own_ref, branch_own_ref), (grads_other_ref, branch_other_ref))
        ):
            token_rows = pl.ds(core * tokens, tokens)
            pairs = [
                (grads.at[i, :, columns], token_right.at[chunk, token_rows, pl.ds(i * wide, wide)])
                for i in range(3)
            ]
            pairs.append((branch.at[:, columns], attn_right.at[chunk, token_rows]))
            for i, (source, target) in enumerate(pairs):
                copies.append(
                    pltpu.make_async_copy(source, target, right_sems.at[chunk, 4 * core + i])
                )
        right_copies.append(copies)
    start_all(left_copies + right_copies[0][:3] + right_copies[0][4:7] + attn_copies)
    start_all(right_copies[0][3:4] + right_copies[0][7:] + right_copies[1] + right_copies[2])
    outward = []
    half = places // 2
    side = side_ref[0]
    for chunk in range(3):
        if chunk == 0:
            wait_all(left_copies + right_copies[0][:3] + right_copies[0][4:7])
        else:
            wait_all(right_copies[chunk])
        token_product = dot_nn(flat(token_left), token_right[chunk]).astype(jnp.bfloat16)
        if chunk == 0:
            wait_all(attn_copies + right_copies[0][3:4] + right_copies[0][7:])
        attn_product = dot_nn(flat(attn_left), attn_right[chunk]).astype(jnp.bfloat16)
        products = [
            token_product[:, :wide],
            attn_product,
            token_product[:, wide : 2 * wide],
            token_product[:, 2 * wide :],
        ]
        for which, product in enumerate(products):
            for place in range(places):
                for tile in range(2):
                    block = product[
                        place * rows : (place + 1) * rows, tile * LANES : (tile + 1) * LANES
                    ]
                    if chunk == 0:
                        made_x[place, which * 2 + tile] = block
                    elif chunk == 1:
                        where = jnp.bitwise_xor(side, which // 2)
                        made_y[where, place, which % 2 * 2 + tile] = block
                    else:
                        made_z[places_z[place], which * 2 + tile] = block
        if chunk == 0:
            pairs = [(made_x.at[:half], keep_x), (made_x.at[half:], send_x)]
        elif chunk == 1:
            pairs = [(made_y.at[0], keep_y), (made_y.at[1], send_y)]
        else:
            pairs = [(made_z.at[:half], keep_z), (made_z.at[half:], send_z)]
        for source, target in pairs:
            copy = pltpu.make_async_copy(source, target, out_sems.at[len(outward)])
            copy.start()
            outward.append(copy)
    wait_all(outward)


def attention_step(
    side, own, other, token_at, attn_at, rows, places_z, grads, grads_other, branch, branch_other
):
    places, _, tokens = own.shape
    wide = 2 * LANES
    low = jnp.bfloat16
    half = places // 2
    shape = jax.ShapeDtypeStruct((half, 8, rows, LANES), low)
    shape_y = jax.ShapeDtypeStruct((places, 4, rows, LANES), low)
    return pl.pallas_call(
        functools.partial(attention_kernel, token_at, attn_at, places_z),
        in_specs=[smem_spec()] + [any_spec(), got_spec()] * 3,
        out_specs=[any_spec()] * 6,
        out_shape=[shape, shape, shape_y, shape_y, shape, shape],
        scratch_shapes=[
            pltpu.VMEM((places, rows, 2 * tokens), low),
            pltpu.VMEM((places, rows, 2 * tokens), low),
            pltpu.VMEM((3, 2 * tokens, 3 * wide), low),
            pltpu.VMEM((3, 2 * tokens, wide), low),
            pltpu.VMEM((places, 8, rows, LANES), low),
            pltpu.VMEM((2, places, 4, rows, LANES), low),
            pltpu.VMEM((places, 8, rows, LANES), low),
            pltpu.SemaphoreType.DMA((2, 2)),
            pltpu.SemaphoreType.DMA((3, 8)),
            pltpu.SemaphoreType.DMA((6,)),
        ],
        compiler_params=compiler_params(),
        cost_estimate=cost(6),
        name="attention_step",
    )(side, own, other, grads, grads_other, branch, branch_other)


def body(
    hidden_states_in,
    piece_sizes,
    matching_passage_number,
    softmax_sharpness,
    question_projection,
    question_offset,
    lookup_projection,
    content_projection,
    content_offset,
    mixing_result_projection,
    mixing_result_offset,
    mixing_layernorm_scale,
    mixing_layernorm_offset,
    widening_projection,
    widening_offset,
    narrowing_projection,
    narrowing_offset,
    perceptron_layernorm_scale,
    perceptron_layernorm_offset,
):
    rows_here, length, width = hidden_states_in.shape
    segments = piece_sizes.shape[1]
    per_device = segments // 2
    groups_y = lax.axis_size("gy")
    rows = width // groups_y
    inner_rows = widening_offset.shape[0] // groups_y
    gy_bits = powers_below(groups_y)
    order_x = gy_bits[1:]
    order_z = gy_bits[2:3] + gy_bits[1:2] + gy_bits[3:]
    here = lax.axis_index("gy").astype(jnp.int32).reshape(1)
    side = (lax.axis_index("gx").astype(jnp.int32) & 1).reshape(1)
    (
        queries,
        keys,
        keys_t,
        values,
        lse,
        normed_one,
        inv_one,
        slope,
        normed_two,
        inv_two,
        pooled,
        message,
        side_own,
        side_send,
    ) = forward_step(
        here,
        piece_sizes,
        matching_passage_number,
        place_masks(order_x),
        place_masks(order_z),
        [
            hidden_states_in[0],
            question_projection,
            lookup_projection,
            content_projection,
            mixing_result_projection,
            widening_projection,
            narrowing_projection,
            question_offset,
            content_offset,
            mixing_result_offset,
            mixing_layernorm_scale,
            mixing_layernorm_offset,
            widening_offset,
            narrowing_offset,
            perceptron_layernorm_scale,
            perceptron_layernorm_offset,
        ],
    )
    gathered, numbers_of, place, side_other = gather_blocks(
        message, swap_with(side_send, "gy", 1)
    )
    numbers = (numbers_of[:, None] * per_device + np.arange(per_device)[None, :]).reshape(1, -1)
    loss_out, grad_hidden_two, branch_two, sums_two = loss_step(
        place.astype(jnp.int32).reshape(1),
        piece_sizes,
        softmax_sharpness,
        jnp.asarray(numbers, jnp.int32),
        gathered,
        pooled,
        normed_two,
        inv_two,
        perceptron_layernorm_scale,
    )
    branch_two_other = swap_with(branch_two, "gy", 1)
    outer_keep_x, outer_send_x, outer_keep_z, outer_send_z = outer_step(
        side_own, side_other, branch_two, branch_two_other, inner_rows // 2
    )
    outer_send_x, outer_send_z, branch_two = tie(outer_send_x, outer_send_z, branch_two)
    outer_got_x = swap_with(outer_send_x, "gy", order_x[0])
    outer_got_z = swap_with(outer_send_z, "gy", order_z[0])
    grad_pre, grad_b_inner, grad_hidden_one, branch_one, grad_attn, sums_one = before_step(
        branch_two,
        slope,
        narrowing_projection,
        widening_projection,
        grad_hidden_two,
        normed_one,
        inv_one,
        mixing_layernorm_scale,
        mixing_result_projection,
    )
    outer_got_x, outer_got_z, grad_pre, branch_one, grad_attn = tie(
        outer_got_x, outer_got_z, grad_pre, branch_one, grad_attn
    )
    grad_pre_other = swap_with(grad_pre, "gy", 1)
    branch_one_other = swap_with(branch_one, "gy", 1)
    (outer_keep_x, outer_send_x), (outer_keep_z, outer_send_z) = add_step(
        [[(outer_keep_x, outer_got_x)], [(outer_keep_z, outer_got_z)]]
    )
    outer_send_x, outer_send_z, grad_attn = tie(outer_send_x, outer_send_z, grad_attn)
    outer_got_x = swap_with(outer_send_x, "gy", order_x[1])
    outer_got_z = swap_with(outer_send_z, "gy", order_z[1])
    grads, sums_attn = attend_back_step(
        piece_sizes,
        queries,
        keys,
        keys_t,
        values,
        lse,
        grad_attn,
    )
    grads, grad_pre_other, branch_one_other, outer_got_x, outer_got_z = tie(
        grads, grad_pre_other, branch_one_other, outer_got_x, outer_got_z
    )
    grads_other = swap_with(grads, "gy", 1)
    (outer_keep_x, outer_send_x), (outer_keep_z, outer_send_z) = add_step(
        [[(outer_keep_x, outer_got_x)], [(outer_keep_z, outer_got_z)]]
    )
    outer_got_x = swap_with(outer_send_x, "gy", order_x[2])
    outer_got_z = swap_with(outer_send_z, "gy", order_z[2])
    inner_keep_x, inner_send_x, inner_keep_y, inner_send_y = inner_step(
        side, side_own, side_other, inner_rows, rows, grad_pre, grad_pre_other
    )
    gx_bits = powers_below(lax.axis_size("gx"))
    inner_send_x, inner_send_y, grads_other = tie(inner_send_x, inner_send_y, grads_other)
    inner_got_x = swap_with(inner_send_x, "gy", order_x[0])
    inner_got_y = swap_with(inner_send_y, "gx", 1)
    masks_x, masks_z = place_masks(order_x), place_masks(order_z)
    attn_keep_x, attn_send_x, attn_keep_y, attn_send_y, attn_keep_z, attn_send_z = attention_step(
        side,
        side_own,
        side_other,
        inner_rows + rows,
        inner_rows + 2 * rows,
        rows,
        [masks_z.index(mask) for mask in masks_x],
        grads,
        grads_other,
        branch_one,
        branch_one_other,
    )
    attn_got_x = swap_with(attn_send_x, "gy", order_x[0])
    attn_got_y = swap_with(attn_send_y, "gx", 1)
    attn_got_z = swap_with(attn_send_z, "gy", order_z[0])
    attn_keep_x, sums_attn = tie(attn_keep_x, sums_attn)
    vectors = jnp.concatenate([sums_attn, sums_one, sums_two], axis=0)
    vectors = vectors.reshape(8, groups_y, rows).transpose(1, 0, 2).reshape(groups_y, 8 * rows)
    vectors = jnp.concatenate([vectors, grad_b_inner.reshape(groups_y, -1)], axis=1)
    used = vectors.shape[1]
    vectors = jnp.pad(vectors, ((0, 0), (0, 8 * LANES - used)))
    vectors = vectors.reshape((2,) * len(gy_bits) + (8 * LANES,))
    for axis, bit in enumerate(reversed(gy_bits)):
        high = (lax.axis_index("gy") & bit) != 0
        vectors = jnp.where(high, jnp.flip(vectors, axis=axis), vectors)
    vectors = vectors.transpose(tuple(reversed(range(len(gy_bits)))) + (len(gy_bits),))
    vectors = vectors.reshape(2, groups_y // 2, 1, 8, LANES)
    vector_got = swap_with(vectors[1], "gy", gy_bits[0])
    gx_hops = [("gx", bit) for bit in gx_bits]
    hops_x = [("gy", bit) for bit in order_x]
    hops_z = [("gy", bit) for bit in order_z]
    hops_y = gx_hops[:1] + hops_x + gx_hops[1:] + gx_hops[:1]

    def chain(keep, got, send, hops, vector=False):
        return {
            "keep": keep,
            "got": got,
            "send": send,
            "hops": list(hops),
            "vector": vector,
        }

    chains = {
        "inner_x": chain(inner_keep_x, ("inner_x", 0), None, hops_x[1:] + gx_hops),
        "inner_y": chain(inner_keep_y, ("inner_y", 0), None, hops_y[1:]),
        "outer_x": chain(outer_keep_x, ("outer_x", 0), None, hops_x[3:] + gx_hops),
        "outer_z": chain(outer_keep_z, ("outer_z", 0), None, hops_z[3:] + gx_hops),
    }
    received = {
        "inner_x": inner_got_x,
        "inner_y": inner_got_y,
        "outer_x": outer_got_x,
        "outer_z": outer_got_z,
    }
    received = {key: item.reshape((-1,) + item.shape[-2:]) for key, item in received.items()}
    finals = {}

    def finish():
        for name, item in chains.items():
            if not item["hops"] and name not in finals:
                hop, at = item["got"]
                count = item["keep"].shape[1]
                finals[name] = (item["keep"][0], received[hop][at : at + count])

    sent = round_step(chains, received, rows, VMEM_BYTES)
    keys = list(sent)
    *items, grads = tie(*[sent[key] for key in keys], grads)
    items = [swap_with(item, key[0], key[1]) for item, key in zip(items, keys)]
    grad_tokens = token_step(
        grad_hidden_one, grads, question_projection, lookup_projection, content_projection
    )
    *items, attn_got_x, attn_got_y, attn_got_z, grad_tokens, vector_got = tie(
        *items, attn_got_x, attn_got_y, attn_got_z, grad_tokens, vector_got
    )
    received = dict(zip(keys, items))
    finish()
    begun = {"attn_x": attn_got_x, "attn_y": attn_got_y, "attn_z": attn_got_z}
    for name, item in begun.items():
        received[name] = item.reshape((-1,) + item.shape[-2:])
    vector_hops = [("gy", bit) for bit in gy_bits[1:]] + gx_hops
    chains["vector"] = chain(vectors[0] + vector_got, None, None, vector_hops, True)
    chains["attn_x"] = chain(attn_keep_x, ("attn_x", 0), None, hops_x[1:] + gx_hops)
    chains["attn_y"] = chain(attn_keep_y, ("attn_y", 0), None, hops_y[1:])
    chains["attn_z"] = chain(attn_keep_z, ("attn_z", 0), None, hops_z[1:] + gx_hops)
    limit = SMALL_BYTES
    while any(item["hops"] for item in chains.values()):
        sent = round_step(chains, received, rows, limit)
        limit = SMALL_BYTES
        keys = list(sent)
        items = tie(*[swap_with(sent[key], key[0], key[1]) for key in keys])
        received = dict(zip(keys, items))
        finish()

    def summed(name):
        mine, other = finals[name]
        return widen(mine) + widen(other)

    def side_by_side(name):
        mine, other = finals[name]
        high = (lax.axis_index("gx") & 1) != 0
        return widen(
            jnp.concatenate([jnp.where(high, other, mine), jnp.where(high, mine, other)], axis=0)
        )

    vectors = sum(join_vector(item, 8) for item in finals["vector"])
    vectors = vectors.reshape(1, 8 * LANES)[:, :used]
    outer_x, outer_z = summed("outer_x"), summed("outer_z")
    attn_x, attn_y, attn_z = summed("attn_x"), side_by_side("attn_y"), summed("attn_z")
    inner_sums = jnp.concatenate([summed("inner_x"), side_by_side("inner_y")], axis=0)
    vector_sums = vectors[0]
    b_query, b_value, b_output, gain_attn, shift_attn, b_outer, gain_ffn, shift_ffn = [
        vector_sums[i * rows : (i + 1) * rows] for i in range(8)
    ]
    grad_w_query, grad_w_output, grad_w_key, grad_w_value = [
        jnp.concatenate(
            [part[2 * i + tile] for part in (attn_x, attn_y, attn_z) for tile in range(2)], axis=1
        )
        for i in range(4)
    ]
    grad_w_outer = jnp.concatenate([share_of(outer_x, width), share_of(outer_z, width)], axis=0)
    return (
        loss_out.reshape(1),
        pooled[None],
        grad_tokens.reshape(rows_here, length, width),
        grad_w_query,
        b_query,
        grad_w_key,
        grad_w_value,
        b_value,
        grad_w_output,
        b_output,
        gain_attn,
        shift_attn,
        share_of(inner_sums, widening_offset.shape[0]),
        vector_sums[8 * rows :],
        grad_w_outer,
        b_outer,
        gain_ffn,
        shift_ffn,
    )


def solution(mesh):
    return jax.shard_map(
        body,
        mesh=mesh,
        in_specs=(
            P(("gx", "gy"), None, None),
            P(("gx", "gy"), None),
            P(("gx", "gy")),
            P(),
            P(),
            P(),
            P(),
            P(),
            P(),
            P(),
            P(),
            P(),
            P(),
            P(),
            P(),
            P(),
            P(),
            P(),
            P(),
        ),
        out_specs=(
            P(),
            P(("gx", "gy"), None, None),
            P(("gx", "gy"), None, None),
            P("gy", None),
            P("gy"),
            P("gy", None),
            P("gy", None),
            P("gy"),
            P("gy", None),
            P("gy"),
            P("gy"),
            P("gy"),
            P("gy", None),
            P("gy"),
            P("gy", None),
            P("gy"),
            P("gy"),
            P("gy"),
        ),
        check_vma=False,
    )
```
